256 devices in a mesh: pa: 16 (over x_lo, y, core), af: 16 (over z, x_hi).
Axes of the slice: x: 4 (x_hi: 2, x_lo: 2; x = x_hi * 2 + x_lo), y: 4, z: 8, core: 2. Of those that a mesh axis runs over, the one named last changes fastest.
Arguments:
- spectra: bfloat16 [2, 57600, 2048], P(None, 'af', 'pa'), may hold values from -64 to 64
- tilt_min: int32 [2048], replicated, may hold values from -70 to -46
- tilt_max: int32 [2048], replicated, may hold values from 46 to 70
- tilt_axis: int32 [2048], replicated, may hold values from 0 to 1
Outputs:
- correlation: float32 [2048, 1152], P(('pa', 'af'))
The draws below stay inside these ranges and needn't reach their ends.
All inputs are finite; a program needn't handle non-finite values.
Results may differ from the reference program's by a relative error of at most 0.0003.
Values may be sent and summed in bfloat16 or wider, within the bound.
A program may use at most 64 MiB of HBM per device.

```python
import math
import jax
import jax.numpy as jnp
from jax import lax

G = 48
P_DEV = 128
VOX = 57600
NPART = 2048
N_PA = 16


def draw_spectra(key, part):
    key = jax.random.fold_in(key, 17)
    common_key, noise_key, level_key, gain_key, shift_key = jax.random.split(key, 5)
    half_len = G // 2 + 1
    flat_index = jnp.arange(VOX, dtype=jnp.int32)
    depth_index = flat_index % half_len
    column = flat_index // half_len % G
    row_index = flat_index // (half_len * G)
    freq_x = jnp.where(row_index < G // 2, row_index, row_index - G).astype(jnp.float32)
    freq_y = jnp.where(column < G // 2, column, column - G).astype(jnp.float32)
    freq_z = depth_index.astype(jnp.float32)
    radius_sq = freq_x * freq_x + freq_y * freq_y + freq_z * freq_z
    common = jnp.clip(jax.random.normal(common_key, (2, VOX), jnp.float32), -4.0, 4.0)
    falloff = 100.0
    noise_part = jnp.clip(jax.random.normal(noise_key, (2, VOX, NPART), jnp.float32), -4.0, 4.0)
    noise_level = jnp.exp(jax.random.uniform(level_key, (NPART,), jnp.float32, math.log(0.5), math.log(2.0)))
    particle_gain = jnp.exp(jax.random.uniform(gain_key, (NPART,), jnp.float32, math.log(0.3), math.log(3.0)))
    shift_reach = 1.5
    envelope = 1.0 / (1.0 + radius_sq / falloff)
    offsets = jax.random.uniform(shift_key, (3, NPART), jnp.float32, -shift_reach, shift_reach)
    phase_angle = -2.0 * math.pi / G * (freq_x[:, None] * offsets[0][None, :] + freq_y[:, None] * offsets[1][None, :] + freq_z[:, None] * offsets[2][None, :])
    cosine = jnp.cos(phase_angle)
    sine_part = jnp.sin(phase_angle)
    amplitude = envelope[:, None] * particle_gain[None, :]
    real_part = amplitude * (common[0][:, None] * cosine - common[1][:, None] * sine_part + noise_level[None, :] * noise_part[0])
    imag_part = amplitude * (common[0][:, None] * sine_part + common[1][:, None] * cosine + noise_level[None, :] * noise_part[1])
    return jnp.stack([real_part, imag_part], axis=0).astype(jnp.bfloat16)


def set_ends(drawn, own_key, least, largest):
    index_at = [jax.random.randint(jax.random.fold_in(own_key, axis), (), 0, length) for axis, length in enumerate(drawn.shape)]
    longest = drawn.shape.index(max(drawn.shape))
    neighbour = index_at[:longest] + [(index_at[longest] + 1) % drawn.shape[longest]] + index_at[longest + 1:]
    return drawn.at[tuple(index_at)].set(least).at[tuple(neighbour)].set(largest)


def setup_inputs(seed: int = 0) -> dict:
    seeds = jax.random.split(jax.random.key(seed), 5)
    spectra = draw_spectra(jax.random.fold_in(seeds[4], 71), 0)
    tilt_min = set_ends(jax.random.randint(seeds[1], (NPART,), -70, -45), jax.random.fold_in(seeds[1], 1), -70, (-45) - 1).astype(jnp.int32)
    tilt_max = set_ends(jax.random.randint(seeds[2], (NPART,), 46, 71), jax.random.fold_in(seeds[2], 1), 46, 70).astype(jnp.int32)
    tilt_axis = set_ends(jax.random.randint(seeds[3], (NPART,), 0, 2), jax.random.fold_in(seeds[3], 1), 0, 1).astype(jnp.int32)
    return dict(spectra=spectra, tilt_min=tilt_min, tilt_max=tilt_max, tilt_axis=tilt_axis)


def wedge_terms(offset, length, tilt_min, tilt_max, tilt_axis):
    half_len = G // 2 + 1
    flat_index = offset + lax.iota(jnp.int32, length)
    depth_index = flat_index % half_len
    column = flat_index // half_len % G
    row_index = flat_index // (half_len * G)
    freq_x = jnp.where(row_index < G // 2, row_index, row_index - G)
    freq_y = jnp.where(column < G // 2, column, column - G)
    tilt_coord = jnp.where(tilt_axis[None, :] == 1, freq_x[:, None], freq_y[:, None])
    radial = jnp.abs(tilt_coord).astype(jnp.float32)
    height = jnp.where(tilt_coord >= 0, -depth_index[:, None], depth_index[:, None]).astype(jnp.float32)
    lower_slope = jnp.tan(tilt_min.astype(jnp.float32) * (math.pi / 180.0))
    upper_slope = jnp.tan(tilt_max.astype(jnp.float32) * (math.pi / 180.0))
    inside = (radial * lower_slope[None, :] <= height) & (height <= radial * upper_slope[None, :])
    wedge_mask = inside.astype(jnp.bfloat16)
    weight = jnp.where((depth_index == 0) | (depth_index == G // 2), 1.0, 2.0).astype(jnp.float32)
    return (wedge_mask, weight)

def masked_power(spectra_block, wedge_mask, weight):
    masked = spectra_block * wedge_mask[None]
    real_part = masked[0].astype(jnp.float32)
    imag_part = masked[1].astype(jnp.float32)
    power = (weight[:, None] * (real_part * real_part + imag_part * imag_part)).astype(jnp.bfloat16)
    return (masked, power)

def inner_sum(first_op, second_op):
    return jnp.einsum('vp,vq->pq', first_op, second_op, precision=lax.Precision.HIGHEST)

def reference(spectra, tilt_min, tilt_max, tilt_axis):
    band_len = N_PA // 2 + 1

    def block_data(block_id):
        row_start = (block_id * P_DEV).astype(jnp.int32)
        wedge_mask, weight = wedge_terms(0, VOX, lax.dynamic_slice_in_dim(tilt_min, row_start, P_DEV), lax.dynamic_slice_in_dim(tilt_max, row_start, P_DEV), lax.dynamic_slice_in_dim(tilt_axis, row_start, P_DEV))
        block_spectra = lax.dynamic_slice_in_dim(spectra, row_start, P_DEV, 2)
        masked, power = masked_power(block_spectra, wedge_mask, weight)
        return (masked, power, wedge_mask, weight)

    def row_band(row_block):
        left_data = block_data(row_block)
        weight = left_data[3]
        left_real = left_data[0][0].astype(jnp.float32) * weight[:, None]
        left_imag = left_data[0][1].astype(jnp.float32) * weight[:, None]
        left_power = left_data[1].astype(jnp.float32)
        left_mask = left_data[2].astype(jnp.float32)

        def pair_block(step_index):
            right_data = block_data((row_block + step_index) % N_PA)
            right_real = right_data[0][0].astype(jnp.float32)
            right_imag = right_data[0][1].astype(jnp.float32)
            cross_sum = inner_sum(left_real, right_real) + inner_sum(left_imag, right_imag)
            own_norm = inner_sum(left_power, right_data[2].astype(jnp.float32))
            other_norm = inner_sum(left_mask, right_data[1].astype(jnp.float32))
            return cross_sum / jnp.sqrt(own_norm * other_norm + 1e-06)
        blocks_out = lax.map(pair_block, jnp.arange(band_len, dtype=jnp.int32))
        return jnp.transpose(blocks_out, (1, 0, 2)).reshape(P_DEV, band_len * P_DEV)
    rows_out = lax.map(row_band, jnp.arange(N_PA, dtype=jnp.int32))
    return rows_out.reshape(NPART, band_len * P_DEV)
```

```python
import functools
import math

import jax
import jax.numpy as jnp
from jax import lax
from jax.experimental import pallas as pl
from jax.experimental.pallas import tpu as pltpu
from jax.sharding import PartitionSpec as P

MESH = pl.DeviceIdType.MESH
F32 = jnp.float32
BF16 = jnp.bfloat16

G = 48
HALF = 25
VD = 3600
KC = 1824
A = 928
B = 896
FA = A // 2
FB = B // 2
CH = 96
T_LO, T_HI, N_T = 46, 70, 25
eps_norm = 1e-06


def coords():
    pa = lax.axis_index("pa")
    af = lax.axis_index("af")
    return pa // 8, (pa // 2) % 4, pa % 2, af // 2, af % 2


def dev(xl, y, core, z, xh):
    return {"pa": (xl * 4 + y) * 2 + core, "af": z * 2 + xh}


def tdot(lhs, rhs):
    return lax.dot_general(lhs, rhs, (((0,), (0,)), ((), ())), preferred_element_type=F32)


def cells(first, shape):
    v = (first + lax.broadcasted_iota(jnp.int32, shape, 0)).astype(F32)
    q = jnp.floor((v + 0.5) * (1.0 / HALF))
    iz = v - q * HALF
    ix = jnp.floor((q + 0.5) * (1.0 / G))
    iy = q - ix * G
    fx = jnp.where(ix < G // 2, ix, ix - G)
    fy = jnp.where(iy < G // 2, iy, iy - G)
    return fx, fy, iz


def kernel(spec_hbm, cols_ref, out_ref, m, o, ow, ra, rb, fa, fb, acc, inc, zl, rz, fin, load_sem, ssem, rsem):
    xl, y, core, z, xh = coords()
    af = lax.axis_index("af")
    yp, ym, y2 = (y + 1) % 4, (y + 3) % 4, (y + 2) % 4
    zp, zm = (z + 1) % 8, (z + 7) % 8
    started = []

    def rdma(src, dst, target):
        i = len(started)
        c = pltpu.make_async_remote_copy(
            src_ref=src, dst_ref=dst, send_sem=ssem.at[i], recv_sem=rsem.at[i], device_id=target, device_id_type=MESH
        )
        c.start()
        started.append(c)
        return c

    loads = [
        pltpu.make_async_copy(spec_hbm.at[p], m.at[p, pl.ds(0, VD)], load_sem.at[p]) for p in range(2)
    ]
    for c in loads:
        c.start()
    barrier = pltpu.get_barrier_semaphore()
    peers = [
        dev(xl, y, 1 - core, z, xh),
        dev(1 - xl, y, core, z, xh),
        dev(1 - xl, y, 1 - core, z, xh),
        dev(xl, yp, core, z, xh),
        dev(xl, ym, core, z, xh),
        dev(1 - xl, y, core, z, 1 - xh),
        dev(xl, y, core, zp, xh),
        dev(xl, y, core, zm, xh),
    ]
    for peer in peers:
        pl.semaphore_signal(barrier, inc=1, device_id=peer, device_id_type=MESH)
    m[:, VD:, :] = jnp.zeros((2, 2 * KC - VD, 128), BF16)
    for c in loads:
        c.wait()

    def own_col(dx, dc):
        return pl.multiple_of(((xl ^ dx) * 2 + (core ^ dc)) * 128, 128)

    lower = cols_ref[0:1, :]
    upper = cols_ref[1:2, :]
    axis = cols_ref[2:3, :]

    def mask_half(half):
        def body(i, carry):
            r0 = pl.multiple_of(half * KC + i * CH, 16)
            fx, fy, iz = cells(af * VD + r0, (CH, 128))
            u = jnp.where(axis > 0.5, fx, fy)
            a = jnp.abs(u)
            b = jnp.where(u >= 0.0, -iz, iz)
            keep = ((a * lower <= b) & (b <= a * upper)).astype(F32)
            for p in range(2):
                m[p, pl.ds(r0, CH), :] = (m[p, pl.ds(r0, CH), :].astype(F32) * keep).astype(BF16)
            return carry

        lax.fori_loop(0, KC // CH, body, 0)

    mask_half(core)
    pl.semaphore_wait(barrier, len(peers))

    mine = pl.multiple_of(core * KC, 16)
    theirs = pl.multiple_of((1 - core) * KC, 16)
    col = own_col(0, 0)
    o[:, pl.ds(col, 128)] = m[xl, pl.ds(mine, KC), :]

    y1 = [None] * 4

    def y_send(p):
        c = own_col(p // 2, p % 2)
        y1[p] = (
            rdma(o.at[pl.ds(0, A), pl.ds(c, 128)], ra.at[:, pl.ds(c, 128)], dev(xl, ym, core, z, xh)),
            rdma(o.at[pl.ds(A, B), pl.ds(c, 128)], rb.at[:, pl.ds(c, 128)], dev(xl, yp, core, z, xh)),
        )

    y_send(0)
    x_same = rdma(m.at[1 - xl, pl.ds(mine, KC)], o.at[:, pl.ds(col, 128)], dev(1 - xl, y, core, z, xh))
    mask_half(1 - core)
    sib = rdma(m.at[xl, pl.ds(theirs, KC)], o.at[:, pl.ds(col, 128)], dev(xl, y, 1 - core, z, xh))
    x_other = rdma(m.at[1 - xl, pl.ds(theirs, KC)], o.at[:, pl.ds(col, 128)], dev(1 - xl, y, 1 - core, z, xh))

    y_2 = [None] * 4

    def forward(p):
        c = own_col(p // 2, p % 2)
        for d in y1[p]:
            d.wait_recv()
        to_m = pl.multiple_of(jnp.where(ym < 2, 0, FA), 16)
        to_p = pl.multiple_of(jnp.where(yp < 2, 0, FB), 16)
        y_2[p] = (
            rdma(ra.at[pl.ds(to_m, FA), pl.ds(c, 128)], fa.at[:, pl.ds(c, 128)], dev(xl, ym, core, z, xh)),
            rdma(rb.at[pl.ds(to_p, FB), pl.ds(c, 128)], fb.at[:, pl.ds(c, 128)], dev(xl, yp, core, z, xh)),
        )

    sib.wait_recv()
    y_send(1)
    forward(0)
    x_same.wait_recv()
    y_send(2)
    forward(1)
    x_other.wait_recv()
    y_send(3)

    def weigh(i, carry):
        r0 = pl.multiple_of(i * CH, 16)
        iz = cells(af * VD + core * KC + r0, (CH, 128))[2]
        w = jnp.where((iz < 0.5) | (iz > 23.5), 1.0, 2.0)
        for q in range(4):
            ow[pl.ds(r0, CH), q * 128 : (q + 1) * 128] = (
                o[pl.ds(r0, CH), q * 128 : (q + 1) * 128].astype(F32) * w
            ).astype(BF16)
        return carry

    lax.fori_loop(0, KC // CH, weigh, 0)

    def put(tile, value):
        acc[tile] = value.reshape(2, 128, 256)

    def side(x):
        return pl.multiple_of(x * 256, 256)

    def wrap(x, cond):
        return x ^ cond.astype(jnp.int32)

    for x in range(2):
        for slot, xo in ((0, x), (4, 1 - x)):
            put(x * 8 + slot, tdot(ow[:, x * 256 : x * 256 + 256], o[:, xo * 256 : xo * 256 + 256]))

    forward(2)
    forward(3)
    for x in range(2):
        put(x * 8 + 1, tdot(ow[0:A, x * 256 : x * 256 + 256], ra[:, pl.ds(side(wrap(x, y == 3)), 256)]))
        put(x * 8 + 5, tdot(ra[:, x * 256 : x * 256 + 256], ow[0:A, pl.ds(side(wrap(1 - x, y == 3)), 256)]))
        put(x * 8 + 3, tdot(ow[A:KC, x * 256 : x * 256 + 256], rb[:, pl.ds(side(wrap(1 - x, y == 0)), 256)]))
        put(x * 8 + 6, tdot(rb[:, x * 256 : x * 256 + 256], ow[A:KC, pl.ds(side(wrap(x, y == 0)), 256)]))

    for p in range(4):
        for d in y_2[p]:
            d.wait_recv()
    at_a = pl.multiple_of(jnp.where(y < 2, 0, FA), 16)
    at_b = pl.multiple_of(A + jnp.where(y < 2, 0, FB), 16)
    for x in range(2):
        mine_x = side(wrap(x, y >= 2))
        other_x = side(wrap(x, y < 2))
        put(
            x * 8 + 2,
            tdot(ow[pl.ds(at_a, FA), x * 256 : x * 256 + 256], fa[:, pl.ds(mine_x, 256)])
            + tdot(ow[pl.ds(at_b, FB), x * 256 : x * 256 + 256], fb[:, pl.ds(mine_x, 256)]),
        )
        put(
            x * 8 + 7,
            tdot(fa[:, x * 256 : x * 256 + 256], ow[pl.ds(at_a, FA), pl.ds(other_x, 256)])
            + tdot(fb[:, x * 256 : x * 256 + 256], ow[pl.ds(at_b, FB), pl.ds(other_x, 256)]),
        )

    pair = rdma(acc.at[:, 1 - core], inc, dev(xl, y, 1 - core, z, xh))
    pair.wait_recv()
    for t in range(16):
        inc[t] = inc[t] + acc[t, core]

    def rows(zz):
        return pl.ds(pl.multiple_of(((zz + 16) % 8) * 16, 16), 16)

    flows = []
    for lo, way, steps in ((0, 1, 3), (0, -1, 4), (8, 1, 4), (8, -1, 3)):
        flows.append(dict(lo=lo, way=way, steps=steps, target=dev(xl, y, core, zp if way > 0 else zm, xh)))
    for s in range(4):
        for f, flow in enumerate(flows):
            if s >= flow["steps"]:
                continue
            tiles = pl.ds(flow["lo"], 8)
            here = rows(z + flow["way"] * (flow["steps"] - s))
            if s == 0:
                src = inc.at[tiles, here]
            else:
                flow["copy"].wait_recv()
                src = zl.at[f, s - 1]
                src[...] = src[...] + inc[tiles, here, :]
            flow["copy"] = rdma(src, zl.at[f, s], flow["target"])
    for flow in flows:
        flow["copy"].wait_recv()
    for f in (0, 2):
        lo = flows[f]["lo"]
        rz[lo : lo + 8] = (
            inc[lo : lo + 8, rows(z), :]
            + zl[f, flows[f]["steps"] - 1]
            + zl[f + 1, flows[f + 1]["steps"] - 1]
        )

    me_x = xh * 2 + xl
    last = []
    for dx in range(4):
        xo = xl ^ (dx % 2)
        ho = xh ^ (dx // 2)
        here = pl.ds(pl.multiple_of(ho * 8, 8), 8)
        base = xo * 8
        if dx:
            last.append(rdma(rz.at[pl.ds(base, 5), here], fin.at[me_x, 0:5], dev(xo, y, core, z, ho)))
        else:
            fin[me_x, 0:5] = rz[pl.ds(base, 5), here, :]
        for slot, yo in ((5, yp), (6, ym), (7, y2)):
            last.append(rdma(rz.at[base + slot, here], fin.at[me_x, slot], dev(xo, yo, core, z, ho)))
    for c in last:
        c.wait_recv()
    s = [fin[0, t] + fin[1, t] + fin[2, t] + fin[3, t] for t in range(8)]
    parts = [s[0], s[1] + s[6], s[2] + s[7], s[3] + s[5], s[4]]
    for g in range(5):
        out_ref[:, g * 256 : (g + 1) * 256] = parts[g]
    for c in started:
        c.wait_send()


def cross_call(spectra, cols):
    scratch = [
        pltpu.VMEM((2, 2 * KC, 128), BF16),
        pltpu.VMEM((KC, 512), BF16),
        pltpu.VMEM((KC, 512), BF16),
        pltpu.VMEM((A, 512), BF16),
        pltpu.VMEM((B, 512), BF16),
        pltpu.VMEM((FA, 512), BF16),
        pltpu.VMEM((FB, 512), BF16),
        pltpu.VMEM((16, 2, 128, 256), F32),
        pltpu.VMEM((16, 128, 256), F32),
        pltpu.VMEM((4, 4, 8, 16, 256), F32),
        pltpu.VMEM((16, 16, 256), F32),
        pltpu.VMEM((4, 8, 8, 256), F32),
        pltpu.SemaphoreType.DMA((2,)),
        pltpu.SemaphoreType.DMA((64,)),
        pltpu.SemaphoreType.DMA((64,)),
    ]
    return pl.pallas_call(
        kernel,
        out_shape=jax.ShapeDtypeStruct((8, 1280), F32),
        in_specs=[pl.BlockSpec(memory_space=pl.ANY), pl.BlockSpec(memory_space=pltpu.VMEM)],
        out_specs=pl.BlockSpec(memory_space=pltpu.VMEM),
        scratch_shapes=scratch,
        compiler_params=pltpu.CompilerParams(
            collective_id=0, has_side_effects=True, vmem_limit_bytes=56 * 2**20
        ),
    )(spectra, cols)


def slopes(degrees):
    return jnp.tan(degrees.astype(F32) * (math.pi / 180.0))


def shards(spectra, tilt_min, tilt_max, tilt_axis):
    pa = lax.axis_index("pa")
    af = lax.axis_index("af")
    lower, upper = slopes(tilt_min), slopes(tilt_max)

    def own(value):
        return lax.dynamic_slice_in_dim(value, pa * 128, 128)

    cols = jnp.zeros((8, 128), F32)
    cols = cols.at[0].set(own(lower)).at[1].set(own(upper)).at[2].set(own(tilt_axis).astype(F32))
    cross = cross_call(spectra, cols)

    fx, fy, iz = cells(af * VD, (VD, 128))
    u = jnp.where(cols[2] > 0.5, fx, fy)
    a = jnp.abs(u)
    b = jnp.where(u >= 0, -iz, iz)
    keep = (a * cols[0] <= b) & (b <= a * cols[1])
    w = jnp.where((iz < 0.5) | (iz > 23.5), 1.0, 2.0)
    real, imag = spectra[0].astype(F32), spectra[1].astype(F32)
    power = jnp.where(keep, w * (real * real + imag * imag), 0.0).astype(BF16)
    lane = jnp.arange(128)
    c_axis, c_side, c_t = lane // 50, (lane // 25) % 2, (lane % 25)
    slope = slopes(c_t + T_LO)
    cu = jnp.where(c_axis == 1, fx, fy)
    c_keep = (
        (iz <= jnp.abs(cu) * slope) & ((cu >= 0) == (c_side == 0)) & (lane < 100)
    ).astype(BF16)
    table = jnp.einsum("vi,vc->ic", power, c_keep, preferred_element_type=F32)
    table = lax.psum(table, "af")
    table = lax.all_gather(table, "pa", tiled=True)

    def hot(t_min, t_max, axis):
        first = axis * 50 + (-t_min - T_LO)
        second = axis * 50 + 25 + (t_max - T_LO)
        return ((lane == first[:, None]) | (lane == second[:, None])).astype(F32)

    hots = hot(tilt_min, tilt_max, tilt_axis)
    band = (pa * 128 + jnp.arange(1152)) % 2048
    row0 = pa * 128 + af * 8
    t_own = lax.dynamic_slice_in_dim(table, row0, 8)
    h_own = lax.dynamic_slice_in_dim(hots, row0, 8)
    highest = lax.Precision.HIGHEST
    own_norm = jnp.einsum("ic,jc->ij", t_own, hots[band], precision=highest)
    other_norm = jnp.einsum("ic,jc->ij", h_own, table[band], precision=highest)
    cross = lax.dynamic_slice_in_dim(cross, (pa % 2) * 128, 1152, 1)
    return cross / jnp.sqrt(own_norm * other_norm + eps_norm)


def solution(mesh):
    in_specs = (P(None, "af", "pa"), P(), P(), P())
    out_specs = P(("pa", "af"), None)
    return jax.shard_map(shards, mesh=mesh, in_specs=in_specs, out_specs=out_specs, check_vma=False)
```

```python
import functools
import math

import jax
import jax.numpy as jnp
from jax import lax
from jax.experimental import pallas as pl
from jax.experimental.pallas import tpu as pltpu
from jax.sharding import PartitionSpec as P

MESH = pl.DeviceIdType.MESH
F32 = jnp.float32
BF16 = jnp.bfloat16

G = 48
HALF = 25
VD = 3600
KC = 1824
A = 928
B = 896
FA = A // 2
FB = B // 2
CH = 96
T_LO, T_HI, N_T = 46, 70, 25
eps_norm = 1e-06


def coords():
    pa = lax.axis_index("pa")
    af = lax.axis_index("af")
    return pa // 8, (pa // 2) % 4, pa % 2, af // 2, af % 2


def dev(xl, y, core, z, xh):
    return {"pa": (xl * 4 + y) * 2 + core, "af": z * 2 + xh}


def tdot(lhs, rhs):
    return lax.dot_general(lhs, rhs, (((0,), (0,)), ((), ())), preferred_element_type=F32)


def cells(first, shape):
    v = (first + lax.broadcasted_iota(jnp.int32, shape, 0)).astype(F32)
    q = jnp.floor((v + 0.5) * (1.0 / HALF))
    iz = v - q * HALF
    ix = jnp.floor((q + 0.5) * (1.0 / G))
    iy = q - ix * G
    fx = jnp.where(ix < G // 2, ix, ix - G)
    fy = jnp.where(iy < G // 2, iy, iy - G)
    return fx, fy, iz

N_SEM = 176


def kernel(spec_hbm, tmin_ref, tmax_ref, axis_ref, out_ref, m, o, ow, ra, rb, fa, fb, acc, inc, xin, zl, rz,
           fin0, fin1, fin2, pw, cm, tt, tl, tg, tf, cls, hot, own, nsend, oth, cross, load_sem, ssem, rsem):
    xl, y, core, z, xh = coords()
    pa = lax.axis_index("pa")
    af = lax.axis_index("af")
    yp, ym, y2 = (y + 1) % 4, (y + 3) % 4, (y + 2) % 4
    zp, zm = (z + 1) % 8, (z + 7) % 8
    me_x = xh * 2 + xl
    started = []

    def rdma(src, dst, target):
        i = len(started)
        c = pltpu.make_async_remote_copy(
            src_ref=src, dst_ref=dst, send_sem=ssem.at[i], recv_sem=rsem.at[i], device_id=target, device_id_type=MESH
        )
        c.start()
        started.append(c)
        return c

    loads = [
        pltpu.make_async_copy(spec_hbm.at[p], m.at[p, pl.ds(0, VD)], load_sem.at[p]) for p in range(2)
    ]
    for c in loads:
        c.start()
    barrier = pltpu.get_barrier_semaphore()
    peers = [
        dev(xl, y, 1 - core, z, xh),
        dev(1 - xl, y, core, z, xh),
        dev(1 - xl, y, 1 - core, z, xh),
        dev(xl, yp, core, z, xh),
        dev(xl, ym, core, z, xh),
        dev(xl, y, core, z, 1 - xh),
        dev(xl, y, core, zp, xh),
        dev(xl, y, core, zm, xh),
    ]
    for peer in peers:
        pl.semaphore_signal(barrier, inc=1, device_id=peer, device_id_type=MESH)
    m[:, VD:, :] = jnp.zeros((2, 2 * KC - VD, 128), BF16)

    cls[0] = axis_ref[...] * 50 + (-T_LO - tmin_ref[...])
    cls[1] = axis_ref[...] * 50 + (N_T - T_LO + tmax_ref[...])
    lower = slopes(tmin_ref[pl.ds(pa, 1), :])
    upper = slopes(tmax_ref[pl.ds(pa, 1), :])
    axis = axis_ref[pl.ds(pa, 1), :]
    lane = lax.broadcasted_iota(jnp.int32, (1, 128), 1)
    c_axis = (lane >= 50).astype(jnp.int32)
    c_side = ((lane - c_axis * 50) >= 25).astype(jnp.int32)
    c_slope = slopes(lane - c_axis * 50 - c_side * 25 + T_LO)
    c_slope = jnp.where(lane < 100, c_slope, -1.0)

    for c in loads:
        c.wait()

    def own_col(dx, dc):
        return pl.multiple_of(((xl ^ dx) * 2 + (core ^ dc)) * 128, 128)

    def mask_half(half):
        def body(i, carry):
            r0 = pl.multiple_of(half * KC + i * CH, 16)
            fx, fy, iz = cells(af * VD + r0, (CH, 128))
            u = jnp.where(axis == 1, fx, fy)
            a = jnp.abs(u)
            b = jnp.where(u >= 0.0, -iz, iz)
            keep = ((a * lower <= b) & (b <= a * upper)).astype(F32)
            for p in range(2):
                m[p, pl.ds(r0, CH), :] = (m[p, pl.ds(r0, CH), :].astype(F32) * keep).astype(BF16)
            return carry

        lax.fori_loop(0, KC // CH, body, 0)

    mask_half(core)
    pl.semaphore_wait(barrier, len(peers))

    mine = pl.multiple_of(core * KC, 16)
    theirs = pl.multiple_of((1 - core) * KC, 16)
    col = own_col(0, 0)
    o[:, pl.ds(col, 128)] = m[xl, pl.ds(mine, KC), :]

    y1a = [[] for _ in range(4)]
    y1b = [[] for _ in range(4)]

    def send_a(p, r0, n):
        c = own_col(p // 2, p % 2)
        y1a[p].append(
            rdma(o.at[pl.ds(r0, n), pl.ds(c, 128)], ra.at[pl.ds(r0, n), pl.ds(c, 128)], dev(xl, ym, core, z, xh))
        )

    def send_b(p, r0, n):
        c = own_col(p // 2, p % 2)
        y1b[p].append(
            rdma(o.at[pl.ds(A + r0, n), pl.ds(c, 128)], rb.at[pl.ds(r0, n), pl.ds(c, 128)], dev(xl, yp, core, z, xh))
        )

    def to_x(r0, n, first, target):
        rows = pl.ds(pl.multiple_of(first + r0, 16), n)
        return rdma(m.at[1 - xl, rows], o.at[pl.ds(r0, n), pl.ds(col, 128)], target)

    send_a(0, 0, A)
    send_b(0, 0, B)
    x_same = [to_x(r0, n, mine, dev(1 - xl, y, core, z, xh)) for r0, n in ((0, A), (A, B))]
    mask_half(1 - core)
    sib = rdma(m.at[xl, pl.ds(theirs, KC)], o.at[:, pl.ds(col, 128)], dev(xl, y, 1 - core, z, xh))
    x_other = [
        to_x(r0, n, theirs, dev(1 - xl, y, 1 - core, z, xh))
        for r0, n in ((0, FA), (A, FB), (FA, FA), (A + FB, FB))
    ]

    def powers(i, carry):
        r0 = pl.multiple_of(i * CH, 16)
        fx, fy, iz = cells(af * VD + r0, (CH, 128))
        re = m[0, pl.ds(r0, CH), :].astype(F32)
        im = m[1, pl.ds(r0, CH), :].astype(F32)
        w = jnp.where((iz < 0.5) | (iz > 23.5), 1.0, 2.0)
        pw[pl.ds(r0, CH), :] = (w * (re * re + im * im)).astype(BF16)
        u = jnp.where(c_axis == 1, fx, fy)
        side = (u < 0.0).astype(jnp.int32)
        cm[pl.ds(r0, CH), :] = ((iz <= jnp.abs(u) * c_slope) & (side == c_side) & (lane < 100)).astype(F32).astype(BF16)
        return carry

    lax.fori_loop(0, 2 * KC // CH, powers, 0)
    tt[...] = tdot(pw[...], cm[...])

    def rows16(zz):
        return pl.ds(pl.multiple_of(((zz + 16) % 8) * 16, 16), 16)

    up, down = dev(xl, y, core, zp, xh), dev(xl, y, core, zm, xh)
    t_flows = [dict(way=1, steps=3, target=up), dict(way=-1, steps=4, target=down)]

    def t_step(s):
        for f, flow in enumerate(t_flows):
            if s > flow["steps"]:
                continue
            if s:
                flow["copy"].wait_recv()
            if s == flow["steps"]:
                continue
            here = rows16(z + flow["way"] * (flow["steps"] - s))
            if s == 0:
                src = tt.at[here]
            else:
                src = tl.at[f, s - 1]
                src[...] = src[...] + tt[here, :]
            flow["copy"] = rdma(src, tl.at[f, s], flow["target"])

    t_step(0)

    y_2 = [None] * 4

    def forward(p):
        c = own_col(p // 2, p % 2)
        to_m = pl.multiple_of(jnp.where(ym < 2, 0, FA), 16)
        to_p = pl.multiple_of(jnp.where(yp < 2, 0, FB), 16)
        for d in y1a[p]:
            d.wait_recv()
        first = rdma(ra.at[pl.ds(to_m, FA), pl.ds(c, 128)], fa.at[:, pl.ds(c, 128)], dev(xl, ym, core, z, xh))
        for d in y1b[p]:
            d.wait_recv()
        second = rdma(rb.at[pl.ds(to_p, FB), pl.ds(c, 128)], fb.at[:, pl.ds(c, 128)], dev(xl, yp, core, z, xh))
        y_2[p] = (first, second)

    sib.wait_recv()
    send_a(1, 0, A)
    send_b(1, 0, B)
    t_step(1)
    forward(0)
    t_step(2)
    x_same[0].wait_recv()
    send_a(2, 0, A)
    x_same[1].wait_recv()
    send_b(2, 0, B)
    t_step(3)
    forward(1)
    t_step(4)
    mine16 = rows16(z)
    tg[xh, mine16, :] = tt[mine16, :] + tl[0, 2] + tl[1, 3]
    gather = []
    for dz in range(8):
        for dh in range(2):
            if dz or dh:
                part = tg.at[xh, mine16]
                gather.append(rdma(part, part, dev(xl, y, core, (z + dz) % 8, xh ^ dh)))

    for d, (send, r0, n) in zip(
        x_other, ((send_a, 0, FA), (send_b, 0, FB), (send_a, FA, FA), (send_b, FB, FB)), strict=True
    ):
        d.wait_recv()
        send(3, r0, n)

    def weigh(i, carry):
        r0 = pl.multiple_of(i * CH, 16)
        iz = cells(af * VD + core * KC + r0, (CH, 128))[2]
        w = jnp.where((iz < 0.5) | (iz > 23.5), 1.0, 2.0)
        for q in range(4):
            ow[pl.ds(r0, CH), q * 128 : (q + 1) * 128] = (
                o[pl.ds(r0, CH), q * 128 : (q + 1) * 128].astype(F32) * w
            ).astype(BF16)
        return carry

    lax.fori_loop(0, KC // CH, weigh, 0)

    def put(tile, value):
        acc[tile] = value.reshape(2, 8, 2, 8, 256)

    def side(x):
        return pl.multiple_of(x * 256, 256)

    def wrap(x, cond):
        return x ^ cond.astype(jnp.int32)

    def pair_sum(lo, n):
        tiles = pl.ds(lo, n)
        return rdma(acc.at[tiles, 1 - core], inc.at[tiles], dev(xl, y, 1 - core, z, xh))

    def pair_add(copy, lo, n):
        copy.wait_recv()
        for t in range(lo, lo + n):
            inc[t] = inc[t] + acc[t, core]

    for x in range(2):
        for slot, xo in ((0, x), (1, 1 - x)):
            put(x * 2 + slot, tdot(ow[:, x * 256 : x * 256 + 256], o[:, xo * 256 : xo * 256 + 256]))
    pair0 = pair_sum(0, 4)
    forward(2)

    def x_send(k, lo):
        copies = []
        for dx in range(1, 4):
            xo, ho = xl ^ (dx % 2), xh ^ (dx // 2)
            copies.append(
                rdma(inc.at[pl.ds(lo + xo * 2, 2), :, ho], xin.at[k, me_x], dev(xo, y, core, z, ho))
            )
        return copies

    def x_sum(k, lo, copies):
        for c in copies:
            c.wait_recv()
        total = inc[pl.ds(lo + xl * 2, 2), :, xh]
        for dx in range(1, 4):
            total = total + xin[k, (xh ^ (dx // 2)) * 2 + (xl ^ (dx % 2))]
        xin[k, me_x] = total

    pair_add(pair0, 0, 4)
    x0 = x_send(0, 0)

    for c in gather:
        c.wait_recv()
    tf[...] = tg[0] + tg[1]

    def split(value):
        hi = value.astype(BF16).astype(F32)
        mid = (value - hi).astype(BF16).astype(F32)
        return hi, mid, value - hi - mid

    wide = lax.broadcasted_iota(jnp.int32, (128, 128), 0)
    pick = lax.broadcasted_iota(jnp.int32, (8, 128), 1) == (
        lax.broadcasted_iota(jnp.int32, (8, 128), 0) + af * 8
    )
    lanes = lax.broadcasted_iota(jnp.int32, (8, 128), 1).astype(F32)
    rows8 = []
    for k in range(9):
        j = (pa + k) % 16
        one, two = cls[0, pl.ds(j, 1), :], cls[1, pl.ds(j, 1), :]
        hot[:, k * 128 : (k + 1) * 128] = ((wide == one) | (wide == two)).astype(F32).astype(BF16)
        i = (pa + 16 - k) % 16
        ends = [
            jnp.sum(jnp.where(pick, cls[e, pl.ds(i, 1), :].astype(F32), 0.0), axis=1, keepdims=True) for e in range(2)
        ]
        rows8.append(((lanes == ends[0]) | (lanes == ends[1])).astype(F32))
    rows8.append(jnp.zeros((8, 128), F32))
    rows80 = jnp.concatenate(rows8, axis=0).astype(BF16)
    t8 = jnp.concatenate([*split(tf[pl.ds(pl.multiple_of(af * 8, 8), 8), :]), jnp.zeros((8, 128), F32)], axis=0)
    t8 = jnp.dot(t8.astype(BF16), hot[...], preferred_element_type=F32)
    own[...] = t8[0:8] + t8[8:16] + t8[16:24]
    others = sum(
        lax.dot_general(rows80, part.astype(BF16), (((1,), (1,)), ((), ())), preferred_element_type=F32)
        for part in split(tf[...])
    )
    for k in range(9):
        nsend[k] = others[k * 8 : (k + 1) * 8]
    oth[0] = nsend[0]

    forward(3)
    for x in range(2):
        put(4 + x * 4, tdot(ow[0:A, x * 256 : x * 256 + 256], ra[:, pl.ds(side(wrap(x, y == 3)), 256)]))
        put(6 + x * 4, tdot(ra[:, x * 256 : x * 256 + 256], ow[0:A, pl.ds(side(wrap(1 - x, y == 3)), 256)]))
        put(5 + x * 4, tdot(ow[A:KC, x * 256 : x * 256 + 256], rb[:, pl.ds(side(wrap(1 - x, y == 0)), 256)]))
        put(7 + x * 4, tdot(rb[:, x * 256 : x * 256 + 256], ow[A:KC, pl.ds(side(wrap(x, y == 0)), 256)]))
    pair1 = pair_sum(4, 8)

    x_sum(0, 0, x0)
    last = []
    for dz in range(1, 8):
        zo = (z + dz) % 8
        last.append(rdma(xin.at[0, me_x, :, zo], fin0.at[z], dev(xl, y, core, zo, xh)))
    fin0[z] = xin[0, me_x, :, z]

    flows = []
    for g in range(4):
        for way in (1, -1):
            steps = 3 if (g % 2 == 0) == (way == 1) else 4
            flows.append(dict(lo=4 + g * 2, way=way, steps=steps, target=up if way > 0 else down))

    def z_step(s):
        for f, flow in enumerate(flows):
            if s > flow["steps"]:
                continue
            if s:
                flow["copy"].wait_recv()
            if s == flow["steps"]:
                continue
            tiles = pl.ds(flow["lo"], 2)
            here = (z + flow["way"] * (flow["steps"] - s) + 16) % 8
            if s == 0:
                src = inc.at[tiles, here]
            else:
                src = zl.at[f, s - 1]
                src[...] = src[...] + inc[tiles, here]
            flow["copy"] = rdma(src, zl.at[f, s], flow["target"])

    pair_add(pair1, 4, 8)
    z_step(0)
    z_step(1)

    for p in range(4):
        for d in y_2[p]:
            d.wait_recv()
    at_a = pl.multiple_of(jnp.where(y < 2, 0, FA), 16)
    at_b = pl.multiple_of(A + jnp.where(y < 2, 0, FB), 16)
    for x in range(2):
        mine_x = side(wrap(x, y >= 2))
        other_x = side(wrap(x, y < 2))
        put(
            12 + x * 2,
            tdot(ow[pl.ds(at_a, FA), x * 256 : x * 256 + 256], fa[:, pl.ds(mine_x, 256)])
            + tdot(ow[pl.ds(at_b, FB), x * 256 : x * 256 + 256], fb[:, pl.ds(mine_x, 256)]),
        )
        put(
            13 + x * 2,
            tdot(fa[:, x * 256 : x * 256 + 256], ow[pl.ds(at_a, FA), pl.ds(other_x, 256)])
            + tdot(fb[:, x * 256 : x * 256 + 256], ow[pl.ds(at_b, FB), pl.ds(other_x, 256)]),
        )
    pair2 = pair_sum(12, 4)
    for k in range(1, 9):
        last.append(rdma(nsend.at[k], oth.at[k], {"pa": (pa + 16 - k) % 16, "af": af}))
    z_step(2)
    pair_add(pair2, 12, 4)
    x2 = x_send(1, 12)
    z_step(3)
    z_step(4)
    for g in range(4):
        lo = 4 + g * 2
        rz[g * 2 : g * 2 + 2] = (
            inc[lo : lo + 2, z] + zl[2 * g, flows[2 * g]["steps"] - 1] + zl[2 * g + 1, flows[2 * g + 1]["steps"] - 1]
        )
    for dx in range(4):
        xo, ho = xl ^ (dx % 2), xh ^ (dx // 2)
        base = xo * 4
        if dx:
            last.append(rdma(rz.at[pl.ds(base, 2), ho], fin1.at[me_x, 0:2], dev(xo, y, core, z, ho)))
        else:
            fin1[me_x, 0:2] = rz[pl.ds(base, 2), ho]
        for slot, yo in ((2, yp), (3, ym)):
            last.append(rdma(rz.at[base + slot, ho], fin1.at[me_x, slot], dev(xo, yo, core, z, ho)))

    x_sum(1, 12, x2)
    for dz in range(8):
        zo = (z + dz) % 8
        last.append(rdma(xin.at[1, me_x, 1, zo], fin2.at[z, 1], dev(xl, y2, core, zo, xh)))
        if dz:
            last.append(rdma(xin.at[1, me_x, 0, zo], fin2.at[z, 0], dev(xl, y, core, zo, xh)))
    fin2[z, 0] = xin[1, me_x, 0, z]
    for c in last:
        c.wait_recv()

    def total(parts):
        return functools.reduce(lambda p, q: p + q, parts)

    cross[:, 0:256] = total([fin0[s, 0] for s in range(8)])
    cross[:, 256:512] = total([fin1[s, t] for t in (0, 3) for s in range(4)])
    cross[:, 512:768] = total([fin2[s, t] for t in range(2) for s in range(8)])
    cross[:, 768:1024] = total([fin1[s, t] for t in (1, 2) for s in range(4)])
    cross[:, 1024:1280] = total([fin0[s, 1] for s in range(8)])
    shift = pl.multiple_of(core * 128, 128)
    for k in range(9):
        here = slice(k * 128, (k + 1) * 128)
        out_ref[:, here] = cross[:, pl.ds(pl.multiple_of(shift + k * 128, 128), 128)] / jnp.sqrt(
            own[:, here] * oth[k] + eps_norm
        )
    for c in started:
        c.wait_send()


def slopes(degrees):
    return jnp.tan(degrees.astype(F32) * (math.pi / 180.0))


def shards(spectra, tilt_min, tilt_max, tilt_axis):
    vmem = pl.BlockSpec(memory_space=pltpu.VMEM)
    scratch = [
        pltpu.VMEM((2, 2 * KC, 128), BF16),
        pltpu.VMEM((KC, 512), BF16),
        pltpu.VMEM((KC, 512), BF16),
        pltpu.VMEM((A, 512), BF16),
        pltpu.VMEM((B, 512), BF16),
        pltpu.VMEM((FA, 512), BF16),
        pltpu.VMEM((FB, 512), BF16),
        pltpu.VMEM((16, 2, 8, 2, 8, 256), F32),
        pltpu.VMEM((16, 8, 2, 8, 256), F32),
        pltpu.VMEM((2, 4, 2, 8, 8, 256), F32),
        pltpu.VMEM((8, 4, 2, 2, 8, 256), F32),
        pltpu.VMEM((8, 2, 8, 256), F32),
        pltpu.VMEM((8, 2, 8, 256), F32),
        pltpu.VMEM((4, 4, 8, 256), F32),
        pltpu.VMEM((8, 2, 8, 256), F32),
        pltpu.VMEM((2 * KC, 128), BF16),
        pltpu.VMEM((2 * KC, 128), BF16),
        pltpu.VMEM((128, 128), F32),
        pltpu.VMEM((2, 4, 16, 128), F32),
        pltpu.VMEM((2, 128, 128), F32),
        pltpu.VMEM((128, 128), F32),
        pltpu.VMEM((2, 16, 128), jnp.int32),
        pltpu.VMEM((128, 1152), BF16),
        pltpu.VMEM((8, 1152), F32),
        pltpu.VMEM((9, 8, 128), F32),
        pltpu.VMEM((9, 8, 128), F32),
        pltpu.VMEM((8, 1280), F32),
        pltpu.SemaphoreType.DMA((2,)),
        pltpu.SemaphoreType.DMA((N_SEM,)),
        pltpu.SemaphoreType.DMA((N_SEM,)),
    ]
    tilts = [t.reshape(16, 128) for t in (tilt_min, tilt_max, tilt_axis)]
    return pl.pallas_call(
        kernel,
        out_shape=jax.ShapeDtypeStruct((8, 1152), F32),
        in_specs=[pl.BlockSpec(memory_space=pl.ANY), vmem, vmem, vmem],
        out_specs=vmem,
        scratch_shapes=scratch,
        compiler_params=pltpu.CompilerParams(
            collective_id=0, has_side_effects=True, vmem_limit_bytes=56 * 2**20
        ),
    )(spectra, *tilts)


def solution(mesh):
    in_specs = (P(None, "af", "pa"), P(), P(), P())
    out_specs = P(("pa", "af"), None)
    return jax.shard_map(shards, mesh=mesh, in_specs=in_specs, out_specs=out_specs, check_vma=False)
```

```python
import functools
import math

import jax
import jax.numpy as jnp
from jax import lax
from jax.experimental import pallas as pl
from jax.experimental.pallas import tpu as pltpu
from jax.sharding import PartitionSpec as P

MESH = pl.DeviceIdType.MESH
F32 = jnp.float32
BF16 = jnp.bfloat16

G = 48
HALF = 25
VD = 3600
Q = 464
KC = 4 * Q
H1, H2 = 240, 224
A = 2 * Q + H1
B = 2 * Q + H2
MID = VD - KC
CHUNKS = ((0, 96), (96, 96), (192, 96), (288, 96), (384, 80))
T_LO, T_HI, N_T = 46, 70, 25
eps_norm = 1e-06


def coords():
    pa = lax.axis_index("pa")
    af = lax.axis_index("af")
    return pa // 8, (pa // 2) % 4, pa % 2, af // 2, af % 2


def dev(xl, y, core, z, xh):
    return {"pa": (xl * 4 + y) * 2 + core, "af": z * 2 + xh}


def tdot(lhs, rhs):
    return lax.dot_general(lhs, rhs, (((0,), (0,)), ((), ())), preferred_element_type=F32)


def cells(first, shape):
    v = (first + lax.broadcasted_iota(jnp.int32, shape, 0)).astype(F32)
    q = jnp.floor((v + 0.5) * (1.0 / HALF))
    iz = v - q * HALF
    ix = jnp.floor((q + 0.5) * (1.0 / G))
    iy = q - ix * G
    fx = jnp.where(ix < G // 2, ix, ix - G)
    fy = jnp.where(iy < G // 2, iy, iy - G)
    return fx, fy, iz

N_SEM = 176


def kernel(spec_hbm, tmin_ref, tmax_ref, axis_ref, out_ref, raw, m, wt, o, ow, ra, rb, rbw, acc, inc, xin0, xin1, xin2,
           zl, rz, fin0, fin1, fin2, fin3, pw, cm, tt, tl, tg, tf, cls, hot, own, nsend, oth, cross, load_sem, ssem, rsem):
    xl, y, core, z, xh = coords()
    pa = lax.axis_index("pa")
    af = lax.axis_index("af")
    yp, ym = (y + 1) % 4, (y + 3) % 4
    zp, zm = (z + 1) % 8, (z + 7) % 8
    me_x = xh * 2 + xl
    started = []

    def rdma(src, dst, target):
        i = len(started)
        c = pltpu.make_async_remote_copy(
            src_ref=src, dst_ref=dst, send_sem=ssem.at[i], recv_sem=rsem.at[i], device_id=target, device_id_type=MESH
        )
        c.start()
        started.append(c)
        return c

    loads = []
    for first, n in ((core * KC, MID), (MID, KC - MID), ((1 - core) * KC, MID)):
        here = pl.ds(first if isinstance(first, int) else pl.multiple_of(first, 16), n)
        for p in range(2):
            c = pltpu.make_async_copy(spec_hbm.at[p, here], raw.at[p, here], load_sem.at[len(loads)])
            c.start()
            loads.append(c)
    barrier = pltpu.get_barrier_semaphore()
    peers = [
        dev(xl, y, 1 - core, z, xh),
        dev(1 - xl, y, core, z, xh),
        dev(1 - xl, y, 1 - core, z, xh),
        dev(xl, yp, core, z, xh),
        dev(xl, ym, core, z, xh),
        dev(xl, y, core, z, 1 - xh),
        dev(xl, y, core, zp, xh),
        dev(xl, y, core, zm, xh),
    ]
    for peer in peers:
        pl.semaphore_signal(barrier, inc=1, device_id=peer, device_id_type=MESH)
    raw[:, VD:, :] = jnp.zeros((2, 2 * KC - VD, 128), BF16)

    cls[0] = axis_ref[...] * 50 + (-T_LO - tmin_ref[...])
    cls[1] = axis_ref[...] * 50 + (N_T - T_LO + tmax_ref[...])
    lower = slopes(tmin_ref[pl.ds(pa, 1), :])
    upper = slopes(tmax_ref[pl.ds(pa, 1), :])
    axis = axis_ref[pl.ds(pa, 1), :]
    lane = lax.broadcasted_iota(jnp.int32, (1, 128), 1)
    c_axis = (lane >= 50).astype(jnp.int32)
    c_side = ((lane - c_axis * 50) >= 25).astype(jnp.int32)
    c_slope = slopes(lane - c_axis * 50 - c_side * 25 + T_LO)
    c_slope = jnp.where(lane < 100, c_slope, -1.0)

    def own_col(dx, dc):
        return pl.multiple_of(((xl ^ dx) * 2 + (core ^ dc)) * 128, 128)

    def by_chunk(half, body):
        def slot(s, carry):
            first = half * KC + (y + 3 - s) % 4 * Q
            for r0, n in CHUNKS:
                body(pl.multiple_of(first + r0, 16), pl.ds(pl.multiple_of(s * Q + r0, 16), n), n)
            return carry

        lax.fori_loop(0, 4, slot, 0)

    def mask_half(half):
        def body(r0, to, n):
            fx, fy, iz = cells(af * VD + r0, (n, 128))
            u = jnp.where(axis == 1, fx, fy)
            a = jnp.abs(u)
            b = jnp.where(u >= 0.0, -iz, iz)
            keep = ((a * lower <= b) & (b <= a * upper)).astype(F32)
            for p in range(2):
                m[p, half, to, :] = (raw[p, pl.ds(r0, n), :].astype(F32) * keep).astype(BF16)

        by_chunk(half, body)

    for c in loads[:4]:
        c.wait()
    mask_half(core)
    pl.semaphore_wait(barrier, len(peers))

    col = own_col(0, 0)
    o[:, pl.ds(col, 128)] = m[xl, core]

    y1 = [[] for _ in range(4)]

    def to_minus(p, r0, n):
        c = pl.ds(own_col(p // 2, p % 2), 128)
        y1[p].append(rdma(o.at[pl.ds(r0, n), c], ra.at[pl.ds(r0 - Q, n), c], dev(xl, ym, core, z, xh)))

    def to_plus(p, r0, n, to):
        c = pl.ds(own_col(p // 2, p % 2), 128)
        y1[p].append(rdma(o.at[pl.ds(r0, n), c], rb.at[pl.ds(to, n), c], dev(xl, yp, core, z, xh)))

    def y_send(p):
        to_plus(p, 3 * Q, Q, 0)
        to_minus(p, Q, A)
        to_plus(p, 0, Q, Q)
        to_plus(p, 2 * Q + H1, H2, 2 * Q)

    def to_x(half, r0, n, target):
        return rdma(m.at[1 - xl, half, pl.ds(r0, n)], o.at[pl.ds(r0, n), pl.ds(col, 128)], target)

    y_send(0)
    x_same = [to_x(core, r0, 2 * Q, dev(1 - xl, y, core, z, xh)) for r0 in (2 * Q, 0)]
    for c in loads[4:]:
        c.wait()
    mask_half(1 - core)
    sib = rdma(m.at[xl, 1 - core], o.at[:, pl.ds(col, 128)], dev(xl, y, 1 - core, z, xh))
    x_other = [to_x(1 - core, q * Q, Q, dev(1 - xl, y, 1 - core, z, xh)) for q in (3, 2, 0, 1)]

    for half in range(2):

        def powers(r0, to, n, half=half):
            fx, fy, iz = cells(af * VD + r0, (n, 128))
            re = m[0, half, to, :].astype(F32)
            im = m[1, half, to, :].astype(F32)
            w = jnp.where((iz < 0.5) | (iz > 23.5), 1.0, 2.0)
            pw[half, to, :] = (w * (re * re + im * im)).astype(BF16)
            u = jnp.where(c_axis == 1, fx, fy)
            side = (u < 0.0).astype(jnp.int32)
            keep = (iz <= jnp.abs(u) * c_slope) & (side == c_side) & (lane < 100)
            cm[half, to, :] = keep.astype(F32).astype(BF16)

        by_chunk(half, powers)
    tt[...] = tdot(pw[0], cm[0]) + tdot(pw[1], cm[1])

    def rows16(zz):
        return pl.ds(pl.multiple_of(((zz + 16) % 8) * 16, 16), 16)

    up, down = dev(xl, y, core, zp, xh), dev(xl, y, core, zm, xh)
    t_flows = [dict(way=1, steps=3, target=up), dict(way=-1, steps=4, target=down)]

    def t_step(s):
        for f, flow in enumerate(t_flows):
            if s > flow["steps"]:
                continue
            if s:
                flow["copy"].wait_recv()
            if s == flow["steps"]:
                continue
            here = rows16(z + flow["way"] * (flow["steps"] - s))
            if s == 0:
                src = tt.at[here]
            else:
                src = tl.at[f, s - 1]
                src[...] = src[...] + tt[here, :]
            flow["copy"] = rdma(src, tl.at[f, s], flow["target"])

    t_step(0)

    def weights(r0, to, n):
        iz = cells(af * VD + r0, (n, 128))[2]
        wt[to, :] = jnp.where((iz < 0.5) | (iz > 23.5), 1.0, 2.0).astype(BF16)

    by_chunk(core, weights)

    def weigh(dst, src, x, n):
        for dc in range(2):
            here = pl.ds(pl.multiple_of(x * 256 + dc * 128, 128), 128)
            dst[:, here] = src[0:n, here] * wt[0:n, :]

    sib.wait_recv()
    y_send(1)
    t_step(1)
    weigh(ow, o, xl, KC)
    t_step(2)
    x_same[0].wait_recv()
    to_plus(2, 3 * Q, Q, 0)
    to_minus(2, 2 * Q, Q + H1)
    to_plus(2, 2 * Q + H1, H2, 2 * Q)
    t_step(3)
    x_same[1].wait_recv()
    to_plus(2, 0, Q, Q)
    to_minus(2, Q, Q)
    t_step(4)
    mine16 = rows16(z)
    tg[xh, mine16, :] = tt[mine16, :] + tl[0, 2] + tl[1, 3]
    gather = []
    for dz in range(8):
        for dh in range(2):
            if dz or dh:
                part = tg.at[xh, mine16]
                gather.append(rdma(part, part, dev(xl, y, core, (z + dz) % 8, xh ^ dh)))

    x_other[0].wait_recv()
    to_plus(3, 3 * Q, Q, 0)
    to_minus(3, 3 * Q, H1)
    x_other[1].wait_recv()
    to_plus(3, 2 * Q + H1, H2, 2 * Q)
    to_minus(3, 2 * Q, Q)
    for p in range(2):
        for d in y1[p]:
            d.wait_recv()
    weigh(rbw, rb, xl, 2 * Q)
    x_other[2].wait_recv()
    to_plus(3, 0, Q, Q)
    x_other[3].wait_recv()
    to_minus(3, Q, Q)
    weigh(ow, o, 1 - xl, KC)

    def put(tile, value):
        acc[tile] = value.reshape(2, 8, 2, 8, 256)

    def side(x):
        return pl.multiple_of(x * 256, 256)

    def wrap(x, cond):
        return x ^ cond.astype(jnp.int32)

    def pair_sum(lo, n):
        tiles = pl.ds(lo, n)
        return rdma(acc.at[tiles, 1 - core], inc.at[tiles], dev(xl, y, 1 - core, z, xh))

    def pair_add(copy, lo, n):
        copy.wait_recv()
        for t in range(lo, lo + n):
            inc[t] = inc[t] + acc[t, core]

    for x in range(2):
        for slot, xo in ((0, x), (1, 1 - x)):
            put(x * 2 + slot, tdot(ow[:, x * 256 : x * 256 + 256], o[:, xo * 256 : xo * 256 + 256]))
    pair0 = pair_sum(0, 4)

    def x_send(lo, n, buf):
        copies = []
        for dx in range(1, 4):
            xo, ho = xl ^ (dx % 2), xh ^ (dx // 2)
            copies.append(
                rdma(inc.at[pl.ds(lo + xo * n, n), :, ho], buf.at[me_x], dev(xo, y, core, z, ho))
            )
        return copies

    def x_sum(lo, n, buf, copies):
        for c in copies:
            c.wait_recv()
        total = inc[pl.ds(lo + xl * n, n), :, xh]
        for dx in range(1, 4):
            total = total + buf[(xh ^ (dx // 2)) * 2 + (xl ^ (dx % 2))]
        buf[me_x] = total

    pair_add(pair0, 0, 4)
    x0 = x_send(0, 2, xin0)

    for c in gather:
        c.wait_recv()
    tf[...] = tg[0] + tg[1]

    def split(value):
        hi = value.astype(BF16).astype(F32)
        mid = (value - hi).astype(BF16).astype(F32)
        return hi, mid, value - hi - mid

    wide = lax.broadcasted_iota(jnp.int32, (128, 128), 0)
    pick = lax.broadcasted_iota(jnp.int32, (8, 128), 1) == (
        lax.broadcasted_iota(jnp.int32, (8, 128), 0) + af * 8
    )
    lanes = lax.broadcasted_iota(jnp.int32, (8, 128), 1).astype(F32)
    rows8 = []
    for k in range(9):
        j = (pa + k) % 16
        one, two = cls[0, pl.ds(j, 1), :], cls[1, pl.ds(j, 1), :]
        hot[:, k * 128 : (k + 1) * 128] = ((wide == one) | (wide == two)).astype(F32).astype(BF16)
        i = (pa + 16 - k) % 16
        ends = [
            jnp.sum(jnp.where(pick, cls[e, pl.ds(i, 1), :].astype(F32), 0.0), axis=1, keepdims=True) for e in range(2)
        ]
        rows8.append(((lanes == ends[0]) | (lanes == ends[1])).astype(F32))
    rows8.append(jnp.zeros((8, 128), F32))
    rows80 = jnp.concatenate(rows8, axis=0).astype(BF16)
    t8 = jnp.concatenate([*split(tf[pl.ds(pl.multiple_of(af * 8, 8), 8), :]), jnp.zeros((8, 128), F32)], axis=0)
    t8 = jnp.dot(t8.astype(BF16), hot[...], preferred_element_type=F32)
    own[...] = t8[0:8] + t8[8:16] + t8[16:24]
    others = sum(
        lax.dot_general(rows80, part.astype(BF16), (((1,), (1,)), ((), ())), preferred_element_type=F32)
        for part in split(tf[...])
    )
    for k in range(9):
        nsend[k] = others[k * 8 : (k + 1) * 8]
    oth[0] = nsend[0]

    for p in range(2, 4):
        for d in y1[p]:
            d.wait_recv()
    weigh(rbw, rb, 1 - xl, 2 * Q)

    def cols(ref, x, first, n):
        return ref[first : first + n, pl.ds(side(x), 256)]

    for x in range(2):
        put(4 + x, tdot(cols(ow, x, 0, A), cols(ra, wrap(x, y == 3), 0, A)))
        put(6 + x, tdot(cols(ra, x, 0, A), cols(ow, wrap(1 - x, y == 3), 0, A)))
    pair1 = pair_sum(4, 4)
    for x in range(2):
        put(
            8 + x,
            tdot(cols(ow, x, 0, Q), cols(rb, wrap(1 - x, y == 0), 0, Q))
            + tdot(cols(ow, x, 3 * Q + H1, H2), cols(rb, wrap(1 - x, y == 0), 2 * Q, H2)),
        )
        put(
            10 + x,
            tdot(cols(rb, x, 0, Q), cols(ow, wrap(x, y == 0), 0, Q))
            + tdot(cols(rb, x, 2 * Q, H2), cols(ow, wrap(x, y == 0), 3 * Q + H1, H2)),
        )
    pair2 = pair_sum(8, 4)

    flows = []
    for g in range(3):
        for way in (1, -1):
            steps = 3 if (g % 2 == 0) == (way == 1) else 4
            flows.append(dict(lo=4 + g * 2, way=way, steps=steps, target=up if way > 0 else down))

    def z_step(s, which=(0, 6)):
        for f, flow in list(enumerate(flows))[which[0] : which[1]]:
            if s > flow["steps"]:
                continue
            if s:
                flow["copy"].wait_recv()
            if s == flow["steps"]:
                continue
            tiles = pl.ds(flow["lo"], 2)
            here = (z + flow["way"] * (flow["steps"] - s) + 16) % 8
            if s == 0:
                src = inc.at[tiles, here]
            else:
                src = zl.at[f, s - 1]
                src[...] = src[...] + inc[tiles, here]
            flow["copy"] = rdma(src, zl.at[f, s], flow["target"])

    pair_add(pair1, 4, 4)
    z_step(0, (0, 4))
    for x in range(2):
        put(12 + x * 2, tdot(cols(rbw, x, 0, 2 * Q), cols(ra, wrap(x, ym >= 2), 0, 2 * Q)))
        put(13 + x * 2, tdot(cols(ra, x, 0, 2 * Q), cols(rbw, wrap(x, yp >= 2), 0, 2 * Q)))
    pair3 = pair_sum(12, 4)
    pair_add(pair2, 8, 4)
    z_step(0, (4, 6))
    x1 = x_send(10, 1, xin1)
    x_sum(0, 2, xin0, x0)
    last = []
    for dz in range(1, 8):
        zo = (z + dz) % 8
        last.append(rdma(xin0.at[me_x, :, zo], fin0.at[z], dev(xl, y, core, zo, xh)))
    fin0[z] = xin0[me_x, :, z]
    pair_add(pair3, 12, 4)
    x2 = x_send(12, 2, xin2)
    z_step(1)
    for k in range(1, 9):
        last.append(rdma(nsend.at[k], oth.at[k], {"pa": (pa + 16 - k) % 16, "af": af}))
    x_sum(10, 1, xin1, x1)
    for dz in range(8):
        zo = (z + dz) % 8
        last.append(rdma(xin1.at[me_x, 0, zo], fin1.at[z], dev(xl, ym, core, zo, xh)))
    z_step(2)
    x_sum(12, 2, xin2, x2)
    for dz in range(8):
        zo = (z + dz) % 8
        last.append(rdma(xin2.at[me_x, 0, zo], fin2.at[z, 0], dev(xl, ym, core, zo, xh)))
        last.append(rdma(xin2.at[me_x, 1, zo], fin2.at[z, 1], dev(xl, yp, core, zo, xh)))
    z_step(3)
    z_step(4)
    for g in range(3):
        lo = 4 + g * 2
        rz[lo - 4 : lo - 2] = (
            inc[lo : lo + 2, z] + zl[2 * g, flows[2 * g]["steps"] - 1] + zl[2 * g + 1, flows[2 * g + 1]["steps"] - 1]
        )
    for dx in range(4):
        xo, ho = xl ^ (dx % 2), xh ^ (dx // 2)
        for slot in range(3):
            if slot == 1:
                last.append(rdma(rz.at[2 + xo, ho], fin3.at[me_x, 1], dev(xo, yp, core, z, ho)))
            elif dx:
                last.append(rdma(rz.at[2 * slot + xo, ho], fin3.at[me_x, slot], dev(xo, y, core, z, ho)))
            else:
                fin3[me_x, slot] = rz[2 * slot + xo, ho]
    for c in last:
        c.wait_recv()

    def total(parts):
        return functools.reduce(lambda p, q: p + q, parts)

    cross[:, 0:256] = total([fin0[s, 0] for s in range(8)])
    cross[:, 256:512] = total([fin1[s] for s in range(8)] + [fin3[s, 0] for s in range(4)])
    cross[:, 512:768] = total([fin2[s, t] for t in range(2) for s in range(8)])
    cross[:, 768:1024] = total([fin3[s, t] for t in (1, 2) for s in range(4)])
    cross[:, 1024:1280] = total([fin0[s, 1] for s in range(8)])
    shift = pl.multiple_of(core * 128, 128)
    for k in range(9):
        here = slice(k * 128, (k + 1) * 128)
        out_ref[:, here] = cross[:, pl.ds(pl.multiple_of(shift + k * 128, 128), 128)] / jnp.sqrt(
            own[:, here] * oth[k] + eps_norm
        )
    for c in started:
        c.wait_send()


def slopes(degrees):
    return jnp.tan(degrees.astype(F32) * (math.pi / 180.0))


def shards(spectra, tilt_min, tilt_max, tilt_axis):
    vmem = pl.BlockSpec(memory_space=pltpu.VMEM)
    scratch = [
        pltpu.VMEM((2, 2 * KC, 128), BF16),
        pltpu.VMEM((2, 2, KC, 128), BF16),
        pltpu.VMEM((KC, 128), BF16),
        pltpu.VMEM((KC, 512), BF16),
        pltpu.VMEM((KC, 512), BF16),
        pltpu.VMEM((A, 512), BF16),
        pltpu.VMEM((B, 512), BF16),
        pltpu.VMEM((2 * Q, 512), BF16),
        pltpu.VMEM((16, 2, 8, 2, 8, 256), F32),
        pltpu.VMEM((16, 8, 2, 8, 256), F32),
        pltpu.VMEM((4, 2, 8, 8, 256), F32),
        pltpu.VMEM((4, 1, 8, 8, 256), F32),
        pltpu.VMEM((4, 2, 8, 8, 256), F32),
        pltpu.VMEM((6, 4, 2, 2, 8, 256), F32),
        pltpu.VMEM((6, 2, 8, 256), F32),
        pltpu.VMEM((8, 2, 8, 256), F32),
        pltpu.VMEM((8, 8, 256), F32),
        pltpu.VMEM((8, 2, 8, 256), F32),
        pltpu.VMEM((4, 3, 8, 256), F32),
        pltpu.VMEM((2, KC, 128), BF16),
        pltpu.VMEM((2, KC, 128), BF16),
        pltpu.VMEM((128, 128), F32),
        pltpu.VMEM((2, 4, 16, 128), F32),
        pltpu.VMEM((2, 128, 128), F32),
        pltpu.VMEM((128, 128), F32),
        pltpu.VMEM((2, 16, 128), jnp.int32),
        pltpu.VMEM((128, 1152), BF16),
        pltpu.VMEM((8, 1152), F32),
        pltpu.VMEM((9, 8, 128), F32),
        pltpu.VMEM((9, 8, 128), F32),
        pltpu.VMEM((8, 1280), F32),
        pltpu.SemaphoreType.DMA((6,)),
        pltpu.SemaphoreType.DMA((N_SEM,)),
        pltpu.SemaphoreType.DMA((N_SEM,)),
    ]
    tilts = [t.reshape(16, 128) for t in (tilt_min, tilt_max, tilt_axis)]
    return pl.pallas_call(
        kernel,
        out_shape=jax.ShapeDtypeStruct((8, 1152), F32),
        in_specs=[pl.BlockSpec(memory_space=pl.ANY), vmem, vmem, vmem],
        out_specs=vmem,
        scratch_shapes=scratch,
        compiler_params=pltpu.CompilerParams(
            collective_id=0, has_side_effects=True, vmem_limit_bytes=56 * 2**20
        ),
    )(spectra, *tilts)


def solution(mesh):
    in_specs = (P(None, "af", "pa"), P(), P(), P())
    out_specs = P(("pa", "af"), None)
    return jax.shard_map(shards, mesh=mesh, in_specs=in_specs, out_specs=out_specs, check_vma=False)
```

```python
import functools
import math

import jax
import jax.numpy as jnp
from jax import lax
from jax.experimental import pallas as pl
from jax.experimental.pallas import tpu as pltpu
from jax.sharding import PartitionSpec as P

MESH = pl.DeviceIdType.MESH
F32 = jnp.float32
BF16 = jnp.bfloat16

G = 48
HALF = 25
VD = 3600
Q = 464
KC = 4 * Q
H1, H2 = 240, 224
A = 2 * Q + H1
B = 2 * Q + H2
MID = VD - KC
CHUNKS = ((0, 96), (96, 96), (192, 96), (288, 96), (384, 80))
T_LO, T_HI, N_T = 46, 70, 25
eps_norm = 1e-06


def coords():
    pa = lax.axis_index("pa")
    af = lax.axis_index("af")
    return pa // 8, (pa // 2) % 4, pa % 2, af // 2, af % 2


def dev(xl, y, core, z, xh):
    return {"pa": (xl * 4 + y) * 2 + core, "af": z * 2 + xh}


def tdot(lhs, rhs):
    return lax.dot_general(lhs, rhs, (((0,), (0,)), ((), ())), preferred_element_type=F32)


def cells(first, shape):
    v = (first + lax.broadcasted_iota(jnp.int32, shape, 0)).astype(F32)
    q = jnp.floor((v + 0.5) * (1.0 / HALF))
    iz = v - q * HALF
    ix = jnp.floor((q + 0.5) * (1.0 / G))
    iy = q - ix * G
    fx = jnp.where(ix < G // 2, ix, ix - G)
    fy = jnp.where(iy < G // 2, iy, iy - G)
    return fx, fy, iz

N_SEM = 256


def kernel(spec_hbm, tmin_hbm, tmax_hbm, axis_hbm, out_ref, tilt, raw, m, wt, o, ow, ra, rb, rbw, acc, inc, xin0, xin2,
           zl, rz, fin0, fin1, fin2, fin3, pw, cm, tt, tl, tg, tf, cls, hot, own, nsend, oth, cross, load_sem, ssem, rsem):
    xl, y, core, z, xh = coords()
    pa = lax.axis_index("pa")
    af = lax.axis_index("af")
    yp, ym = (y + 1) % 4, (y + 3) % 4
    zp, zm = (z + 1) % 8, (z + 7) % 8
    me_x = xh * 2 + xl
    started = []

    def rdma(src, dst, target):
        i = len(started)
        c = pltpu.make_async_remote_copy(
            src_ref=src, dst_ref=dst, send_sem=ssem.at[i], recv_sem=rsem.at[i], device_id=target, device_id_type=MESH
        )
        c.start()
        started.append(c)
        return c

    loads = []
    for i, ref in enumerate((tmin_hbm, tmax_hbm, axis_hbm)):
        c = pltpu.make_async_copy(ref, tilt.at[i], load_sem.at[i])
        c.start()
        loads.append(c)
    tmin_ref, tmax_ref, axis_ref = tilt.at[0], tilt.at[1], tilt.at[2]
    for first, n in ((core * KC, MID), (MID, KC - MID), ((1 - core) * KC, MID)):
        here = pl.ds(first if isinstance(first, int) else pl.multiple_of(first, 16), n)
        for p in range(2):
            c = pltpu.make_async_copy(spec_hbm.at[p, here], raw.at[p, here], load_sem.at[len(loads)])
            c.start()
            loads.append(c)
    barrier = pltpu.get_barrier_semaphore()
    peers = [
        dev(xl, y, 1 - core, z, xh),
        dev(1 - xl, y, core, z, xh),
        dev(1 - xl, y, 1 - core, z, xh),
        dev(xl, yp, core, z, xh),
        dev(xl, ym, core, z, xh),
        dev(xl, y, core, z, 1 - xh),
        dev(xl, y, core, zp, xh),
        dev(xl, y, core, zm, xh),
    ]
    for peer in peers:
        pl.semaphore_signal(barrier, inc=1, device_id=peer, device_id_type=MESH)
    raw[:, VD:, :] = jnp.zeros((2, 2 * KC - VD, 128), BF16)

    for c in loads[:3]:
        c.wait()
    cls[0] = axis_ref[...] * 50 + (-T_LO - tmin_ref[...])
    cls[1] = axis_ref[...] * 50 + (N_T - T_LO + tmax_ref[...])
    lower = slopes(tmin_ref[pl.ds(pa, 1), :])
    upper = slopes(tmax_ref[pl.ds(pa, 1), :])
    axis = axis_ref[pl.ds(pa, 1), :]
    lane = lax.broadcasted_iota(jnp.int32, (1, 128), 1)
    c_axis = (lane >= 50).astype(jnp.int32)
    c_side = ((lane - c_axis * 50) >= 25).astype(jnp.int32)
    c_slope = slopes(lane - c_axis * 50 - c_side * 25 + T_LO)
    c_slope = jnp.where(lane < 100, c_slope, -1.0)

    def own_col(dx, dc):
        return pl.multiple_of(((xl ^ dx) * 2 + (core ^ dc)) * 128, 128)

    def by_chunk(half, body, slots=(0, 4)):
        def slot(s, carry):
            first = half * KC + (y + 3 - s) % 4 * Q
            for r0, n in CHUNKS:
                body(pl.multiple_of(first + r0, 16), pl.ds(pl.multiple_of(s * Q + r0, 16), n), n)
            return carry

        lax.fori_loop(*slots, slot, 0)

    def mask_half(half, slots=(0, 4)):
        def body(r0, to, n):
            fx, fy, iz = cells(af * VD + r0, (n, 128))
            u = jnp.where(axis == 1, fx, fy)
            a = jnp.abs(u)
            b = jnp.where(u >= 0.0, -iz, iz)
            keep = ((a * lower <= b) & (b <= a * upper)).astype(F32)
            for p in range(2):
                m[p, half, to, :] = (raw[p, pl.ds(r0, n), :].astype(F32) * keep).astype(BF16)

        by_chunk(half, body, slots)

    for c in loads[3:7]:
        c.wait()
    mask_half(core, (2, 4))
    pl.semaphore_wait(barrier, len(peers))

    col = own_col(0, 0)

    y1 = [[] for _ in range(4)]

    def to_minus(p, r0, n):
        c = pl.ds(own_col(p // 2, p % 2), 128)
        y1[p].append(rdma(o.at[pl.ds(r0, n), c], ra.at[pl.ds(r0 - Q, n), c], dev(xl, ym, core, z, xh)))

    def to_plus(p, r0, n, to):
        c = pl.ds(own_col(p // 2, p % 2), 128)
        y1[p].append(rdma(o.at[pl.ds(r0, n), c], rb.at[pl.ds(to, n), c], dev(xl, yp, core, z, xh)))

    def y_high(p):
        to_plus(p, 3 * Q, Q, 0)
        to_minus(p, 2 * Q, Q + H1)
        to_plus(p, 2 * Q + H1, H2, 2 * Q)

    def y_low(p):
        to_plus(p, 0, Q, Q)
        to_minus(p, Q, Q)

    def to_x(half, r0, n, target):
        return rdma(m.at[1 - xl, half, pl.ds(r0, n)], o.at[pl.ds(r0, n), pl.ds(col, 128)], target)

    own_high, own_low = pl.ds(2 * Q, 2 * Q), pl.ds(0, 2 * Q)
    x_same = [to_x(core, 2 * Q, 2 * Q, dev(1 - xl, y, core, z, xh))]
    o[own_high, pl.ds(col, 128)] = m[xl, core, own_high]
    y_high(0)
    mask_half(core, (0, 2))
    x_same.append(to_x(core, 0, 2 * Q, dev(1 - xl, y, core, z, xh)))
    o[own_low, pl.ds(col, 128)] = m[xl, core, own_low]
    y_low(0)
    for c in loads[7:]:
        c.wait()
    mask_half(1 - core)
    sib = rdma(m.at[xl, 1 - core], o.at[:, pl.ds(col, 128)], dev(xl, y, 1 - core, z, xh))
    x_other = [to_x(1 - core, q * Q, Q, dev(1 - xl, y, 1 - core, z, xh)) for q in (3, 2, 0, 1)]

    for half in range(2):

        def powers(r0, to, n, half=half):
            fx, fy, iz = cells(af * VD + r0, (n, 128))
            re = m[0, half, to, :].astype(F32)
            im = m[1, half, to, :].astype(F32)
            w = jnp.where((iz < 0.5) | (iz > 23.5), 1.0, 2.0)
            pw[half, to, :] = (w * (re * re + im * im)).astype(BF16)
            u = jnp.where(c_axis == 1, fx, fy)
            side = (u < 0.0).astype(jnp.int32)
            keep = (iz <= jnp.abs(u) * c_slope) & (side == c_side) & (lane < 100)
            cm[half, to, :] = keep.astype(F32).astype(BF16)

        by_chunk(half, powers)
        if half == 0:
            sib.wait_recv()
            y_high(1)
            y_low(1)
    tt[...] = tdot(pw[0], cm[0]) + tdot(pw[1], cm[1])

    def rows16(zz):
        return pl.ds(pl.multiple_of(((zz + 16) % 8) * 16, 16), 16)

    up, down = dev(xl, y, core, zp, xh), dev(xl, y, core, zm, xh)
    t_flows = [dict(way=1, steps=3, target=up), dict(way=-1, steps=4, target=down)]

    def t_step(s):
        for f, flow in enumerate(t_flows):
            if s > flow["steps"]:
                continue
            if s:
                flow["copy"].wait_recv()
            if s == flow["steps"]:
                continue
            here = rows16(z + flow["way"] * (flow["steps"] - s))
            if s == 0:
                src = tt.at[here]
            else:
                src = tl.at[f, s - 1]
                src[...] = src[...] + tt[here, :]
            flow["copy"] = rdma(src, tl.at[f, s], flow["target"])

    t_step(0)

    def weights(r0, to, n):
        iz = cells(af * VD + r0, (n, 128))[2]
        wt[to, :] = jnp.where((iz < 0.5) | (iz > 23.5), 1.0, 2.0).astype(BF16)

    by_chunk(core, weights)

    def weigh(dst, src, x, n):
        for dc in range(2):
            here = pl.ds(pl.multiple_of(x * 256 + dc * 128, 128), 128)
            dst[:, here] = src[0:n, here] * wt[0:n, :]

    x_same[0].wait_recv()
    y_high(2)
    t_step(1)
    weigh(ow, o, xl, KC)
    x_same[1].wait_recv()
    y_low(2)
    t_step(2)
    x_other[0].wait_recv()
    to_plus(3, 3 * Q, Q, 0)
    to_minus(3, 3 * Q, H1)
    t_step(3)
    x_other[1].wait_recv()
    to_plus(3, 2 * Q + H1, H2, 2 * Q)
    to_minus(3, 2 * Q, Q)
    t_step(4)
    mine16 = rows16(z)
    tg[xh, mine16, :] = tt[mine16, :] + tl[0, 2] + tl[1, 3]
    gather = []
    for dz in range(8):
        for dh in range(2):
            if dz or dh:
                part = tg.at[xh, mine16]
                gather.append(rdma(part, part, dev(xl, y, core, (z + dz) % 8, xh ^ dh)))

    x_other[2].wait_recv()
    to_plus(3, 0, Q, Q)
    x_other[3].wait_recv()
    to_minus(3, Q, Q)
    weigh(ow, o, 1 - xl, KC)

    def put(tile, value):
        acc[tile] = value.reshape(2, 8, 2, 8, 256)

    def side(x):
        return pl.multiple_of(x * 256, 256)

    def wrap(x, cond):
        return x ^ cond.astype(jnp.int32)

    def pair_sum(lo, n):
        tiles = pl.ds(lo, n)
        return rdma(acc.at[tiles, 1 - core], inc.at[tiles], dev(xl, y, 1 - core, z, xh))

    def pair_add(copy, lo, n):
        copy.wait_recv()
        for t in range(lo, lo + n):
            inc[t] = inc[t] + acc[t, core]

    for x in range(2):
        for slot, xo in ((0, x), (1, 1 - x)):
            put(x * 2 + slot, tdot(ow[:, x * 256 : x * 256 + 256], o[:, xo * 256 : xo * 256 + 256]))
    pair0 = pair_sum(0, 4)

    def x_send(lo, n, buf):
        copies = []
        for dx in range(1, 4):
            xo, ho = xl ^ (dx % 2), xh ^ (dx // 2)
            copies.append(
                rdma(inc.at[pl.ds(lo + xo * n, n), :, ho], buf.at[me_x], dev(xo, y, core, z, ho))
            )
        return copies

    def x_sum(lo, n, buf, copies):
        for c in copies:
            c.wait_recv()
        total = inc[pl.ds(lo + xl * n, n), :, xh]
        for dx in range(1, 4):
            total = total + buf[(xh ^ (dx // 2)) * 2 + (xl ^ (dx % 2))]
        buf[me_x] = total

    def cols(ref, x, first, n):
        return ref[first : first + n, pl.ds(side(x), 256)]

    early = (wrap(xl, y == 3), xl, wrap(1 - xl, y == 0), xl)

    def kinds(lo, late):
        x0, x1, x2, x3 = (x ^ late for x in early)
        xr = xl ^ late
        put(lo, tdot(cols(ow, x0, 0, A), cols(ra, xr, 0, A)))
        put(lo + 1, tdot(cols(ra, x1, 0, A), cols(ow, wrap(1 - x1, y == 3), 0, A)))
        put(
            lo + 2,
            tdot(cols(ow, x2, 0, Q), cols(rb, xr, 0, Q))
            + tdot(cols(ow, x2, 3 * Q + H1, H2), cols(rb, xr, 2 * Q, H2)),
        )
        put(
            lo + 3,
            tdot(cols(rb, x3, 0, Q), cols(ow, wrap(x3, y == 0), 0, Q))
            + tdot(cols(rb, x3, 2 * Q, H2), cols(ow, wrap(x3, y == 0), 3 * Q + H1, H2)),
        )
        return pair_sum(lo, 4)

    for p in range(2):
        for d in y1[p]:
            d.wait_recv()
    pair1 = kinds(4, 0)
    weigh(rbw, rb, xl, 2 * Q)
    pair_add(pair0, 0, 4)
    x0 = x_send(0, 2, xin0)

    owners = (y, yp, y, ym)
    last = []
    flows = []
    for g in range(4):
        for way in (1, -1):
            flows.append(
                dict(
                    lo=4 + g * 2,
                    way=way,
                    far=(g % 2 == 0) == (way == -1),
                    near=up if way > 0 else down,
                    second=dev(xl, y, core, (z + 2 * way + 8) % 8, xh),
                )
            )
    early_flows, late_flows = (0, 4), (4, 8)

    def z_step(s, which):
        for f, flow in list(enumerate(flows))[which[0] : which[1]]:
            tiles, way = pl.ds(flow["lo"], 2), flow["way"]

            def rows_for(d, way=way):
                return (z + way * d + 8) % 8

            if s == 0:
                flow["copy"] = rdma(inc.at[tiles, rows_for(3)], zl.at[f, 0], flow["near"])
                if flow["far"]:
                    flow["copy2"] = rdma(inc.at[tiles, rows_for(4)], zl.at[f, 1], flow["second"])
            elif s == 1:
                flow["copy"].wait_recv()
                value = zl[f, 0] + inc[tiles, rows_for(2)]
                if flow["far"]:
                    flow["copy2"].wait_recv()
                    value = value + zl[f, 1]
                zl[f, 0] = value
                flow["copy"] = rdma(zl.at[f, 0], zl.at[f, 2], flow["near"])
            else:
                flow["copy"].wait_recv()
                zl[f, 2] = zl[f, 2] + inc[tiles, rows_for(1)]
                for i in range(2):
                    kind, late = (flow["lo"] + i) % 4, f // 4
                    for ho in (xh, 1 - xh):
                        last.append(
                            rdma(
                                zl.at[f, 2, i, ho],
                                fin1.at[(1 - way) // 2, me_x, kind],
                                dev(early[kind] ^ late, owners[kind], core, rows_for(1), ho),
                            )
                        )

    def own_rows():
        for kind in range(4):
            rz[kind * 2 + early[kind]] = inc[4 + kind, z]
            rz[kind * 2 + (early[kind] ^ 1)] = inc[8 + kind, z]
        for dx in range(4):
            xo, ho = xl ^ (dx % 2), xh ^ (dx // 2)
            for kind, yo in enumerate(owners):
                if dx or kind % 2:
                    last.append(rdma(rz.at[2 * kind + xo, ho], fin3.at[me_x, kind], dev(xo, yo, core, z, ho)))
                else:
                    fin3[me_x, kind] = rz[2 * kind + xo, ho]

    pair_add(pair1, 4, 4)
    z_step(0, early_flows)
    for p in range(2, 4):
        for d in y1[p]:
            d.wait_recv()
    weigh(rbw, rb, 1 - xl, 2 * Q)
    for x in range(2):
        put(12 + x * 2, tdot(cols(rbw, x, 0, 2 * Q), cols(ra, wrap(x, ym >= 2), 0, 2 * Q)))
        put(13 + x * 2, tdot(cols(ra, x, 0, 2 * Q), cols(rbw, wrap(x, yp >= 2), 0, 2 * Q)))
    pair3 = pair_sum(12, 4)
    pair2 = kinds(8, 1)
    pair_add(pair3, 12, 4)
    x2 = x_send(12, 2, xin2)
    pair_add(pair2, 8, 4)
    z_step(0, late_flows)
    z_step(1, early_flows)
    own_rows()
    x_sum(0, 2, xin0, x0)
    for dz in range(1, 8):
        zo = (z + dz) % 8
        last.append(rdma(xin0.at[me_x, :, zo], fin0.at[z], dev(xl, y, core, zo, xh)))
    fin0[z] = xin0[me_x, :, z]
    z_step(1, late_flows)
    z_step(2, early_flows)

    for c in gather:
        c.wait_recv()
    tf[...] = tg[0] + tg[1]

    def split(value):
        hi = value.astype(BF16).astype(F32)
        mid = (value - hi).astype(BF16).astype(F32)
        return hi, mid, value - hi - mid

    wide = lax.broadcasted_iota(jnp.int32, (128, 128), 0)
    pick = lax.broadcasted_iota(jnp.int32, (8, 128), 1) == (
        lax.broadcasted_iota(jnp.int32, (8, 128), 0) + af * 8
    )
    lanes = lax.broadcasted_iota(jnp.int32, (8, 128), 1).astype(F32)
    rows8 = []
    for k in range(9):
        j = (pa + k) % 16
        one, two = cls[0, pl.ds(j, 1), :], cls[1, pl.ds(j, 1), :]
        hot[:, k * 128 : (k + 1) * 128] = ((wide == one) | (wide == two)).astype(F32).astype(BF16)
        i = (pa + 16 - k) % 16
        ends = [
            jnp.sum(jnp.where(pick, cls[e, pl.ds(i, 1), :].astype(F32), 0.0), axis=1, keepdims=True) for e in range(2)
        ]
        rows8.append(((lanes == ends[0]) | (lanes == ends[1])).astype(F32))
    rows8.append(jnp.zeros((8, 128), F32))
    rows80 = jnp.concatenate(rows8, axis=0).astype(BF16)
    t8 = jnp.concatenate([*split(tf[pl.ds(pl.multiple_of(af * 8, 8), 8), :]), jnp.zeros((8, 128), F32)], axis=0)
    t8 = jnp.dot(t8.astype(BF16), hot[...], preferred_element_type=F32)
    own[...] = t8[0:8] + t8[8:16] + t8[16:24]
    others = sum(
        lax.dot_general(rows80, part.astype(BF16), (((1,), (1,)), ((), ())), preferred_element_type=F32)
        for part in split(tf[...])
    )
    for k in range(9):
        nsend[k] = others[k * 8 : (k + 1) * 8]
    oth[0] = nsend[0]

    for k in range(1, 9):
        last.append(rdma(nsend.at[k], oth.at[k], {"pa": (pa + 16 - k) % 16, "af": af}))
    z_step(2, late_flows)
    x_sum(12, 2, xin2, x2)
    for dz in range(8):
        zo = (z + dz) % 8
        last.append(rdma(xin2.at[me_x, 0, zo], fin2.at[z, 0], dev(xl, ym, core, zo, xh)))
        last.append(rdma(xin2.at[me_x, 1, zo], fin2.at[z, 1], dev(xl, yp, core, zo, xh)))
    for c in last:
        c.wait_recv()

    def total(parts):
        return functools.reduce(lambda p, q: p + q, parts)

    cross[:, 0:256] = total([fin0[s, 0] for s in range(8)])
    def kind_sum(kinds_of):
        return total(
            [fin3[s, t] for t in kinds_of for s in range(4)]
            + [fin1[w, s, t] for t in kinds_of for w in range(2) for s in range(4)]
        )

    cross[:, 256:512] = kind_sum((0, 3))
    cross[:, 512:768] = total([fin2[s, t] for t in range(2) for s in range(8)])
    cross[:, 768:1024] = kind_sum((1, 2))
    cross[:, 1024:1280] = total([fin0[s, 1] for s in range(8)])
    shift = pl.multiple_of(core * 128, 128)
    for k in range(9):
        here = slice(k * 128, (k + 1) * 128)
        out_ref[:, here] = cross[:, pl.ds(pl.multiple_of(shift + k * 128, 128), 128)] / jnp.sqrt(
            own[:, here] * oth[k] + eps_norm
        )
    for c in started:
        c.wait_send()


def slopes(degrees):
    return jnp.tan(degrees.astype(F32) * (math.pi / 180.0))


def shards(spectra, tilt_min, tilt_max, tilt_axis):
    vmem = pl.BlockSpec(memory_space=pltpu.VMEM)
    scratch = [
        pltpu.VMEM((3, 16, 128), jnp.int32),
        pltpu.VMEM((2, 2 * KC, 128), BF16),
        pltpu.VMEM((2, 2, KC, 128), BF16),
        pltpu.VMEM((KC, 128), BF16),
        pltpu.VMEM((KC, 512), BF16),
        pltpu.VMEM((KC, 512), BF16),
        pltpu.VMEM((A, 512), BF16),
        pltpu.VMEM((B, 512), BF16),
        pltpu.VMEM((2 * Q, 512), BF16),
        pltpu.VMEM((16, 2, 8, 2, 8, 256), F32),
        pltpu.VMEM((16, 8, 2, 8, 256), F32),
        pltpu.VMEM((4, 2, 8, 8, 256), F32),
        pltpu.VMEM((4, 2, 8, 8, 256), F32),
        pltpu.VMEM((8, 3, 2, 2, 8, 256), F32),
        pltpu.VMEM((8, 2, 8, 256), F32),
        pltpu.VMEM((8, 2, 8, 256), F32),
        pltpu.VMEM((2, 4, 4, 8, 256), F32),
        pltpu.VMEM((8, 2, 8, 256), F32),
        pltpu.VMEM((4, 4, 8, 256), F32),
        pltpu.VMEM((2, KC, 128), BF16),
        pltpu.VMEM((2, KC, 128), BF16),
        pltpu.VMEM((128, 128), F32),
        pltpu.VMEM((2, 4, 16, 128), F32),
        pltpu.VMEM((2, 128, 128), F32),
        pltpu.VMEM((128, 128), F32),
        pltpu.VMEM((2, 16, 128), jnp.int32),
        pltpu.VMEM((128, 1152), BF16),
        pltpu.VMEM((8, 1152), F32),
        pltpu.VMEM((9, 8, 128), F32),
        pltpu.VMEM((9, 8, 128), F32),
        pltpu.VMEM((8, 1280), F32),
        pltpu.SemaphoreType.DMA((9,)),
        pltpu.SemaphoreType.DMA((N_SEM,)),
        pltpu.SemaphoreType.DMA((N_SEM,)),
    ]
    tilts = [t.reshape(16, 128) for t in (tilt_min, tilt_max, tilt_axis)]
    return pl.pallas_call(
        kernel,
        out_shape=jax.ShapeDtypeStruct((8, 1152), F32),
        in_specs=[pl.BlockSpec(memory_space=pl.ANY)] * 4,
        out_specs=vmem,
        scratch_shapes=scratch,
        compiler_params=pltpu.CompilerParams(
            collective_id=0, has_side_effects=True, vmem_limit_bytes=56 * 2**20
        ),
    )(spectra, *tilts)


def solution(mesh):
    in_specs = (P(None, "af", "pa"), P(), P(), P())
    out_specs = P(("pa", "af"), None)
    return jax.shard_map(shards, mesh=mesh, in_specs=in_specs, out_specs=out_specs, check_vma=False)
```

```python
import functools
import math

import jax
import jax.numpy as jnp
from jax import lax
from jax.experimental import pallas as pl
from jax.experimental.pallas import tpu as pltpu
from jax.sharding import PartitionSpec as P

MESH = pl.DeviceIdType.MESH
F32 = jnp.float32
BF16 = jnp.bfloat16

G = 48
HALF = 25
VD = 3600
Q = 464
KC = 4 * Q
H1, H2 = 240, 224
A = 2 * Q + H1
B = 2 * Q + H2
MID = VD - KC
CHUNKS = ((0, 96), (96, 96), (192, 96), (288, 96), (384, 80))
T_LO, T_HI, N_T = 46, 70, 25
eps_norm = 1e-06


def coords():
    pa = lax.axis_index("pa")
    af = lax.axis_index("af")
    return pa // 8, (pa // 2) % 4, pa % 2, af // 2, af % 2


def dev(xl, y, core, z, xh):
    return {"pa": (xl * 4 + y) * 2 + core, "af": z * 2 + xh}


def tdot(lhs, rhs):
    return lax.dot_general(lhs, rhs, (((0,), (0,)), ((), ())), preferred_element_type=F32)


def cells(first, shape):
    v = (first + lax.broadcasted_iota(jnp.int32, shape, 0)).astype(F32)
    q = jnp.floor((v + 0.5) * (1.0 / HALF))
    iz = v - q * HALF
    ix = jnp.floor((q + 0.5) * (1.0 / G))
    iy = q - ix * G
    fx = jnp.where(ix < G // 2, ix, ix - G)
    fy = jnp.where(iy < G // 2, iy, iy - G)
    return fx, fy, iz

N_RECV = 65
N_SEND = 40


def kernel(spec_hbm, tmin_hbm, tmax_hbm, axis_hbm, out_ref, tilt, raw, m, wt, o, ow, ra, rb, rbw, acc, inc, xin0, xin2,
           zl, rz, fin0, fin1, fin2, fin3, pw, cm, tt, tl, tg, tf, cls, hot, own, nsend, oth, cross, load_sem, ssem, rsem, gsend, grecv):
    xl, y, core, z, xh = coords()
    pa = lax.axis_index("pa")
    af = lax.axis_index("af")
    yp, ym = (y + 1) % 4, (y + 3) % 4
    zp, zm = (z + 1) % 8, (z + 7) % 8
    me_x = xh * 2 + xl
    started = []

    def rdma(src, dst, target):
        i = len(started)
        if i >= N_SEND:
            started[i - N_SEND].wait_send()
        c = pltpu.make_async_remote_copy(
            src_ref=src,
            dst_ref=dst,
            send_sem=ssem.at[i % N_SEND],
            recv_sem=rsem.at[i],
            device_id=target,
            device_id_type=MESH,
        )
        c.start()
        started.append(c)
        return c

    def in_group(g, src, dst, target):
        return pltpu.make_async_remote_copy(
            src_ref=src, dst_ref=dst, send_sem=gsend.at[g], recv_sem=grecv.at[g], device_id=target, device_id_type=MESH
        )

    def group_wait(g, size):
        c = in_group(g, size, size, dev(xl, y, 1 - core, z, xh))
        c.wait_recv()
        c.wait_send()

    loads = []
    for i, ref in enumerate((tmin_hbm, tmax_hbm, axis_hbm)):
        c = pltpu.make_async_copy(ref, tilt.at[i], load_sem.at[i])
        c.start()
        loads.append(c)
    tmin_ref, tmax_ref, axis_ref = tilt.at[0], tilt.at[1], tilt.at[2]
    for first, n in ((core * KC, MID), (MID, KC - MID), ((1 - core) * KC, MID)):
        here = pl.ds(first if isinstance(first, int) else pl.multiple_of(first, 16), n)
        for p in range(2):
            c = pltpu.make_async_copy(spec_hbm.at[p, here], raw.at[p, here], load_sem.at[len(loads)])
            c.start()
            loads.append(c)
    barrier = pltpu.get_barrier_semaphore()
    peers = [
        dev(xl, y, 1 - core, z, xh),
        dev(1 - xl, y, core, z, xh),
        dev(1 - xl, y, 1 - core, z, xh),
        dev(xl, yp, core, z, xh),
        dev(xl, ym, core, z, xh),
        dev(xl, y, core, z, 1 - xh),
        dev(xl, y, core, zp, xh),
        dev(xl, y, core, zm, xh),
    ]
    for peer in peers:
        pl.semaphore_signal(barrier, inc=1, device_id=peer, device_id_type=MESH)
    raw[:, VD:, :] = jnp.zeros((2, 2 * KC - VD, 128), BF16)

    for c in loads[:3]:
        c.wait()
    cls[0] = axis_ref[...] * 50 + (-T_LO - tmin_ref[...])
    cls[1] = axis_ref[...] * 50 + (N_T - T_LO + tmax_ref[...])
    lower = slopes(tmin_ref[pl.ds(pa, 1), :])
    upper = slopes(tmax_ref[pl.ds(pa, 1), :])
    axis = axis_ref[pl.ds(pa, 1), :]
    lane = lax.broadcasted_iota(jnp.int32, (1, 128), 1)
    c_axis = (lane >= 50).astype(jnp.int32)
    c_side = ((lane - c_axis * 50) >= 25).astype(jnp.int32)
    c_slope = slopes(lane - c_axis * 50 - c_side * 25 + T_LO)
    c_slope = jnp.where(lane < 100, c_slope, -1.0)

    def own_col(dx, dc):
        return pl.multiple_of(((xl ^ dx) * 2 + (core ^ dc)) * 128, 128)

    def by_chunk(half, body, slots=(0, 4)):
        def slot(s, carry):
            first = half * KC + (y + 3 - s) % 4 * Q
            for r0, n in CHUNKS:
                body(pl.multiple_of(first + r0, 16), pl.ds(pl.multiple_of(s * Q + r0, 16), n), n)
            return carry

        lax.fori_loop(*slots, slot, 0)

    def mask_half(half, slots=(0, 4)):
        def body(r0, to, n):
            fx, fy, iz = cells(af * VD + r0, (n, 128))
            u = jnp.where(axis == 1, fx, fy)
            a = jnp.abs(u)
            b = jnp.where(u >= 0.0, -iz, iz)
            keep = ((a * lower <= b) & (b <= a * upper)).astype(F32)
            for p in range(2):
                m[p, half, to, :] = (raw[p, pl.ds(r0, n), :].astype(F32) * keep).astype(BF16)

        by_chunk(half, body, slots)

    for c in loads[3:7]:
        c.wait()
    mask_half(core, (2, 4))
    pl.semaphore_wait(barrier, len(peers))

    col = own_col(0, 0)

    y1 = [[] for _ in range(4)]

    def to_minus(p, r0, n):
        c = pl.ds(own_col(p // 2, p % 2), 128)
        y1[p].append(rdma(o.at[pl.ds(r0, n), c], ra.at[pl.ds(r0 - Q, n), c], dev(xl, ym, core, z, xh)))

    def to_plus(p, r0, n, to):
        c = pl.ds(own_col(p // 2, p % 2), 128)
        y1[p].append(rdma(o.at[pl.ds(r0, n), c], rb.at[pl.ds(to, n), c], dev(xl, yp, core, z, xh)))

    def y_high(p):
        to_plus(p, 3 * Q, Q, 0)
        to_minus(p, 2 * Q, Q + H1)
        to_plus(p, 2 * Q + H1, H2, 2 * Q)

    def y_low(p):
        to_plus(p, 0, Q, Q)
        to_minus(p, Q, Q)

    def to_x(half, r0, n, target):
        return rdma(m.at[1 - xl, half, pl.ds(r0, n)], o.at[pl.ds(r0, n), pl.ds(col, 128)], target)

    own_high, own_low = pl.ds(2 * Q, 2 * Q), pl.ds(0, 2 * Q)
    x_same = [to_x(core, 2 * Q, 2 * Q, dev(1 - xl, y, core, z, xh))]
    o[own_high, pl.ds(col, 128)] = m[xl, core, own_high]
    y_high(0)
    mask_half(core, (0, 2))
    x_same.append(to_x(core, 0, 2 * Q, dev(1 - xl, y, core, z, xh)))
    o[own_low, pl.ds(col, 128)] = m[xl, core, own_low]
    y_low(0)
    for c in loads[7:]:
        c.wait()
    mask_half(1 - core)
    sib = rdma(m.at[xl, 1 - core], o.at[:, pl.ds(col, 128)], dev(xl, y, 1 - core, z, xh))
    x_other = [to_x(1 - core, q * Q, Q, dev(1 - xl, y, 1 - core, z, xh)) for q in (3, 2, 0, 1)]

    for half in range(2):

        def powers(r0, to, n, half=half):
            fx, fy, iz = cells(af * VD + r0, (n, 128))
            re = m[0, half, to, :].astype(F32)
            im = m[1, half, to, :].astype(F32)
            w = jnp.where((iz < 0.5) | (iz > 23.5), 1.0, 2.0)
            pw[half, to, :] = (w * (re * re + im * im)).astype(BF16)
            u = jnp.where(c_axis == 1, fx, fy)
            side = (u < 0.0).astype(jnp.int32)
            keep = (iz <= jnp.abs(u) * c_slope) & (side == c_side) & (lane < 100)
            cm[half, to, :] = keep.astype(F32).astype(BF16)

        by_chunk(half, powers)
        if half == 0:
            sib.wait_recv()
            y_high(1)
            y_low(1)
    tt[...] = tdot(pw[0], cm[0]) + tdot(pw[1], cm[1])

    def rows16(zz):
        return pl.ds(pl.multiple_of(((zz + 16) % 8) * 16, 16), 16)

    up, down = dev(xl, y, core, zp, xh), dev(xl, y, core, zm, xh)
    t_flows = [dict(way=1, steps=3, target=up), dict(way=-1, steps=4, target=down)]

    def t_step(s):
        for f, flow in enumerate(t_flows):
            if s > flow["steps"]:
                continue
            if s:
                flow["copy"].wait_recv()
            if s == flow["steps"]:
                continue
            here = rows16(z + flow["way"] * (flow["steps"] - s))
            if s == 0:
                src = tt.at[here]
            else:
                src = tl.at[f, s - 1]
                src[...] = src[...] + tt[here, :]
            flow["copy"] = rdma(src, tl.at[f, s], flow["target"])

    t_step(0)

    def weights(r0, to, n):
        iz = cells(af * VD + r0, (n, 128))[2]
        wt[to, :] = jnp.where((iz < 0.5) | (iz > 23.5), 1.0, 2.0).astype(BF16)

    by_chunk(core, weights)

    def weigh(dst, src, x, n):
        for dc in range(2):
            here = pl.ds(pl.multiple_of(x * 256 + dc * 128, 128), 128)
            dst[:, here] = src[0:n, here] * wt[0:n, :]

    x_same[0].wait_recv()
    y_high(2)
    t_step(1)
    weigh(ow, o, xl, KC)
    x_same[1].wait_recv()
    y_low(2)
    t_step(2)
    x_other[0].wait_recv()
    to_plus(3, 3 * Q, Q, 0)
    to_minus(3, 3 * Q, H1)
    t_step(3)
    x_other[1].wait_recv()
    to_plus(3, 2 * Q + H1, H2, 2 * Q)
    to_minus(3, 2 * Q, Q)
    t_step(4)
    mine16 = rows16(z)
    mine_g = pl.ds(pl.multiple_of(xh * 128 + z * 16, 16), 16)
    tg[mine_g, :] = tt[mine16, :] + tl[0, 2] + tl[1, 3]
    for dz in range(8):
        for dh in range(2):
            if dz or dh:
                part = tg.at[mine_g]
                in_group(0, part, part, dev(xl, y, core, (z + dz) % 8, xh ^ dh)).start()

    x_other[2].wait_recv()
    to_plus(3, 0, Q, Q)
    x_other[3].wait_recv()
    to_minus(3, Q, Q)
    weigh(ow, o, 1 - xl, KC)

    def put(tile, value):
        acc[tile] = value.reshape(2, 8, 2, 8, 256)

    def side(x):
        return pl.multiple_of(x * 256, 256)

    def wrap(x, cond):
        return x ^ cond.astype(jnp.int32)

    def pair_sum(lo, n):
        tiles = pl.ds(lo, n)
        return rdma(acc.at[tiles, 1 - core], inc.at[tiles], dev(xl, y, 1 - core, z, xh))

    def pair_add(copy, lo, n):
        copy.wait_recv()
        for t in range(lo, lo + n):
            inc[t] = inc[t] + acc[t, core]

    for x in range(2):
        for slot, xo in ((0, x), (1, 1 - x)):
            put(x * 2 + slot, tdot(ow[:, x * 256 : x * 256 + 256], o[:, xo * 256 : xo * 256 + 256]))
    pair0 = pair_sum(0, 4)

    def x_send(lo, n, buf):
        copies = []
        for dx in range(1, 4):
            xo, ho = xl ^ (dx % 2), xh ^ (dx // 2)
            copies.append(
                rdma(inc.at[pl.ds(lo + xo * n, n), :, ho], buf.at[me_x], dev(xo, y, core, z, ho))
            )
        return copies

    def x_sum(lo, n, buf, copies):
        for c in copies:
            c.wait_recv()
        total = inc[pl.ds(lo + xl * n, n), :, xh]
        for dx in range(1, 4):
            total = total + buf[(xh ^ (dx // 2)) * 2 + (xl ^ (dx % 2))]
        buf[me_x] = total

    def cols(ref, x, first, n):
        return ref[first : first + n, pl.ds(side(x), 256)]

    early = (wrap(xl, y == 3), xl, wrap(1 - xl, y == 0), xl)

    def kinds(lo, late):
        x0, x1, x2, x3 = (x ^ late for x in early)
        xr = xl ^ late
        put(lo, tdot(cols(ow, x0, 0, A), cols(ra, xr, 0, A)))
        put(lo + 1, tdot(cols(ra, x1, 0, A), cols(ow, wrap(1 - x1, y == 3), 0, A)))
        put(
            lo + 2,
            tdot(cols(ow, x2, 0, Q), cols(rb, xr, 0, Q))
            + tdot(cols(ow, x2, 3 * Q + H1, H2), cols(rb, xr, 2 * Q, H2)),
        )
        put(
            lo + 3,
            tdot(cols(rb, x3, 0, Q), cols(ow, wrap(x3, y == 0), 0, Q))
            + tdot(cols(rb, x3, 2 * Q, H2), cols(ow, wrap(x3, y == 0), 3 * Q + H1, H2)),
        )
        return pair_sum(lo, 4)

    for p in range(2):
        for d in y1[p]:
            d.wait_recv()
    pair1 = kinds(4, 0)
    weigh(rbw, rb, xl, 2 * Q)
    pair_add(pair0, 0, 4)
    x0 = x_send(0, 2, xin0)

    owners = (y, yp, y, ym)
    flows = []
    for g in range(4):
        for way in (1, -1):
            flows.append(
                dict(
                    lo=4 + g * 2,
                    way=way,
                    far=(g % 2 == 0) == (way == -1),
                    near=up if way > 0 else down,
                    second=dev(xl, y, core, (z + 2 * way + 8) % 8, xh),
                )
            )
    early_flows, late_flows = (0, 4), (4, 8)

    def z_step(s, which):
        for f, flow in list(enumerate(flows))[which[0] : which[1]]:
            tiles, way = pl.ds(flow["lo"], 2), flow["way"]

            def rows_for(d, way=way):
                return (z + way * d + 8) % 8

            if s == 0:
                flow["copy"] = rdma(inc.at[tiles, rows_for(3)], zl.at[f, 0], flow["near"])
                if flow["far"]:
                    flow["copy2"] = rdma(inc.at[tiles, rows_for(4)], zl.at[f, 1], flow["second"])
            elif s == 1:
                flow["copy"].wait_recv()
                value = zl[f, 0] + inc[tiles, rows_for(2)]
                if flow["far"]:
                    flow["copy2"].wait_recv()
                    value = value + zl[f, 1]
                zl[f, 0] = value
                flow["copy"] = rdma(zl.at[f, 0], zl.at[f, 2], flow["near"])
            else:
                flow["copy"].wait_recv()
                zl[f, 2] = zl[f, 2] + inc[tiles, rows_for(1)]
                for i in range(2):
                    kind, late = (flow["lo"] + i) % 4, f // 4
                    for ho in (xh, 1 - xh):
                        in_group(
                            1,
                            zl.at[f, 2, i, ho],
                            fin1.at[(1 - way) // 2, me_x, kind],
                            dev(early[kind] ^ late, owners[kind], core, rows_for(1), ho),
                        ).start()

    def own_rows():
        for kind in range(4):
            rz[kind * 2 + early[kind]] = inc[4 + kind, z]
            rz[kind * 2 + (early[kind] ^ 1)] = inc[8 + kind, z]
        for dx in range(4):
            xo, ho = xl ^ (dx % 2), xh ^ (dx // 2)
            for kind, yo in enumerate(owners):
                if dx or kind % 2:
                    in_group(2, rz.at[2 * kind + xo, ho], fin3.at[me_x * 4 + kind], dev(xo, yo, core, z, ho)).start()
                else:
                    fin3[me_x * 4 + kind] = rz[2 * kind + xo, ho]

    pair_add(pair1, 4, 4)
    z_step(0, early_flows)
    for p in range(2, 4):
        for d in y1[p]:
            d.wait_recv()
    weigh(rbw, rb, 1 - xl, 2 * Q)
    for x in range(2):
        put(12 + x * 2, tdot(cols(rbw, x, 0, 2 * Q), cols(ra, wrap(x, ym >= 2), 0, 2 * Q)))
        put(13 + x * 2, tdot(cols(ra, x, 0, 2 * Q), cols(rbw, wrap(x, yp >= 2), 0, 2 * Q)))
    pair3 = pair_sum(12, 4)
    pair2 = kinds(8, 1)
    pair_add(pair3, 12, 4)
    x2 = x_send(12, 2, xin2)
    pair_add(pair2, 8, 4)
    z_step(0, late_flows)
    z_step(1, early_flows)
    own_rows()
    x_sum(0, 2, xin0, x0)
    for dz in range(1, 8):
        zo = (z + dz) % 8
        in_group(3, xin0.at[me_x, :, zo], fin0.at[z], dev(xl, y, core, zo, xh)).start()
    fin0[z] = xin0[me_x, :, z]
    z_step(1, late_flows)
    z_step(2, early_flows)

    group_wait(0, tg.at[0:240])
    tf[...] = tg[0:128] + tg[128:256]

    def split(value):
        hi = value.astype(BF16).astype(F32)
        mid = (value - hi).astype(BF16).astype(F32)
        return hi, mid, value - hi - mid

    wide = lax.broadcasted_iota(jnp.int32, (128, 128), 0)
    pick = lax.broadcasted_iota(jnp.int32, (8, 128), 1) == (
        lax.broadcasted_iota(jnp.int32, (8, 128), 0) + af * 8
    )
    lanes = lax.broadcasted_iota(jnp.int32, (8, 128), 1).astype(F32)
    rows8 = []
    for k in range(9):
        j = (pa + k) % 16
        one, two = cls[0, pl.ds(j, 1), :], cls[1, pl.ds(j, 1), :]
        hot[:, k * 128 : (k + 1) * 128] = ((wide == one) | (wide == two)).astype(F32).astype(BF16)
        i = (pa + 16 - k) % 16
        ends = [
            jnp.sum(jnp.where(pick, cls[e, pl.ds(i, 1), :].astype(F32), 0.0), axis=1, keepdims=True) for e in range(2)
        ]
        rows8.append(((lanes == ends[0]) | (lanes == ends[1])).astype(F32))
    rows8.append(jnp.zeros((8, 128), F32))
    rows80 = jnp.concatenate(rows8, axis=0).astype(BF16)
    t8 = jnp.concatenate([*split(tf[pl.ds(pl.multiple_of(af * 8, 8), 8), :]), jnp.zeros((8, 128), F32)], axis=0)
    t8 = jnp.dot(t8.astype(BF16), hot[...], preferred_element_type=F32)
    own[...] = t8[0:8] + t8[8:16] + t8[16:24]
    others = sum(
        lax.dot_general(rows80, part.astype(BF16), (((1,), (1,)), ((), ())), preferred_element_type=F32)
        for part in split(tf[...])
    )
    for k in range(9):
        nsend[k] = others[k * 8 : (k + 1) * 8]
    oth[0] = nsend[0]

    for k in range(1, 9):
        in_group(4, nsend.at[k], oth.at[k], {"pa": (pa + 16 - k) % 16, "af": af}).start()
    z_step(2, late_flows)
    x_sum(12, 2, xin2, x2)
    for dz in range(8):
        zo = (z + dz) % 8
        in_group(5, xin2.at[me_x, 0, zo], fin2.at[z, 0], dev(xl, ym, core, zo, xh)).start()
        in_group(5, xin2.at[me_x, 1, zo], fin2.at[z, 1], dev(xl, yp, core, zo, xh)).start()
    for c in started[-N_SEND:]:
        c.wait_send()
    group_wait(3, fin0.at[0:7])
    group_wait(4, oth.at[0:8])
    group_wait(2, fin3.at[0:14])
    group_wait(1, fin1)
    group_wait(5, fin2)

    def total(parts):
        return functools.reduce(lambda p, q: p + q, parts)

    cross[:, 0:256] = total([fin0[s, 0] for s in range(8)])
    def kind_sum(kinds_of):
        return total(
            [fin3[s * 4 + t] for t in kinds_of for s in range(4)]
            + [fin1[w, s, t] for t in kinds_of for w in range(2) for s in range(4)]
        )

    cross[:, 256:512] = kind_sum((0, 3))
    cross[:, 512:768] = total([fin2[s, t] for t in range(2) for s in range(8)])
    cross[:, 768:1024] = kind_sum((1, 2))
    cross[:, 1024:1280] = total([fin0[s, 1] for s in range(8)])
    shift = pl.multiple_of(core * 128, 128)
    for k in range(9):
        here = slice(k * 128, (k + 1) * 128)
        out_ref[:, here] = cross[:, pl.ds(pl.multiple_of(shift + k * 128, 128), 128)] / jnp.sqrt(
            own[:, here] * oth[k] + eps_norm
        )


def slopes(degrees):
    return jnp.tan(degrees.astype(F32) * (math.pi / 180.0))


def shards(spectra, tilt_min, tilt_max, tilt_axis):
    vmem = pl.BlockSpec(memory_space=pltpu.VMEM)
    scratch = [
        pltpu.VMEM((3, 16, 128), jnp.int32),
        pltpu.VMEM((2, 2 * KC, 128), BF16),
        pltpu.VMEM((2, 2, KC, 128), BF16),
        pltpu.VMEM((KC, 128), BF16),
        pltpu.VMEM((KC, 512), BF16),
        pltpu.VMEM((KC, 512), BF16),
        pltpu.VMEM((A, 512), BF16),
        pltpu.VMEM((B, 512), BF16),
        pltpu.VMEM((2 * Q, 512), BF16),
        pltpu.VMEM((16, 2, 8, 2, 8, 256), F32),
        pltpu.VMEM((16, 8, 2, 8, 256), F32),
        pltpu.VMEM((4, 2, 8, 8, 256), F32),
        pltpu.VMEM((4, 2, 8, 8, 256), F32),
        pltpu.VMEM((8, 3, 2, 2, 8, 256), F32),
        pltpu.VMEM((8, 2, 8, 256), F32),
        pltpu.VMEM((8, 2, 8, 256), F32),
        pltpu.VMEM((2, 4, 4, 8, 256), F32),
        pltpu.VMEM((8, 2, 8, 256), F32),
        pltpu.VMEM((16, 8, 256), F32),
        pltpu.VMEM((2, KC, 128), BF16),
        pltpu.VMEM((2, KC, 128), BF16),
        pltpu.VMEM((128, 128), F32),
        pltpu.VMEM((2, 4, 16, 128), F32),
        pltpu.VMEM((256, 128), F32),
        pltpu.VMEM((128, 128), F32),
        pltpu.VMEM((2, 16, 128), jnp.int32),
        pltpu.VMEM((128, 1152), BF16),
        pltpu.VMEM((8, 1152), F32),
        pltpu.VMEM((9, 8, 128), F32),
        pltpu.VMEM((9, 8, 128), F32),
        pltpu.VMEM((8, 1280), F32),
        pltpu.SemaphoreType.DMA((9,)),
        pltpu.SemaphoreType.DMA((N_SEND,)),
        pltpu.SemaphoreType.DMA((N_RECV,)),
        pltpu.SemaphoreType.DMA((6,)),
        pltpu.SemaphoreType.DMA((6,)),
    ]
    tilts = [t.reshape(16, 128) for t in (tilt_min, tilt_max, tilt_axis)]
    return pl.pallas_call(
        kernel,
        out_shape=jax.ShapeDtypeStruct((8, 1152), F32),
        in_specs=[pl.BlockSpec(memory_space=pl.ANY)] * 4,
        out_specs=vmem,
        scratch_shapes=scratch,
        compiler_params=pltpu.CompilerParams(
            collective_id=0, has_side_effects=True, vmem_limit_bytes=56 * 2**20
        ),
    )(spectra, *tilts)


def solution(mesh):
    in_specs = (P(None, "af", "pa"), P(), P(), P())
    out_specs = P(("pa", "af"), None)
    return jax.shard_map(shards, mesh=mesh, in_specs=in_specs, out_specs=out_specs, check_vma=False)
```

```python
import functools
import math

import jax
import jax.numpy as jnp
from jax import lax
from jax.experimental import pallas as pl
from jax.experimental.pallas import tpu as pltpu
from jax.sharding import PartitionSpec as P

MESH = pl.DeviceIdType.MESH
F32 = jnp.float32
BF16 = jnp.bfloat16

G = 48
HALF = 25
VD = 3600
Q = 464
KC = 4 * Q
H1, H2 = 240, 224
A = 2 * Q + H1
B = 2 * Q + H2
MID = VD - KC
CHUNKS = ((0, 96), (96, 96), (192, 96), (288, 96), (384, 80))
T_LO, T_HI, N_T = 46, 70, 25
eps_norm = 1e-06


def coords():
    pa = lax.axis_index("pa")
    af = lax.axis_index("af")
    return pa // 8, (pa // 2) % 4, pa % 2, af // 2, af % 2


def dev(xl, y, core, z, xh):
    return {"pa": (xl * 4 + y) * 2 + core, "af": z * 2 + xh}


def tdot(lhs, rhs):
    return lax.dot_general(lhs, rhs, (((0,), (0,)), ((), ())), preferred_element_type=F32)


def cells(first, shape):
    v = (first + lax.broadcasted_iota(jnp.int32, shape, 0)).astype(F32)
    q = jnp.floor((v + 0.5) * (1.0 / HALF))
    iz = v - q * HALF
    ix = jnp.floor((q + 0.5) * (1.0 / G))
    iy = q - ix * G
    fx = jnp.where(ix < G // 2, ix, ix - G)
    fy = jnp.where(iy < G // 2, iy, iy - G)
    return fx, fy, iz

N_RECV = 70
N_SEND = 32


def kernel(spec_hbm, tmin_hbm, tmax_hbm, axis_hbm, out_ref, tilt, raw, m, wt, o, ow, ra, rb, rbw, acc, inc, xin0, xin2,
           zl, rz, fin0, fin1, fin2, fin3, pw, cm, tt, tl, tg, tf, cls, hot, own, nsend, oth, cross, load_sem, ssem, rsem, gsend, grecv):
    xl, y, core, z, xh = coords()
    pa = lax.axis_index("pa")
    af = lax.axis_index("af")
    yp, ym = (y + 1) % 4, (y + 3) % 4
    zp, zm = (z + 1) % 8, (z + 7) % 8
    me_x = xh * 2 + xl
    started = []

    def rdma(src, dst, target):
        i = len(started)
        if i >= N_SEND:
            started[i - N_SEND].wait_send()
        c = pltpu.make_async_remote_copy(
            src_ref=src,
            dst_ref=dst,
            send_sem=ssem.at[i % N_SEND],
            recv_sem=rsem.at[i],
            device_id=target,
            device_id_type=MESH,
        )
        c.start()
        started.append(c)
        return c

    def in_group(g, src, dst, target):
        return pltpu.make_async_remote_copy(
            src_ref=src, dst_ref=dst, send_sem=gsend.at[g], recv_sem=grecv.at[g], device_id=target, device_id_type=MESH
        )

    def group_wait(g, size):
        c = in_group(g, size, size, dev(xl, y, 1 - core, z, xh))
        c.wait_recv()
        c.wait_send()

    loads = []
    for i, ref in enumerate((tmin_hbm, tmax_hbm, axis_hbm)):
        c = pltpu.make_async_copy(ref, tilt.at[i], load_sem.at[i])
        c.start()
        loads.append(c)
    tmin_ref, tmax_ref, axis_ref = tilt.at[0], tilt.at[1], tilt.at[2]
    for first, n in ((core * KC, MID), (MID, KC - MID), ((1 - core) * KC, MID)):
        here = pl.ds(first if isinstance(first, int) else pl.multiple_of(first, 16), n)
        for p in range(2):
            c = pltpu.make_async_copy(spec_hbm.at[p, here], raw.at[p, here], load_sem.at[len(loads)])
            c.start()
            loads.append(c)
    barrier = pltpu.get_barrier_semaphore()
    peers = [
        dev(xl, y, 1 - core, z, xh),
        dev(1 - xl, y, core, z, xh),
        dev(1 - xl, y, 1 - core, z, xh),
        dev(xl, yp, core, z, xh),
        dev(xl, ym, core, z, xh),
        dev(xl, y, core, z, 1 - xh),
        dev(xl, y, core, zp, xh),
        dev(xl, y, core, zm, xh),
    ]
    for peer in peers:
        pl.semaphore_signal(barrier, inc=1, device_id=peer, device_id_type=MESH)
    raw[:, VD:, :] = jnp.zeros((2, 2 * KC - VD, 128), BF16)

    for c in loads[:3]:
        c.wait()
    cls[0] = axis_ref[...] * 50 + (-T_LO - tmin_ref[...])
    cls[1] = axis_ref[...] * 50 + (N_T - T_LO + tmax_ref[...])
    lower = slopes(tmin_ref[pl.ds(pa, 1), :])
    upper = slopes(tmax_ref[pl.ds(pa, 1), :])
    axis = axis_ref[pl.ds(pa, 1), :]
    lane = lax.broadcasted_iota(jnp.int32, (1, 128), 1)
    c_axis = (lane >= 50).astype(jnp.int32)
    c_side = ((lane - c_axis * 50) >= 25).astype(jnp.int32)
    c_slope = slopes(lane - c_axis * 50 - c_side * 25 + T_LO)
    c_slope = jnp.where(lane < 100, c_slope, -1.0)

    def own_col(dx, dc):
        return pl.multiple_of(((xl ^ dx) * 2 + (core ^ dc)) * 128, 128)

    def by_chunk(half, body, slots=(0, 4)):
        def slot(s, carry):
            first = half * KC + (y + 3 - s) % 4 * Q
            for r0, n in CHUNKS:
                body(pl.multiple_of(first + r0, 16), pl.ds(pl.multiple_of(s * Q + r0, 16), n), n)
            return carry

        lax.fori_loop(*slots, slot, 0)

    def mask_half(half, slots=(0, 4)):
        def body(r0, to, n):
            fx, fy, iz = cells(af * VD + r0, (n, 128))
            u = jnp.where(axis == 1, fx, fy)
            a = jnp.abs(u)
            b = jnp.where(u >= 0.0, -iz, iz)
            keep = ((a * lower <= b) & (b <= a * upper)).astype(F32)
            for p in range(2):
                m[p, half, to, :] = (raw[p, pl.ds(r0, n), :].astype(F32) * keep).astype(BF16)

        by_chunk(half, body, slots)

    for c in loads[3:7]:
        c.wait()
    mask_half(core, (2, 4))
    pl.semaphore_wait(barrier, len(peers))

    col = own_col(0, 0)

    y1 = [[] for _ in range(4)]

    def to_minus(p, r0, n):
        c = pl.ds(own_col(p // 2, p % 2), 128)
        y1[p].append(rdma(o.at[pl.ds(r0, n), c], ra.at[pl.ds(r0 - Q, n), c], dev(xl, ym, core, z, xh)))

    def to_plus(p, r0, n, to):
        c = pl.ds(own_col(p // 2, p % 2), 128)
        y1[p].append(rdma(o.at[pl.ds(r0, n), c], rb.at[pl.ds(to, n), c], dev(xl, yp, core, z, xh)))

    def y_high(p):
        to_plus(p, 3 * Q, Q, 0)
        to_minus(p, 2 * Q, Q + H1)
        to_plus(p, 2 * Q + H1, H2, 2 * Q)

    def y_low(p):
        to_plus(p, 0, Q, Q)
        to_minus(p, Q, Q)

    def to_x(half, r0, n, target):
        return rdma(m.at[1 - xl, half, pl.ds(r0, n)], o.at[pl.ds(r0, n), pl.ds(col, 128)], target)

    own_high, own_low = pl.ds(2 * Q, 2 * Q), pl.ds(0, 2 * Q)
    x_same = [to_x(core, 2 * Q, 2 * Q, dev(1 - xl, y, core, z, xh))]
    o[own_high, pl.ds(col, 128)] = m[xl, core, own_high]
    y_high(0)
    mask_half(core, (0, 2))
    x_same.append(to_x(core, 0, 2 * Q, dev(1 - xl, y, core, z, xh)))
    o[own_low, pl.ds(col, 128)] = m[xl, core, own_low]
    y_low(0)
    for c in loads[7:]:
        c.wait()
    mask_half(1 - core)
    sib = rdma(m.at[xl, 1 - core], o.at[:, pl.ds(col, 128)], dev(xl, y, 1 - core, z, xh))
    x_other = [to_x(1 - core, q * Q, Q, dev(1 - xl, y, 1 - core, z, xh)) for q in (3, 2, 0, 1)]

    for half in range(2):

        def powers(r0, to, n, half=half):
            fx, fy, iz = cells(af * VD + r0, (n, 128))
            re = m[0, half, to, :].astype(F32)
            im = m[1, half, to, :].astype(F32)
            w = jnp.where((iz < 0.5) | (iz > 23.5), 1.0, 2.0)
            pw[half, to, :] = (w * (re * re + im * im)).astype(BF16)
            u = jnp.where(c_axis == 1, fx, fy)
            side = (u < 0.0).astype(jnp.int32)
            keep = (iz <= jnp.abs(u) * c_slope) & (side == c_side) & (lane < 100)
            cm[half, to, :] = keep.astype(F32).astype(BF16)

        by_chunk(half, powers)
        if half == 0:
            sib.wait_recv()
            y_high(1)
            y_low(1)
    tt[...] = tdot(pw[0], cm[0]) + tdot(pw[1], cm[1])

    def rows16(zz):
        return pl.ds(pl.multiple_of(((zz + 16) % 8) * 16, 16), 16)

    up, down = dev(xl, y, core, zp, xh), dev(xl, y, core, zm, xh)
    t_flows = [dict(way=1, steps=3, target=up), dict(way=-1, steps=4, target=down)]

    def t_step(s):
        for f, flow in enumerate(t_flows):
            if s > flow["steps"]:
                continue
            if s:
                flow["copy"].wait_recv()
            if s == flow["steps"]:
                continue
            here = rows16(z + flow["way"] * (flow["steps"] - s))
            if s == 0:
                src = tt.at[here]
            else:
                src = tl.at[f, s - 1]
                src[...] = src[...] + tt[here, :]
            flow["copy"] = rdma(src, tl.at[f, s], flow["target"])

    t_step(0)

    def weights(r0, to, n):
        iz = cells(af * VD + r0, (n, 128))[2]
        wt[to, :] = jnp.where((iz < 0.5) | (iz > 23.5), 1.0, 2.0).astype(BF16)

    by_chunk(core, weights)

    def weigh(dst, src, x, first, n):
        rows = slice(first, first + n)
        for dc in range(2):
            here = pl.ds(pl.multiple_of(x * 256 + dc * 128, 128), 128)
            dst[rows, here] = src[rows, here] * wt[rows, :]

    x_same[0].wait_recv()
    y_high(2)
    t_step(1)
    weigh(ow, o, xl, 0, KC)
    x_same[1].wait_recv()
    y_low(2)
    t_step(2)
    x_other[0].wait_recv()
    to_plus(3, 3 * Q, Q, 0)
    to_minus(3, 3 * Q, H1)
    t_step(3)
    x_other[1].wait_recv()
    to_plus(3, 2 * Q + H1, H2, 2 * Q)
    to_minus(3, 2 * Q, Q)
    t_step(4)
    mine16 = rows16(z)
    mine_g = pl.ds(pl.multiple_of(xh * 128 + z * 16, 16), 16)
    tg[mine_g, :] = tt[mine16, :] + tl[0, 2] + tl[1, 3]
    for dz in range(8):
        for dh in range(2):
            if dz or dh:
                part = tg.at[mine_g]
                in_group(0, part, part, dev(xl, y, core, (z + dz) % 8, xh ^ dh)).start()

    def put(tile, value):
        acc[tile] = value.reshape(2, 8, 2, 8, 256)

    def side(x):
        return pl.multiple_of(x * 256, 256)

    def wrap(x, cond):
        return x ^ cond.astype(jnp.int32)

    def pair_sum(lo, n):
        tiles = pl.ds(lo, n)
        return rdma(acc.at[tiles, 1 - core], inc.at[tiles], dev(xl, y, 1 - core, z, xh))

    def pair_add(copy, lo, n):
        copy.wait_recv()
        for t in range(lo, lo + n):
            inc[t] = inc[t] + acc[t, core]

    def cols(ref, x, first, n):
        return ref[first : first + n, pl.ds(side(x), 256)]

    def add(tile, value):
        acc[tile] = acc[tile] + value.reshape(2, 8, 2, 8, 256)

    def own_tiles(first, n, store):
        for x in range(2):
            for slot, xo in ((0, x), (1, 1 - x)):
                store(x * 2 + slot, tdot(cols(ow, x, first, n), cols(o, xo, first, n)))

    weigh(ow, o, 1 - xl, 2 * Q, 2 * Q)
    own_tiles(2 * Q, 2 * Q, put)
    x_other[2].wait_recv()
    to_plus(3, 0, Q, Q)
    weigh(ow, o, 1 - xl, 0, Q)
    own_tiles(0, Q, add)
    x_other[3].wait_recv()
    to_minus(3, Q, Q)
    weigh(ow, o, 1 - xl, Q, Q)
    own_tiles(Q, Q, add)
    pair0 = pair_sum(0, 4)

    def x_send(lo, n, buf):
        copies = []
        for dx in range(1, 4):
            xo, ho = xl ^ (dx % 2), xh ^ (dx // 2)
            copies.append(
                rdma(inc.at[pl.ds(lo + xo * n, n), :, ho], buf.at[me_x], dev(xo, y, core, z, ho))
            )
        return copies

    def x_sum(lo, n, buf, copies):
        for c in copies:
            c.wait_recv()
        total = inc[pl.ds(lo + xl * n, n), :, xh]
        for dx in range(1, 4):
            total = total + buf[(xh ^ (dx // 2)) * 2 + (xl ^ (dx % 2))]
        buf[me_x] = total

    early = (wrap(xl, y == 3), xl, wrap(1 - xl, y == 0), xl)

    def plus_kinds(lo, late, first, n, store):
        x0, x1 = early[0] ^ late, early[1] ^ late
        store(lo, tdot(cols(ow, x0, first, n), cols(ra, xl ^ late, first, n)))
        store(lo + 1, tdot(cols(ra, x1, first, n), cols(ow, wrap(1 - x1, y == 3), first, n)))

    def minus_kinds(lo, late):
        x2, x3 = early[2] ^ late, early[3] ^ late
        xr = xl ^ late
        put(
            lo + 2,
            tdot(cols(ow, x2, 0, Q), cols(rb, xr, 0, Q))
            + tdot(cols(ow, x2, 3 * Q + H1, H2), cols(rb, xr, 2 * Q, H2)),
        )
        put(
            lo + 3,
            tdot(cols(rb, x3, 0, Q), cols(ow, wrap(x3, y == 0), 0, Q))
            + tdot(cols(rb, x3, 2 * Q, H2), cols(ow, wrap(x3, y == 0), 3 * Q + H1, H2)),
        )

    def second_minus(first, n, store):
        for x in range(2):
            store(12 + x, tdot(cols(rbw, x, first, n), cols(ra, wrap(x, ym >= 2), first, n)))

    def second_plus(first, n, store):
        for x in range(2):
            store(14 + x, tdot(cols(ra, x, first, n), cols(rbw, wrap(x, yp >= 2), first, n)))

    for p in range(2):
        for d in y1[p]:
            d.wait_recv()
    plus_kinds(4, 0, 0, A, put)
    minus_kinds(4, 0)
    pair1 = pair_sum(4, 4)
    weigh(rbw, rb, xl, 0, 2 * Q)
    pair_add(pair0, 0, 4)
    x0 = x_send(0, 2, xin0)

    owners = (y, yp, y, ym)
    flows = []
    for g in range(4):
        for way in (1, -1):
            flows.append(
                dict(
                    lo=4 + g * 2,
                    way=way,
                    far=(g % 2 == 0) == (way == -1),
                    near=up if way > 0 else down,
                    second=dev(xl, y, core, (z + 2 * way + 8) % 8, xh),
                )
            )
    early_flows, late_flows = (0, 4), (4, 8)

    def z_step(s, which):
        for f, flow in list(enumerate(flows))[which[0] : which[1]]:
            tiles, way = pl.ds(flow["lo"], 2), flow["way"]

            def rows_for(d, way=way):
                return (z + way * d + 8) % 8

            if s == 0:
                flow["copy"] = rdma(inc.at[tiles, rows_for(3)], zl.at[f, 0], flow["near"])
                if flow["far"]:
                    flow["copy2"] = rdma(inc.at[tiles, rows_for(4)], zl.at[f, 1], flow["second"])
            elif s == 1:
                flow["copy"].wait_recv()
                value = zl[f, 0] + inc[tiles, rows_for(2)]
                if flow["far"]:
                    flow["copy2"].wait_recv()
                    value = value + zl[f, 1]
                zl[f, 0] = value
                flow["copy"] = rdma(zl.at[f, 0], zl.at[f, 2], flow["near"])
            else:
                flow["copy"].wait_recv()
                zl[f, 2] = zl[f, 2] + inc[tiles, rows_for(1)]
                for i in range(2):
                    kind, late = (flow["lo"] + i) % 4, f // 4
                    for ho in (xh, 1 - xh):
                        in_group(
                            1,
                            zl.at[f, 2, i, ho],
                            fin1.at[(1 - way) // 2, me_x, kind],
                            dev(early[kind] ^ late, owners[kind], core, rows_for(1), ho),
                        ).start()

    def own_rows():
        for kind in range(4):
            rz[kind * 2 + early[kind]] = inc[4 + kind, z]
            rz[kind * 2 + (early[kind] ^ 1)] = inc[8 + kind, z]
        for dx in range(4):
            xo, ho = xl ^ (dx % 2), xh ^ (dx // 2)
            for kind, yo in enumerate(owners):
                if dx or kind % 2:
                    in_group(2, rz.at[2 * kind + xo, ho], fin3.at[me_x * 4 + kind], dev(xo, yo, core, z, ho)).start()
                else:
                    fin3[me_x * 4 + kind] = rz[2 * kind + xo, ho]

    pair_add(pair1, 4, 4)
    z_step(0, early_flows)
    for d in y1[2] + y1[3][:-1]:
        d.wait_recv()
    minus_kinds(8, 1)
    pair_b = pair_sum(10, 2)
    weigh(rbw, rb, 1 - xl, 0, 2 * Q)
    second_minus(Q, Q, put)
    second_plus(Q, Q, put)
    plus_kinds(8, 1, Q, Q + H1, put)
    pair_add(pair_b, 10, 2)
    z_step(0, (6, 8))
    y1[3][-1].wait_recv()
    second_minus(0, Q, add)
    pair_c = pair_sum(12, 2)
    second_plus(0, Q, add)
    pair_d = pair_sum(14, 2)
    plus_kinds(8, 1, 0, Q, add)
    pair_a = pair_sum(8, 2)
    pair_add(pair_c, 12, 2)
    x2 = x_send(12, 1, xin2.at[0])
    pair_add(pair_d, 14, 2)
    x3 = x_send(14, 1, xin2.at[1])
    pair_add(pair_a, 8, 2)
    z_step(0, (4, 6))
    z_step(1, early_flows)
    group_wait(0, tg.at[0:240])
    tf[...] = tg[0:128] + tg[128:256]

    def split(value):
        hi = value.astype(BF16).astype(F32)
        mid = (value - hi).astype(BF16).astype(F32)
        return hi, mid, value - hi - mid

    wide = lax.broadcasted_iota(jnp.int32, (128, 128), 0)
    pick = lax.broadcasted_iota(jnp.int32, (8, 128), 1) == (
        lax.broadcasted_iota(jnp.int32, (8, 128), 0) + af * 8
    )
    lanes = lax.broadcasted_iota(jnp.int32, (8, 128), 1).astype(F32)
    rows8 = []
    for k in range(9):
        j = (pa + k) % 16
        one, two = cls[0, pl.ds(j, 1), :], cls[1, pl.ds(j, 1), :]
        hot[:, k * 128 : (k + 1) * 128] = ((wide == one) | (wide == two)).astype(F32).astype(BF16)
        i = (pa + 16 - k) % 16
        ends = [
            jnp.sum(jnp.where(pick, cls[e, pl.ds(i, 1), :].astype(F32), 0.0), axis=1, keepdims=True) for e in range(2)
        ]
        rows8.append(((lanes == ends[0]) | (lanes == ends[1])).astype(F32))
    rows8.append(jnp.zeros((8, 128), F32))
    rows80 = jnp.concatenate(rows8, axis=0).astype(BF16)
    t8 = jnp.concatenate([*split(tf[pl.ds(pl.multiple_of(af * 8, 8), 8), :]), jnp.zeros((8, 128), F32)], axis=0)
    t8 = jnp.dot(t8.astype(BF16), hot[...], preferred_element_type=F32)
    own[...] = t8[0:8] + t8[8:16] + t8[16:24]
    others = sum(
        lax.dot_general(rows80, part.astype(BF16), (((1,), (1,)), ((), ())), preferred_element_type=F32)
        for part in split(tf[...])
    )
    for k in range(9):
        nsend[k] = others[k * 8 : (k + 1) * 8]
    oth[0] = nsend[0]

    for k in range(1, 9):
        in_group(4, nsend.at[k], oth.at[k], {"pa": (pa + 16 - k) % 16, "af": af}).start()
    z_step(1, (6, 8))
    x_sum(0, 2, xin0, x0)
    for dz in range(1, 8):
        zo = (z + dz) % 8
        in_group(3, xin0.at[me_x, :, zo], fin0.at[z], dev(xl, y, core, zo, xh)).start()
    fin0[z] = xin0[me_x, :, z]
    z_step(1, (4, 6))
    z_step(2, early_flows)
    z_step(2, (6, 8))
    own_rows()

    z_step(2, (4, 6))
    for i, (copies, yo) in enumerate(((x2, ym), (x3, yp))):
        x_sum(12 + 2 * i, 1, xin2.at[i], copies)
        for dz in (4, 3, 5, 2, 6, 1, 7, 0):
            zo = (z + dz) % 8
            in_group(5, xin2.at[i, me_x, 0, zo], fin2.at[z, i], dev(xl, yo, core, zo, xh)).start()
    for c in started[-N_SEND:]:
        c.wait_send()
    group_wait(3, fin0.at[0:7])
    group_wait(4, oth.at[0:8])
    group_wait(2, fin3.at[0:14])
    group_wait(1, fin1)
    group_wait(5, fin2)

    def total(parts):
        return functools.reduce(lambda p, q: p + q, parts)

    cross[:, 0:256] = total([fin0[s, 0] for s in range(8)])
    def kind_sum(kinds_of):
        return total(
            [fin3[s * 4 + t] for t in kinds_of for s in range(4)]
            + [fin1[w, s, t] for t in kinds_of for w in range(2) for s in range(4)]
        )

    cross[:, 256:512] = kind_sum((0, 3))
    cross[:, 512:768] = total([fin2[s, t] for t in range(2) for s in range(8)])
    cross[:, 768:1024] = kind_sum((1, 2))
    cross[:, 1024:1280] = total([fin0[s, 1] for s in range(8)])
    shift = pl.multiple_of(core * 128, 128)
    for k in range(9):
        here = slice(k * 128, (k + 1) * 128)
        out_ref[:, here] = cross[:, pl.ds(pl.multiple_of(shift + k * 128, 128), 128)] / jnp.sqrt(
            own[:, here] * oth[k] + eps_norm
        )


def slopes(degrees):
    return jnp.tan(degrees.astype(F32) * (math.pi / 180.0))


def shards(spectra, tilt_min, tilt_max, tilt_axis):
    vmem = pl.BlockSpec(memory_space=pltpu.VMEM)
    scratch = [
        pltpu.VMEM((3, 16, 128), jnp.int32),
        pltpu.VMEM((2, 2 * KC, 128), BF16),
        pltpu.VMEM((2, 2, KC, 128), BF16),
        pltpu.VMEM((KC, 128), BF16),
        pltpu.VMEM((KC, 512), BF16),
        pltpu.VMEM((KC, 512), BF16),
        pltpu.VMEM((A, 512), BF16),
        pltpu.VMEM((B, 512), BF16),
        pltpu.VMEM((2 * Q, 512), BF16),
        pltpu.VMEM((16, 2, 8, 2, 8, 256), F32),
        pltpu.VMEM((16, 8, 2, 8, 256), F32),
        pltpu.VMEM((4, 2, 8, 8, 256), F32),
        pltpu.VMEM((2, 4, 1, 8, 8, 256), F32),
        pltpu.VMEM((8, 3, 2, 2, 8, 256), F32),
        pltpu.VMEM((8, 2, 8, 256), F32),
        pltpu.VMEM((8, 2, 8, 256), F32),
        pltpu.VMEM((2, 4, 4, 8, 256), F32),
        pltpu.VMEM((8, 2, 8, 256), F32),
        pltpu.VMEM((16, 8, 256), F32),
        pltpu.VMEM((2, KC, 128), BF16),
        pltpu.VMEM((2, KC, 128), BF16),
        pltpu.VMEM((128, 128), F32),
        pltpu.VMEM((2, 4, 16, 128), F32),
        pltpu.VMEM((256, 128), F32),
        pltpu.VMEM((128, 128), F32),
        pltpu.VMEM((2, 16, 128), jnp.int32),
        pltpu.VMEM((128, 1152), BF16),
        pltpu.VMEM((8, 1152), F32),
        pltpu.VMEM((9, 8, 128), F32),
        pltpu.VMEM((9, 8, 128), F32),
        pltpu.VMEM((8, 1280), F32),
        pltpu.SemaphoreType.DMA((9,)),
        pltpu.SemaphoreType.DMA((N_SEND,)),
        pltpu.SemaphoreType.DMA((N_RECV,)),
        pltpu.SemaphoreType.DMA((6,)),
        pltpu.SemaphoreType.DMA((6,)),
    ]
    tilts = [t.reshape(16, 128) for t in (tilt_min, tilt_max, tilt_axis)]
    return pl.pallas_call(
        kernel,
        out_shape=jax.ShapeDtypeStruct((8, 1152), F32),
        in_specs=[pl.BlockSpec(memory_space=pl.ANY)] * 4,
        out_specs=vmem,
        scratch_shapes=scratch,
        compiler_params=pltpu.CompilerParams(
            collective_id=0, has_side_effects=True, vmem_limit_bytes=56 * 2**20
        ),
    )(spectra, *tilts)


def solution(mesh):
    in_specs = (P(None, "af", "pa"), P(), P(), P())
    out_specs = P(("pa", "af"), None)
    return jax.shard_map(shards, mesh=mesh, in_specs=in_specs, out_specs=out_specs, check_vma=False)
```

```python
import functools
import math

import jax
import jax.numpy as jnp
from jax import lax
from jax.experimental import pallas as pl
from jax.experimental.pallas import tpu as pltpu
from jax.sharding import PartitionSpec as P

MESH = pl.DeviceIdType.MESH
F32 = jnp.float32
BF16 = jnp.bfloat16

G = 48
HALF = 25
VD = 3600
Q = 464
KC = 4 * Q
H1, H2 = 240, 224
A = 2 * Q + H1
B = 2 * Q + H2
MID = VD - KC
CHUNKS = ((0, 96), (96, 96), (192, 96), (288, 96), (384, 80))
T_LO, T_HI, N_T = 46, 70, 25
eps_norm = 1e-06


def coords():
    pa = lax.axis_index("pa")
    af = lax.axis_index("af")
    return pa // 8, (pa // 2) % 4, pa % 2, af // 2, af % 2


def dev(xl, y, core, z, xh):
    return {"pa": (xl * 4 + y) * 2 + core, "af": z * 2 + xh}


def tdot(lhs, rhs):
    return lax.dot_general(lhs, rhs, (((0,), (0,)), ((), ())), preferred_element_type=F32)


def cells(first, shape):
    v = (first + lax.broadcasted_iota(jnp.int32, shape, 0)).astype(F32)
    q = jnp.floor((v + 0.5) * (1.0 / HALF))
    iz = v - q * HALF
    ix = jnp.floor((q + 0.5) * (1.0 / G))
    iy = q - ix * G
    fx = jnp.where(ix < G // 2, ix, ix - G)
    fy = jnp.where(iy < G // 2, iy, iy - G)
    return fx, fy, iz

N_RECV = 72
N_SEND = 32


def kernel(spec_hbm, tmin_hbm, tmax_hbm, axis_hbm, out_ref, tilt, raw, m, wt, o, ow, ra, rb, rbw, acc, inc, xin0, xin2,
           zl, rz, fin0, fin1, fin2, fin3, pw, cm, tt, tl, tg, tf, cls, hot, own, nsend, oth, cross, load_sem, ssem, rsem, gsend, grecv):
    xl, y, core, z, xh = coords()
    pa = lax.axis_index("pa")
    af = lax.axis_index("af")
    yp, ym = (y + 1) % 4, (y + 3) % 4
    zp, zm = (z + 1) % 8, (z + 7) % 8
    me_x = xh * 2 + xl
    started = []

    def rdma(src, dst, target):
        i = len(started)
        if i >= N_SEND:
            started[i - N_SEND].wait_send()
        c = pltpu.make_async_remote_copy(
            src_ref=src,
            dst_ref=dst,
            send_sem=ssem.at[i % N_SEND],
            recv_sem=rsem.at[i],
            device_id=target,
            device_id_type=MESH,
        )
        c.start()
        started.append(c)
        return c

    def in_group(g, src, dst, target):
        return pltpu.make_async_remote_copy(
            src_ref=src, dst_ref=dst, send_sem=gsend.at[g], recv_sem=grecv.at[g], device_id=target, device_id_type=MESH
        )

    def group_wait(g, size):
        c = in_group(g, size, size, dev(xl, y, 1 - core, z, xh))
        c.wait_recv()
        c.wait_send()

    barrier = pltpu.get_barrier_semaphore()
    peers = [
        dev(xl, y, 1 - core, z, xh),
        dev(1 - xl, y, core, z, xh),
        dev(1 - xl, y, 1 - core, z, xh),
        dev(xl, yp, core, z, xh),
        dev(xl, ym, core, z, xh),
        dev(xl, y, core, z, 1 - xh),
        dev(xl, y, core, zp, xh),
        dev(xl, y, core, zm, xh),
    ]
    for peer in peers:
        pl.semaphore_signal(barrier, inc=1, device_id=peer, device_id_type=MESH)
    loads = []
    for i, ref in enumerate((tmin_hbm, tmax_hbm, axis_hbm)):
        c = pltpu.make_async_copy(ref, tilt.at[i], load_sem.at[i])
        c.start()
        loads.append(c)
    tmin_ref, tmax_ref, axis_ref = tilt.at[0], tilt.at[1], tilt.at[2]
    for first, n in ((core * KC, MID), (MID, KC - MID), ((1 - core) * KC, MID)):
        here = pl.ds(first if isinstance(first, int) else pl.multiple_of(first, 16), n)
        for p in range(2):
            c = pltpu.make_async_copy(spec_hbm.at[p, here], raw.at[p, here], load_sem.at[len(loads)])
            c.start()
            loads.append(c)
    raw[:, VD:, :] = jnp.zeros((2, 2 * KC - VD, 128), BF16)

    for c in loads[:3]:
        c.wait()
    cls[0] = axis_ref[...] * 50 + (-T_LO - tmin_ref[...])
    cls[1] = axis_ref[...] * 50 + (N_T - T_LO + tmax_ref[...])
    lower = slopes(tmin_ref[pl.ds(pa, 1), :])
    upper = slopes(tmax_ref[pl.ds(pa, 1), :])
    axis = axis_ref[pl.ds(pa, 1), :]
    lane = lax.broadcasted_iota(jnp.int32, (1, 128), 1)
    c_axis = (lane >= 50).astype(jnp.int32)
    c_side = ((lane - c_axis * 50) >= 25).astype(jnp.int32)
    c_slope = slopes(lane - c_axis * 50 - c_side * 25 + T_LO)
    c_slope = jnp.where(lane < 100, c_slope, -1.0)

    def own_col(dx, dc):
        return pl.multiple_of(((xl ^ dx) * 2 + (core ^ dc)) * 128, 128)

    def by_chunk(half, body, slots=(0, 4)):
        def slot(s, carry):
            first = half * KC + (y + 3 - s) % 4 * Q
            for r0, n in CHUNKS:
                body(pl.multiple_of(first + r0, 16), pl.ds(pl.multiple_of(s * Q + r0, 16), n), n)
            return carry

        lax.fori_loop(*slots, slot, 0)

    def mask_half(half, slots=(0, 4)):
        def body(r0, to, n):
            fx, fy, iz = cells(af * VD + r0, (n, 128))
            u = jnp.where(axis == 1, fx, fy)
            a = jnp.abs(u)
            b = jnp.where(u >= 0.0, -iz, iz)
            keep = ((a * lower <= b) & (b <= a * upper)).astype(F32)
            for p in range(2):
                m[p, half, to, :] = (raw[p, pl.ds(r0, n), :].astype(F32) * keep).astype(BF16)

        by_chunk(half, body, slots)

    for c in loads[3:7]:
        c.wait()
    mask_half(core, (3, 4))
    pl.semaphore_wait(barrier, len(peers))

    col = own_col(0, 0)

    y1 = [[] for _ in range(4)]

    def to_minus(p, r0, n):
        c = pl.ds(own_col(p // 2, p % 2), 128)
        y1[p].append(rdma(o.at[pl.ds(r0, n), c], ra.at[pl.ds(r0 - Q, n), c], dev(xl, ym, core, z, xh)))

    def to_plus(p, r0, n, to):
        c = pl.ds(own_col(p // 2, p % 2), 128)
        y1[p].append(rdma(o.at[pl.ds(r0, n), c], rb.at[pl.ds(to, n), c], dev(xl, yp, core, z, xh)))

    def y_high(p):
        to_plus(p, 3 * Q, Q, 0)
        to_minus(p, 2 * Q, Q + H1)
        to_plus(p, 2 * Q + H1, H2, 2 * Q)

    def y_low(p):
        to_plus(p, 0, Q, Q)
        to_minus(p, Q, Q)

    def to_x(half, r0, n, target):
        return rdma(m.at[1 - xl, half, pl.ds(r0, n)], o.at[pl.ds(r0, n), pl.ds(col, 128)], target)

    x_same = []

    def first(slots, r0, n):
        if slots:
            mask_half(core, slots)
        here = pl.ds(r0, n)
        x_same.append(to_x(core, r0, n, dev(1 - xl, y, core, z, xh)))
        o[here, pl.ds(col, 128)] = m[xl, core, here]

    first(None, 3 * Q, Q)
    to_plus(0, 3 * Q, Q, 0)
    to_minus(0, 3 * Q, H1)
    first((2, 3), 2 * Q, Q)
    to_minus(0, 2 * Q, Q)
    to_plus(0, 2 * Q + H1, H2, 2 * Q)
    first((0, 2), 0, 2 * Q)
    y_low(0)
    for c in loads[7:]:
        c.wait()
    mask_half(1 - core)
    sib = rdma(m.at[xl, 1 - core], o.at[:, pl.ds(col, 128)], dev(xl, y, 1 - core, z, xh))
    x_other = [to_x(1 - core, q * Q, Q, dev(1 - xl, y, 1 - core, z, xh)) for q in (3, 2, 0, 1)]

    for half in range(2):

        def powers(r0, to, n, half=half):
            fx, fy, iz = cells(af * VD + r0, (n, 128))
            re = m[0, half, to, :].astype(F32)
            im = m[1, half, to, :].astype(F32)
            w = jnp.where((iz < 0.5) | (iz > 23.5), 1.0, 2.0)
            pw[half, to, :] = (w * (re * re + im * im)).astype(BF16)
            u = jnp.where(c_axis == 1, fx, fy)
            side = (u < 0.0).astype(jnp.int32)
            keep = (iz <= jnp.abs(u) * c_slope) & (side == c_side) & (lane < 100)
            cm[half, to, :] = keep.astype(F32).astype(BF16)

        by_chunk(half, powers)
        if half == 0:
            sib.wait_recv()
            y_high(1)
            y_low(1)
    tt[...] = tdot(pw[0], cm[0]) + tdot(pw[1], cm[1])

    def rows16(zz):
        return pl.ds(pl.multiple_of(((zz + 16) % 8) * 16, 16), 16)

    up, down = dev(xl, y, core, zp, xh), dev(xl, y, core, zm, xh)
    t_flows = [dict(way=1, steps=3, target=up), dict(way=-1, steps=4, target=down)]

    def t_step(s):
        for f, flow in enumerate(t_flows):
            if s > flow["steps"]:
                continue
            if s:
                flow["copy"].wait_recv()
            if s == flow["steps"]:
                continue
            here = rows16(z + flow["way"] * (flow["steps"] - s))
            if s == 0:
                src = tt.at[here]
            else:
                src = tl.at[f, s - 1]
                src[...] = src[...] + tt[here, :]
            flow["copy"] = rdma(src, tl.at[f, s], flow["target"])

    t_step(0)

    def weights(r0, to, n):
        iz = cells(af * VD + r0, (n, 128))[2]
        wt[to, :] = jnp.where((iz < 0.5) | (iz > 23.5), 1.0, 2.0).astype(BF16)

    by_chunk(core, weights)

    def weigh(dst, src, x, first, n):
        rows = slice(first, first + n)
        for dc in range(2):
            here = pl.ds(pl.multiple_of(x * 256 + dc * 128, 128), 128)
            dst[rows, here] = src[rows, here] * wt[rows, :]

    x_same[0].wait_recv()
    x_same[1].wait_recv()
    y_high(2)
    t_step(1)
    weigh(ow, o, xl, 0, KC)
    x_same[2].wait_recv()
    y_low(2)
    t_step(2)
    x_other[0].wait_recv()
    to_plus(3, 3 * Q, Q, 0)
    to_minus(3, 3 * Q, H1)
    t_step(3)
    x_other[1].wait_recv()
    to_plus(3, 2 * Q + H1, H2, 2 * Q)
    to_minus(3, 2 * Q, Q)
    t_step(4)
    mine16 = rows16(z)
    mine_g = pl.ds(pl.multiple_of(xh * 128 + z * 16, 16), 16)
    tg[mine_g, :] = tt[mine16, :] + tl[0, 2] + tl[1, 3]
    for dz in range(8):
        for dh in range(2):
            if dz or dh:
                part = tg.at[mine_g]
                in_group(0, part, part, dev(xl, y, core, (z + dz) % 8, xh ^ dh)).start()

    def put(tile, value):
        acc[tile] = value.reshape(2, 8, 2, 8, 256)

    def side(x):
        return pl.multiple_of(x * 256, 256)

    def wrap(x, cond):
        return x ^ cond.astype(jnp.int32)

    def pair_sum(lo, n):
        tiles = pl.ds(lo, n)
        return rdma(acc.at[tiles, 1 - core], inc.at[tiles], dev(xl, y, 1 - core, z, xh))

    def pair_add(copy, lo, n):
        copy.wait_recv()
        for t in range(lo, lo + n):
            inc[t] = inc[t] + acc[t, core]

    def cols(ref, x, first, n):
        return ref[first : first + n, pl.ds(side(x), 256)]

    def add(tile, value):
        acc[tile] = acc[tile] + value.reshape(2, 8, 2, 8, 256)

    def own_tiles(first, n, store):
        for x in range(2):
            for slot, xo in ((0, x), (1, 1 - x)):
                store(x * 2 + slot, tdot(cols(ow, x, first, n), cols(o, xo, first, n)))

    weigh(ow, o, 1 - xl, 2 * Q, 2 * Q)
    own_tiles(2 * Q, 2 * Q, put)
    x_other[2].wait_recv()
    to_plus(3, 0, Q, Q)
    weigh(ow, o, 1 - xl, 0, Q)
    own_tiles(0, Q, add)
    x_other[3].wait_recv()
    to_minus(3, Q, Q)
    weigh(ow, o, 1 - xl, Q, Q)
    own_tiles(Q, Q, add)
    pair0 = pair_sum(0, 4)

    def x_send(lo, n, buf):
        copies = []
        for dx in range(1, 4):
            xo, ho = xl ^ (dx % 2), xh ^ (dx // 2)
            copies.append(
                rdma(inc.at[pl.ds(lo + xo * n, n), :, ho], buf.at[me_x], dev(xo, y, core, z, ho))
            )
        return copies

    def x_sum(lo, n, buf, copies):
        for c in copies:
            c.wait_recv()
        total = inc[pl.ds(lo + xl * n, n), :, xh]
        for dx in range(1, 4):
            total = total + buf[(xh ^ (dx // 2)) * 2 + (xl ^ (dx % 2))]
        buf[me_x] = total

    early = (wrap(xl, y == 3), xl, wrap(1 - xl, y == 0), xl)

    def plus_kinds(lo, late, first, n, store):
        x0, x1 = early[0] ^ late, early[1] ^ late
        store(lo, tdot(cols(ow, x0, first, n), cols(ra, xl ^ late, first, n)))
        store(lo + 1, tdot(cols(ra, x1, first, n), cols(ow, wrap(1 - x1, y == 3), first, n)))

    def minus_kinds(lo, late):
        x2, x3 = early[2] ^ late, early[3] ^ late
        xr = xl ^ late
        put(
            lo + 2,
            tdot(cols(ow, x2, 0, Q), cols(rb, xr, 0, Q))
            + tdot(cols(ow, x2, 3 * Q + H1, H2), cols(rb, xr, 2 * Q, H2)),
        )
        put(
            lo + 3,
            tdot(cols(rb, x3, 0, Q), cols(ow, wrap(x3, y == 0), 0, Q))
            + tdot(cols(rb, x3, 2 * Q, H2), cols(ow, wrap(x3, y == 0), 3 * Q + H1, H2)),
        )

    def second_minus(first, n, store):
        for x in range(2):
            store(12 + x, tdot(cols(rbw, x, first, n), cols(ra, wrap(x, ym >= 2), first, n)))

    def second_plus(first, n, store):
        for x in range(2):
            store(14 + x, tdot(cols(ra, x, first, n), cols(rbw, wrap(x, yp >= 2), first, n)))

    for p in range(2):
        for d in y1[p]:
            d.wait_recv()
    plus_kinds(4, 0, 0, A, put)
    minus_kinds(4, 0)
    pair1 = pair_sum(4, 4)
    weigh(rbw, rb, xl, 0, 2 * Q)
    pair_add(pair0, 0, 4)
    x0 = x_send(0, 2, xin0)

    owners = (y, yp, y, ym)
    flows = []
    for g in range(4):
        for way in (1, -1):
            flows.append(
                dict(
                    lo=4 + g * 2,
                    way=way,
                    far=(g % 2 == 0) == (way == -1),
                    near=up if way > 0 else down,
                    second=dev(xl, y, core, (z + 2 * way + 8) % 8, xh),
                )
            )
    early_flows, late_flows = (0, 4), (4, 8)

    def z_step(s, which):
        for f, flow in list(enumerate(flows))[which[0] : which[1]]:
            tiles, way = pl.ds(flow["lo"], 2), flow["way"]

            def rows_for(d, way=way):
                return (z + way * d + 8) % 8

            if s == 0:
                flow["copy"] = rdma(inc.at[tiles, rows_for(3)], zl.at[f, 0], flow["near"])
                if flow["far"]:
                    flow["copy2"] = rdma(inc.at[tiles, rows_for(4)], zl.at[f, 1], flow["second"])
            elif s == 1:
                flow["copy"].wait_recv()
                value = zl[f, 0] + inc[tiles, rows_for(2)]
                if flow["far"]:
                    flow["copy2"].wait_recv()
                    value = value + zl[f, 1]
                zl[f, 0] = value
                flow["copy"] = rdma(zl.at[f, 0], zl.at[f, 2], flow["near"])
            else:
                flow["copy"].wait_recv()
                zl[f, 2] = zl[f, 2] + inc[tiles, rows_for(1)]
                for i in range(2):
                    kind, late = (flow["lo"] + i) % 4, f // 4
                    for ho in (xh, 1 - xh):
                        in_group(
                            1,
                            zl.at[f, 2, i, ho],
                            fin1.at[(1 - way) // 2, me_x, kind],
                            dev(early[kind] ^ late, owners[kind], core, rows_for(1), ho),
                        ).start()

    def own_rows():
        for kind in range(4):
            rz[kind * 2 + early[kind]] = inc[4 + kind, z]
            rz[kind * 2 + (early[kind] ^ 1)] = inc[8 + kind, z]
        for dx in range(4):
            xo, ho = xl ^ (dx % 2), xh ^ (dx // 2)
            for kind, yo in enumerate(owners):
                if dx or kind % 2:
                    in_group(2, rz.at[2 * kind + xo, ho], fin3.at[me_x * 4 + kind], dev(xo, yo, core, z, ho)).start()
                else:
                    fin3[me_x * 4 + kind] = rz[2 * kind + xo, ho]

    pair_add(pair1, 4, 4)
    z_step(0, early_flows)
    for d in y1[2] + y1[3][:-1]:
        d.wait_recv()
    minus_kinds(8, 1)
    pair_b = pair_sum(10, 2)
    weigh(rbw, rb, 1 - xl, 0, 2 * Q)
    second_minus(Q, Q, put)
    second_plus(Q, Q, put)
    plus_kinds(8, 1, Q, Q + H1, put)
    pair_add(pair_b, 10, 2)
    z_step(0, (6, 8))
    y1[3][-1].wait_recv()
    second_minus(0, Q, add)
    pair_c = pair_sum(12, 2)
    second_plus(0, Q, add)
    pair_d = pair_sum(14, 2)
    plus_kinds(8, 1, 0, Q, add)
    pair_a = pair_sum(8, 2)
    pair_add(pair_c, 12, 2)
    x2 = x_send(12, 1, xin2.at[0])
    pair_add(pair_d, 14, 2)
    x3 = x_send(14, 1, xin2.at[1])
    pair_add(pair_a, 8, 2)
    z_step(0, (4, 6))
    z_step(1, early_flows)
    group_wait(0, tg.at[0:240])
    tf[...] = tg[0:128] + tg[128:256]

    def split(value):
        hi = value.astype(BF16).astype(F32)
        mid = (value - hi).astype(BF16).astype(F32)
        return hi, mid, value - hi - mid

    wide = lax.broadcasted_iota(jnp.int32, (128, 128), 0)
    pick = lax.broadcasted_iota(jnp.int32, (8, 128), 1) == (
        lax.broadcasted_iota(jnp.int32, (8, 128), 0) + af * 8
    )
    lanes = lax.broadcasted_iota(jnp.int32, (8, 128), 1).astype(F32)
    rows8 = []
    for k in range(9):
        j = (pa + k) % 16
        one, two = cls[0, pl.ds(j, 1), :], cls[1, pl.ds(j, 1), :]
        hot[:, k * 128 : (k + 1) * 128] = ((wide == one) | (wide == two)).astype(F32).astype(BF16)
        i = (pa + 16 - k) % 16
        ends = [
            jnp.sum(jnp.where(pick, cls[e, pl.ds(i, 1), :].astype(F32), 0.0), axis=1, keepdims=True) for e in range(2)
        ]
        rows8.append(((lanes == ends[0]) | (lanes == ends[1])).astype(F32))
    rows8.append(jnp.zeros((8, 128), F32))
    rows80 = jnp.concatenate(rows8, axis=0).astype(BF16)
    t8 = jnp.concatenate([*split(tf[pl.ds(pl.multiple_of(af * 8, 8), 8), :]), jnp.zeros((8, 128), F32)], axis=0)
    t8 = jnp.dot(t8.astype(BF16), hot[...], preferred_element_type=F32)
    own[...] = t8[0:8] + t8[8:16] + t8[16:24]
    others = sum(
        lax.dot_general(rows80, part.astype(BF16), (((1,), (1,)), ((), ())), preferred_element_type=F32)
        for part in split(tf[...])
    )
    for k in range(9):
        nsend[k] = others[k * 8 : (k + 1) * 8]
    oth[0] = nsend[0]

    for k in range(1, 9):
        in_group(4, nsend.at[k], oth.at[k], {"pa": (pa + 16 - k) % 16, "af": af}).start()
    z_step(1, (6, 8))
    x_sum(0, 2, xin0, x0)
    for dz in range(1, 8):
        zo = (z + dz) % 8
        in_group(3, xin0.at[me_x, :, zo], fin0.at[z], dev(xl, y, core, zo, xh)).start()
    fin0[z] = xin0[me_x, :, z]
    z_step(1, (4, 6))
    z_step(2, early_flows)
    z_step(2, (6, 8))
    own_rows()

    z_step(2, (4, 6))
    for i, (copies, yo) in enumerate(((x2, ym), (x3, yp))):
        x_sum(12 + 2 * i, 1, xin2.at[i], copies)
        for dz in (4, 3, 5, 2, 6, 1, 7, 0):
            zo = (z + dz) % 8
            in_group(5, xin2.at[i, me_x, 0, zo], fin2.at[z, i], dev(xl, yo, core, zo, xh)).start()
    for c in started[-N_SEND:]:
        c.wait_send()
    group_wait(3, fin0.at[0:7])
    group_wait(4, oth.at[0:8])
    group_wait(2, fin3.at[0:14])
    group_wait(1, fin1)
    group_wait(5, fin2)

    def total(parts):
        return functools.reduce(lambda p, q: p + q, parts)

    cross[:, 0:256] = total([fin0[s, 0] for s in range(8)])
    def kind_sum(kinds_of):
        return total(
            [fin3[s * 4 + t] for t in kinds_of for s in range(4)]
            + [fin1[w, s, t] for t in kinds_of for w in range(2) for s in range(4)]
        )

    cross[:, 256:512] = kind_sum((0, 3))
    cross[:, 512:768] = total([fin2[s, t] for t in range(2) for s in range(8)])
    cross[:, 768:1024] = kind_sum((1, 2))
    cross[:, 1024:1280] = total([fin0[s, 1] for s in range(8)])
    shift = pl.multiple_of(core * 128, 128)
    for k in range(9):
        here = slice(k * 128, (k + 1) * 128)
        out_ref[:, here] = cross[:, pl.ds(pl.multiple_of(shift + k * 128, 128), 128)] / jnp.sqrt(
            own[:, here] * oth[k] + eps_norm
        )


def slopes(degrees):
    return jnp.tan(degrees.astype(F32) * (math.pi / 180.0))


def shards(spectra, tilt_min, tilt_max, tilt_axis):
    vmem = pl.BlockSpec(memory_space=pltpu.VMEM)
    scratch = [
        pltpu.VMEM((3, 16, 128), jnp.int32),
        pltpu.VMEM((2, 2 * KC, 128), BF16),
        pltpu.VMEM((2, 2, KC, 128), BF16),
        pltpu.VMEM((KC, 128), BF16),
        pltpu.VMEM((KC, 512), BF16),
        pltpu.VMEM((KC, 512), BF16),
        pltpu.VMEM((A, 512), BF16),
        pltpu.VMEM((B, 512), BF16),
        pltpu.VMEM((2 * Q, 512), BF16),
        pltpu.VMEM((16, 2, 8, 2, 8, 256), F32),
        pltpu.VMEM((16, 8, 2, 8, 256), F32),
        pltpu.VMEM((4, 2, 8, 8, 256), F32),
        pltpu.VMEM((2, 4, 1, 8, 8, 256), F32),
        pltpu.VMEM((8, 3, 2, 2, 8, 256), F32),
        pltpu.VMEM((8, 2, 8, 256), F32),
        pltpu.VMEM((8, 2, 8, 256), F32),
        pltpu.VMEM((2, 4, 4, 8, 256), F32),
        pltpu.VMEM((8, 2, 8, 256), F32),
        pltpu.VMEM((16, 8, 256), F32),
        pltpu.VMEM((2, KC, 128), BF16),
        pltpu.VMEM((2, KC, 128), BF16),
        pltpu.VMEM((128, 128), F32),
        pltpu.VMEM((2, 4, 16, 128), F32),
        pltpu.VMEM((256, 128), F32),
        pltpu.VMEM((128, 128), F32),
        pltpu.VMEM((2, 16, 128), jnp.int32),
        pltpu.VMEM((128, 1152), BF16),
        pltpu.VMEM((8, 1152), F32),
        pltpu.VMEM((9, 8, 128), F32),
        pltpu.VMEM((9, 8, 128), F32),
        pltpu.VMEM((8, 1280), F32),
        pltpu.SemaphoreType.DMA((9,)),
        pltpu.SemaphoreType.DMA((N_SEND,)),
        pltpu.SemaphoreType.DMA((N_RECV,)),
        pltpu.SemaphoreType.DMA((6,)),
        pltpu.SemaphoreType.DMA((6,)),
    ]
    tilts = [t.reshape(16, 128) for t in (tilt_min, tilt_max, tilt_axis)]
    return pl.pallas_call(
        kernel,
        out_shape=pltpu.VMEM((8, 1152), F32),
        in_specs=[pl.BlockSpec(memory_space=pl.ANY)] * 4,
        out_specs=vmem,
        scratch_shapes=scratch,
        compiler_params=pltpu.CompilerParams(
            collective_id=0, has_side_effects=True, vmem_limit_bytes=56 * 2**20
        ),
    )(spectra, *tilts)


def solution(mesh):
    in_specs = (P(None, "af", "pa"), P(), P(), P())
    out_specs = P(("pa", "af"), None)
    return jax.shard_map(shards, mesh=mesh, in_specs=in_specs, out_specs=out_specs, check_vma=False)
```

```python
import functools
import math

import jax
import jax.numpy as jnp
from jax import lax
from jax.experimental import pallas as pl
from jax.experimental.pallas import tpu as pltpu
from jax.sharding import PartitionSpec as P

MESH = pl.DeviceIdType.MESH
F32 = jnp.float32
BF16 = jnp.bfloat16

G = 48
HALF = 25
VD = 3600
Q = 464
KC = 4 * Q
H1, H2 = 240, 224
A = 2 * Q + H1
B = 2 * Q + H2
MID = VD - KC
CHUNKS = ((0, 96), (96, 96), (192, 96), (288, 96), (384, 80))
T_LO, T_HI, N_T = 46, 70, 25
eps_norm = 1e-06


def coords():
    pa = lax.axis_index("pa")
    af = lax.axis_index("af")
    return pa // 8, (pa // 2) % 4, pa % 2, af // 2, af % 2


def dev(xl, y, core, z, xh):
    return {"pa": (xl * 4 + y) * 2 + core, "af": z * 2 + xh}


def tdot(lhs, rhs):
    return lax.dot_general(lhs, rhs, (((0,), (0,)), ((), ())), preferred_element_type=F32)


def cells(first, shape):
    v = (first + lax.broadcasted_iota(jnp.int32, shape, 0)).astype(F32)
    q = jnp.floor((v + 0.5) * (1.0 / HALF))
    iz = v - q * HALF
    ix = jnp.floor((q + 0.5) * (1.0 / G))
    iy = q - ix * G
    fx = jnp.where(ix < G // 2, ix, ix - G)
    fy = jnp.where(iy < G // 2, iy, iy - G)
    return fx, fy, iz

N_RECV = 74
N_SEND = 32


def kernel(spec_hbm, tmin_hbm, tmax_hbm, axis_hbm, out_ref, tilt, raw, m, wt, o, ow, ra, rb, rbw, acc, inc, xin0, xin2,
           zl, rz, fin0, fin1, fin2, fin3, pw, cm, tt, tl, tg, tf, cls, hot, own, nsend, oth, cross, load_sem, ssem, rsem, gsend, grecv):
    xl, y, core, z, xh = coords()
    pa = lax.axis_index("pa")
    af = lax.axis_index("af")
    yp, ym = (y + 1) % 4, (y + 3) % 4
    zp, zm = (z + 1) % 8, (z + 7) % 8
    me_x = xh * 2 + xl
    started = []

    def rdma(src, dst, target):
        i = len(started)
        if i >= N_SEND:
            started[i - N_SEND].wait_send()
        c = pltpu.make_async_remote_copy(
            src_ref=src,
            dst_ref=dst,
            send_sem=ssem.at[i % N_SEND],
            recv_sem=rsem.at[i],
            device_id=target,
            device_id_type=MESH,
        )
        c.start()
        started.append(c)
        return c

    def in_group(g, src, dst, target):
        return pltpu.make_async_remote_copy(
            src_ref=src, dst_ref=dst, send_sem=gsend.at[g], recv_sem=grecv.at[g], device_id=target, device_id_type=MESH
        )

    def group_wait(g, size):
        c = in_group(g, size, size, dev(xl, y, 1 - core, z, xh))
        c.wait_recv()
        c.wait_send()

    barrier = pltpu.get_barrier_semaphore()
    peers = [
        dev(xl, y, 1 - core, z, xh),
        dev(1 - xl, y, core, z, xh),
        dev(1 - xl, y, 1 - core, z, xh),
        dev(xl, yp, core, z, xh),
        dev(xl, ym, core, z, xh),
        dev(xl, y, core, z, 1 - xh),
        dev(xl, y, core, zp, xh),
        dev(xl, y, core, zm, xh),
    ]
    for peer in peers:
        pl.semaphore_signal(barrier, inc=1, device_id=peer, device_id_type=MESH)
    loads = []
    for i, ref in enumerate((tmin_hbm, tmax_hbm, axis_hbm)):
        c = pltpu.make_async_copy(ref, tilt.at[i], load_sem.at[i])
        c.start()
        loads.append(c)
    tmin_ref, tmax_ref, axis_ref = tilt.at[0], tilt.at[1], tilt.at[2]
    for first, n in ((core * KC, MID), (MID, KC - MID), ((1 - core) * KC, MID)):
        here = pl.ds(first if isinstance(first, int) else pl.multiple_of(first, 16), n)
        for p in range(2):
            c = pltpu.make_async_copy(spec_hbm.at[p, here], raw.at[p, here], load_sem.at[len(loads)])
            c.start()
            loads.append(c)
    raw[:, VD:, :] = jnp.zeros((2, 2 * KC - VD, 128), BF16)

    for c in loads[:3]:
        c.wait()
    cls[0] = axis_ref[...] * 50 + (-T_LO - tmin_ref[...])
    cls[1] = axis_ref[...] * 50 + (N_T - T_LO + tmax_ref[...])
    lower = slopes(tmin_ref[pl.ds(pa, 1), :])
    upper = slopes(tmax_ref[pl.ds(pa, 1), :])
    axis = axis_ref[pl.ds(pa, 1), :]
    lane = lax.broadcasted_iota(jnp.int32, (1, 128), 1)
    c_axis = (lane >= 50).astype(jnp.int32)
    c_side = ((lane - c_axis * 50) >= 25).astype(jnp.int32)
    c_slope = slopes(lane - c_axis * 50 - c_side * 25 + T_LO)
    c_slope = jnp.where(lane < 100, c_slope, -1.0)

    def own_col(dx, dc):
        return pl.multiple_of(((xl ^ dx) * 2 + (core ^ dc)) * 128, 128)

    def by_chunk(half, body, slots=(0, 4)):
        def slot(s, carry):
            first = half * KC + (y + 3 - s) % 4 * Q
            for r0, n in CHUNKS:
                body(pl.multiple_of(first + r0, 16), pl.ds(pl.multiple_of(s * Q + r0, 16), n), n)
            return carry

        lax.fori_loop(*slots, slot, 0)

    def mask_half(half, slots=(0, 4)):
        def body(r0, to, n):
            fx, fy, iz = cells(af * VD + r0, (n, 128))
            u = jnp.where(axis == 1, fx, fy)
            a = jnp.abs(u)
            b = jnp.where(u >= 0.0, -iz, iz)
            keep = ((a * lower <= b) & (b <= a * upper)).astype(F32)
            for p in range(2):
                m[p, half, to, :] = (raw[p, pl.ds(r0, n), :].astype(F32) * keep).astype(BF16)

        by_chunk(half, body, slots)

    for c in loads[3:7]:
        c.wait()
    mask_half(core, (3, 4))
    pl.semaphore_wait(barrier, len(peers))

    col = own_col(0, 0)

    y1 = [[] for _ in range(4)]

    def to_minus(p, r0, n):
        c = pl.ds(own_col(p // 2, p % 2), 128)
        y1[p].append(rdma(o.at[pl.ds(r0, n), c], ra.at[pl.ds(r0 - Q, n), c], dev(xl, ym, core, z, xh)))

    def to_plus(p, r0, n, to):
        c = pl.ds(own_col(p // 2, p % 2), 128)
        y1[p].append(rdma(o.at[pl.ds(r0, n), c], rb.at[pl.ds(to, n), c], dev(xl, yp, core, z, xh)))

    def y_high(p):
        to_plus(p, 3 * Q, Q, 0)
        to_minus(p, 2 * Q, Q + H1)
        to_plus(p, 2 * Q + H1, H2, 2 * Q)

    def y_low(p):
        to_plus(p, 0, Q, Q)
        to_minus(p, Q, Q)

    def to_x(half, r0, n, target):
        return rdma(m.at[1 - xl, half, pl.ds(r0, n)], o.at[pl.ds(r0, n), pl.ds(col, 128)], target)

    x_same = []

    def first(slots, r0, n):
        if slots:
            mask_half(core, slots)
        here = pl.ds(r0, n)
        x_same.append(to_x(core, r0, n, dev(1 - xl, y, core, z, xh)))
        o[here, pl.ds(col, 128)] = m[xl, core, here]

    first(None, 3 * Q, Q)
    to_plus(0, 3 * Q, Q, 0)
    to_minus(0, 3 * Q, H1)
    first((2, 3), 2 * Q, Q)
    to_minus(0, 2 * Q, Q)
    to_plus(0, 2 * Q + H1, H2, 2 * Q)
    first((0, 2), 0, 2 * Q)
    y_low(0)
    for c in loads[7:]:
        c.wait()
    mask_half(1 - core)
    sib = rdma(m.at[xl, 1 - core], o.at[:, pl.ds(col, 128)], dev(xl, y, 1 - core, z, xh))
    x_other = [
        to_x(1 - core, r0, n, dev(1 - xl, y, 1 - core, z, xh))
        for r0, n in ((3 * Q, Q), (2 * Q, Q), (0, Q), (Q, H1), (Q + H1, H2))
    ]

    for half in range(2):

        def powers(r0, to, n, half=half):
            fx, fy, iz = cells(af * VD + r0, (n, 128))
            re = m[0, half, to, :].astype(F32)
            im = m[1, half, to, :].astype(F32)
            w = jnp.where((iz < 0.5) | (iz > 23.5), 1.0, 2.0)
            pw[half, to, :] = (w * (re * re + im * im)).astype(BF16)
            u = jnp.where(c_axis == 1, fx, fy)
            side = (u < 0.0).astype(jnp.int32)
            keep = (iz <= jnp.abs(u) * c_slope) & (side == c_side) & (lane < 100)
            cm[half, to, :] = keep.astype(F32).astype(BF16)

        by_chunk(half, powers)
        if half == 0:
            sib.wait_recv()
            y_high(1)
            y_low(1)
    tt[...] = tdot(pw[0], cm[0]) + tdot(pw[1], cm[1])

    def rows16(zz):
        return pl.ds(pl.multiple_of(((zz + 16) % 8) * 16, 16), 16)

    up, down = dev(xl, y, core, zp, xh), dev(xl, y, core, zm, xh)
    t_flows = [dict(way=1, steps=3, target=up), dict(way=-1, steps=4, target=down)]

    def t_step(s):
        for f, flow in enumerate(t_flows):
            if s > flow["steps"]:
                continue
            if s:
                flow["copy"].wait_recv()
            if s == flow["steps"]:
                continue
            here = rows16(z + flow["way"] * (flow["steps"] - s))
            if s == 0:
                src = tt.at[here]
            else:
                src = tl.at[f, s - 1]
                src[...] = src[...] + tt[here, :]
            flow["copy"] = rdma(src, tl.at[f, s], flow["target"])

    t_step(0)

    def weights(r0, to, n):
        iz = cells(af * VD + r0, (n, 128))[2]
        wt[to, :] = jnp.where((iz < 0.5) | (iz > 23.5), 1.0, 2.0).astype(BF16)

    by_chunk(core, weights)

    def weigh(dst, src, x, first, n):
        rows = slice(first, first + n)
        for dc in range(2):
            here = pl.ds(pl.multiple_of(x * 256 + dc * 128, 128), 128)
            dst[rows, here] = src[rows, here] * wt[rows, :]

    x_same[0].wait_recv()
    x_same[1].wait_recv()
    y_high(2)
    t_step(1)
    weigh(ow, o, xl, 0, KC)
    x_same[2].wait_recv()
    y_low(2)
    t_step(2)
    x_other[0].wait_recv()
    to_plus(3, 3 * Q, Q, 0)
    to_minus(3, 3 * Q, H1)
    t_step(3)
    x_other[1].wait_recv()
    to_plus(3, 2 * Q + H1, H2, 2 * Q)
    to_minus(3, 2 * Q, Q)
    t_step(4)
    def put(tile, value):
        acc[tile] = value.reshape(2, 8, 2, 8, 256)

    def side(x):
        return pl.multiple_of(x * 256, 256)

    def wrap(x, cond):
        return x ^ cond.astype(jnp.int32)

    def pair_sum(lo, n):
        tiles = pl.ds(lo, n)
        return rdma(acc.at[tiles, 1 - core], inc.at[tiles], dev(xl, y, 1 - core, z, xh))

    def pair_add(copy, lo, n):
        copy.wait_recv()
        for t in range(lo, lo + n):
            inc[t] = inc[t] + acc[t, core]

    def cols(ref, x, first, n):
        return ref[first : first + n, pl.ds(side(x), 256)]

    def add(tile, value):
        acc[tile] = acc[tile] + value.reshape(2, 8, 2, 8, 256)

    def own_tiles(first, n, store):
        for x in range(2):
            for slot, xo in ((0, x), (1, 1 - x)):
                store(x * 2 + slot, tdot(cols(ow, x, first, n), cols(o, xo, first, n)))

    weigh(ow, o, 1 - xl, 2 * Q, 2 * Q)
    own_tiles(2 * Q, 2 * Q, put)
    x_other[2].wait_recv()
    to_plus(3, 0, Q, Q)
    weigh(ow, o, 1 - xl, 0, Q)
    own_tiles(0, Q, add)
    x_other[3].wait_recv()
    to_minus(3, Q, H1)
    x_other[4].wait_recv()
    to_minus(3, Q + H1, H2)
    weigh(ow, o, 1 - xl, Q, Q)
    own_tiles(Q, Q, add)
    pair0 = pair_sum(0, 4)
    mine16 = rows16(z)
    mine_g = pl.ds(pl.multiple_of(xh * 128 + z * 16, 16), 16)
    tg[mine_g, :] = tt[mine16, :] + tl[0, 2] + tl[1, 3]
    for dz in range(8):
        for dh in range(2):
            if dz or dh:
                part = tg.at[mine_g]
                in_group(0, part, part, dev(xl, y, core, (z + dz) % 8, xh ^ dh)).start()


    def x_send(lo, n, buf):
        copies = []
        for dx in range(1, 4):
            xo, ho = xl ^ (dx % 2), xh ^ (dx // 2)
            copies.append(
                rdma(inc.at[pl.ds(lo + xo * n, n), :, ho], buf.at[me_x], dev(xo, y, core, z, ho))
            )
        return copies

    def x_sum(lo, n, buf, copies):
        for c in copies:
            c.wait_recv()
        total = inc[pl.ds(lo + xl * n, n), :, xh]
        for dx in range(1, 4):
            total = total + buf[(xh ^ (dx // 2)) * 2 + (xl ^ (dx % 2))]
        buf[me_x] = total

    early = (wrap(xl, y == 3), xl, wrap(1 - xl, y == 0), xl)

    def plus_kinds(lo, late, first, n, store):
        x0, x1 = early[0] ^ late, early[1] ^ late
        store(lo, tdot(cols(ow, x0, first, n), cols(ra, xl ^ late, first, n)))
        store(lo + 1, tdot(cols(ra, x1, first, n), cols(ow, wrap(1 - x1, y == 3), first, n)))

    def minus_kinds(lo, late):
        x2, x3 = early[2] ^ late, early[3] ^ late
        xr = xl ^ late
        put(
            lo + 2,
            tdot(cols(ow, x2, 0, Q), cols(rb, xr, 0, Q))
            + tdot(cols(ow, x2, 3 * Q + H1, H2), cols(rb, xr, 2 * Q, H2)),
        )
        put(
            lo + 3,
            tdot(cols(rb, x3, 0, Q), cols(ow, wrap(x3, y == 0), 0, Q))
            + tdot(cols(rb, x3, 2 * Q, H2), cols(ow, wrap(x3, y == 0), 3 * Q + H1, H2)),
        )

    def second_minus(first, n, store):
        for x in range(2):
            store(12 + x, tdot(cols(rbw, x, first, n), cols(ra, wrap(x, ym >= 2), first, n)))

    def second_plus(first, n, store):
        for x in range(2):
            store(14 + x, tdot(cols(ra, x, first, n), cols(rbw, wrap(x, yp >= 2), first, n)))

    for p in range(2):
        for d in y1[p]:
            d.wait_recv()
    plus_kinds(4, 0, 0, A, put)
    minus_kinds(4, 0)
    pair1 = pair_sum(4, 4)
    weigh(rbw, rb, xl, 0, 2 * Q)
    pair_add(pair0, 0, 4)
    x0 = x_send(0, 2, xin0)

    owners = (y, yp, y, ym)
    flows = []
    for g in range(4):
        for way in (1, -1):
            flows.append(
                dict(
                    lo=4 + g * 2,
                    way=way,
                    far=(g % 2 == 0) == (way == -1),
                    near=up if way > 0 else down,
                    second=dev(xl, y, core, (z + 2 * way + 8) % 8, xh),
                )
            )
    early_flows, late_flows = (0, 4), (4, 8)

    def z_step(s, which):
        for f, flow in list(enumerate(flows))[which[0] : which[1]]:
            tiles, way = pl.ds(flow["lo"], 2), flow["way"]

            def rows_for(d, way=way):
                return (z + way * d + 8) % 8

            if s == 0:
                flow["copy"] = rdma(inc.at[tiles, rows_for(3)], zl.at[f, 0], flow["near"])
                if flow["far"]:
                    flow["copy2"] = rdma(inc.at[tiles, rows_for(4)], zl.at[f, 1], flow["second"])
            elif s == 1:
                flow["copy"].wait_recv()
                value = zl[f, 0] + inc[tiles, rows_for(2)]
                if flow["far"]:
                    flow["copy2"].wait_recv()
                    value = value + zl[f, 1]
                zl[f, 0] = value
                flow["copy"] = rdma(zl.at[f, 0], zl.at[f, 2], flow["near"])
            else:
                flow["copy"].wait_recv()
                zl[f, 2] = zl[f, 2] + inc[tiles, rows_for(1)]
                for i in range(2):
                    kind, late = (flow["lo"] + i) % 4, f // 4
                    for ho in (xh, 1 - xh):
                        in_group(
                            1,
                            zl.at[f, 2, i, ho],
                            fin1.at[(1 - way) // 2, me_x, kind],
                            dev(early[kind] ^ late, owners[kind], core, rows_for(1), ho),
                        ).start()

    def own_rows():
        for kind in range(4):
            rz[kind * 2 + early[kind]] = inc[4 + kind, z]
            rz[kind * 2 + (early[kind] ^ 1)] = inc[8 + kind, z]
        for dx in range(4):
            xo, ho = xl ^ (dx % 2), xh ^ (dx // 2)
            for kind, yo in enumerate(owners):
                if dx or kind % 2:
                    in_group(2, rz.at[2 * kind + xo, ho], fin3.at[me_x * 4 + kind], dev(xo, yo, core, z, ho)).start()
                else:
                    fin3[me_x * 4 + kind] = rz[2 * kind + xo, ho]

    pair_add(pair1, 4, 4)
    z_step(0, early_flows)
    for d in y1[2] + y1[3][:-1]:
        d.wait_recv()
    minus_kinds(8, 1)
    pair_b = pair_sum(10, 2)
    weigh(rbw, rb, 1 - xl, 0, 2 * Q)
    second_minus(Q, Q, put)
    second_plus(Q, Q, put)
    plus_kinds(8, 1, Q, Q + H1, put)
    pair_add(pair_b, 10, 2)
    z_step(0, (6, 8))
    y1[3][-1].wait_recv()
    second_minus(0, Q, add)
    pair_c = pair_sum(12, 2)
    second_plus(0, Q, add)
    pair_d = pair_sum(14, 2)
    plus_kinds(8, 1, 0, Q, add)
    pair_a = pair_sum(8, 2)
    pair_add(pair_c, 12, 2)
    x2 = x_send(12, 1, xin2.at[0])
    pair_add(pair_d, 14, 2)
    x3 = x_send(14, 1, xin2.at[1])
    pair_add(pair_a, 8, 2)
    z_step(0, (4, 6))
    z_step(1, early_flows)
    group_wait(0, tg.at[0:240])
    tf[...] = tg[0:128] + tg[128:256]

    def split(value):
        hi = value.astype(BF16).astype(F32)
        mid = (value - hi).astype(BF16).astype(F32)
        return hi, mid, value - hi - mid

    wide = lax.broadcasted_iota(jnp.int32, (128, 128), 0)
    pick = lax.broadcasted_iota(jnp.int32, (8, 128), 1) == (
        lax.broadcasted_iota(jnp.int32, (8, 128), 0) + af * 8
    )
    lanes = lax.broadcasted_iota(jnp.int32, (8, 128), 1).astype(F32)
    rows8 = []
    for k in range(9):
        j = (pa + k) % 16
        one, two = cls[0, pl.ds(j, 1), :], cls[1, pl.ds(j, 1), :]
        hot[:, k * 128 : (k + 1) * 128] = ((wide == one) | (wide == two)).astype(F32).astype(BF16)
        i = (pa + 16 - k) % 16
        ends = [
            jnp.sum(jnp.where(pick, cls[e, pl.ds(i, 1), :].astype(F32), 0.0), axis=1, keepdims=True) for e in range(2)
        ]
        rows8.append(((lanes == ends[0]) | (lanes == ends[1])).astype(F32))
    rows8.append(jnp.zeros((8, 128), F32))
    rows80 = jnp.concatenate(rows8, axis=0).astype(BF16)
    t8 = jnp.concatenate([*split(tf[pl.ds(pl.multiple_of(af * 8, 8), 8), :]), jnp.zeros((8, 128), F32)], axis=0)
    t8 = jnp.dot(t8.astype(BF16), hot[...], preferred_element_type=F32)
    own[...] = t8[0:8] + t8[8:16] + t8[16:24]
    others = sum(
        lax.dot_general(rows80, part.astype(BF16), (((1,), (1,)), ((), ())), preferred_element_type=F32)
        for part in split(tf[...])
    )
    for k in range(9):
        nsend[k] = others[k * 8 : (k + 1) * 8]
    oth[0] = nsend[0]

    for k in range(1, 9):
        in_group(4, nsend.at[k], oth.at[k], {"pa": (pa + 16 - k) % 16, "af": af}).start()
    z_step(1, (6, 8))
    x_sum(0, 2, xin0, x0)
    for dz in range(1, 8):
        zo = (z + dz) % 8
        in_group(3, xin0.at[me_x, :, zo], fin0.at[z], dev(xl, y, core, zo, xh)).start()
    fin0[z] = xin0[me_x, :, z]
    z_step(1, (4, 6))
    z_step(2, early_flows)
    z_step(2, (6, 8))
    own_rows()

    z_step(2, (4, 6))
    for i, (copies, yo) in enumerate(((x2, ym), (x3, yp))):
        x_sum(12 + 2 * i, 1, xin2.at[i], copies)
        for dz in (4, 3, 5, 2, 6, 1, 7, 0):
            zo = (z + dz) % 8
            in_group(5, xin2.at[i, me_x, 0, zo], fin2.at[z, i], dev(xl, yo, core, zo, xh)).start()
    for c in started[-N_SEND:]:
        c.wait_send()
    group_wait(3, fin0.at[0:7])
    group_wait(4, oth.at[0:8])
    group_wait(2, fin3.at[0:14])
    group_wait(1, fin1)
    group_wait(5, fin2)

    def total(parts):
        return functools.reduce(lambda p, q: p + q, parts)

    cross[:, 0:256] = total([fin0[s, 0] for s in range(8)])
    def kind_sum(kinds_of):
        return total(
            [fin3[s * 4 + t] for t in kinds_of for s in range(4)]
            + [fin1[w, s, t] for t in kinds_of for w in range(2) for s in range(4)]
        )

    cross[:, 256:512] = kind_sum((0, 3))
    cross[:, 512:768] = total([fin2[s, t] for t in range(2) for s in range(8)])
    cross[:, 768:1024] = kind_sum((1, 2))
    cross[:, 1024:1280] = total([fin0[s, 1] for s in range(8)])
    shift = pl.multiple_of(core * 128, 128)
    for k in range(9):
        here = slice(k * 128, (k + 1) * 128)
        out_ref[:, here] = cross[:, pl.ds(pl.multiple_of(shift + k * 128, 128), 128)] / jnp.sqrt(
            own[:, here] * oth[k] + eps_norm
        )


def slopes(degrees):
    return jnp.tan(degrees.astype(F32) * (math.pi / 180.0))


def shards(spectra, tilt_min, tilt_max, tilt_axis):
    vmem = pl.BlockSpec(memory_space=pltpu.VMEM)
    scratch = [
        pltpu.VMEM((3, 16, 128), jnp.int32),
        pltpu.VMEM((2, 2 * KC, 128), BF16),
        pltpu.VMEM((2, 2, KC, 128), BF16),
        pltpu.VMEM((KC, 128), BF16),
        pltpu.VMEM((KC, 512), BF16),
        pltpu.VMEM((KC, 512), BF16),
        pltpu.VMEM((A, 512), BF16),
        pltpu.VMEM((B, 512), BF16),
        pltpu.VMEM((2 * Q, 512), BF16),
        pltpu.VMEM((16, 2, 8, 2, 8, 256), F32),
        pltpu.VMEM((16, 8, 2, 8, 256), F32),
        pltpu.VMEM((4, 2, 8, 8, 256), F32),
        pltpu.VMEM((2, 4, 1, 8, 8, 256), F32),
        pltpu.VMEM((8, 3, 2, 2, 8, 256), F32),
        pltpu.VMEM((8, 2, 8, 256), F32),
        pltpu.VMEM((8, 2, 8, 256), F32),
        pltpu.VMEM((2, 4, 4, 8, 256), F32),
        pltpu.VMEM((8, 2, 8, 256), F32),
        pltpu.VMEM((16, 8, 256), F32),
        pltpu.VMEM((2, KC, 128), BF16),
        pltpu.VMEM((2, KC, 128), BF16),
        pltpu.VMEM((128, 128), F32),
        pltpu.VMEM((2, 4, 16, 128), F32),
        pltpu.VMEM((256, 128), F32),
        pltpu.VMEM((128, 128), F32),
        pltpu.VMEM((2, 16, 128), jnp.int32),
        pltpu.VMEM((128, 1152), BF16),
        pltpu.VMEM((8, 1152), F32),
        pltpu.VMEM((9, 8, 128), F32),
        pltpu.VMEM((9, 8, 128), F32),
        pltpu.VMEM((8, 1280), F32),
        pltpu.SemaphoreType.DMA((9,)),
        pltpu.SemaphoreType.DMA((N_SEND,)),
        pltpu.SemaphoreType.DMA((N_RECV,)),
        pltpu.SemaphoreType.DMA((6,)),
        pltpu.SemaphoreType.DMA((6,)),
    ]
    tilts = [t.reshape(16, 128) for t in (tilt_min, tilt_max, tilt_axis)]
    return pl.pallas_call(
        kernel,
        out_shape=pltpu.VMEM((8, 1152), F32),
        in_specs=[pl.BlockSpec(memory_space=pl.ANY)] * 4,
        out_specs=vmem,
        scratch_shapes=scratch,
        compiler_params=pltpu.CompilerParams(
            collective_id=0, has_side_effects=True, vmem_limit_bytes=56 * 2**20
        ),
    )(spectra, *tilts)


def solution(mesh):
    in_specs = (P(None, "af", "pa"), P(), P(), P())
    out_specs = P(("pa", "af"), None)
    return jax.shard_map(shards, mesh=mesh, in_specs=in_specs, out_specs=out_specs, check_vma=False)
```

```python
import functools
import math

import jax
import jax.numpy as jnp
from jax import lax
from jax.experimental import pallas as pl
from jax.experimental.pallas import tpu as pltpu
from jax.sharding import PartitionSpec as P

MESH = pl.DeviceIdType.MESH
F32 = jnp.float32
BF16 = jnp.bfloat16

G = 48
HALF = 25
VD = 3600
Q = 464
KC = 4 * Q
H1, H2 = 240, 224
A = 2 * Q + H1
B = 2 * Q + H2
MID = VD - KC
CHUNKS = ((0, 96), (96, 96), (192, 96), (288, 96), (384, 80))
T_LO, T_HI, N_T = 46, 70, 25
eps_norm = 1e-06


def coords():
    pa = lax.axis_index("pa")
    af = lax.axis_index("af")
    return pa // 8, (pa // 2) % 4, pa % 2, af // 2, af % 2


def dev(xl, y, core, z, xh):
    return {"pa": (xl * 4 + y) * 2 + core, "af": z * 2 + xh}


def tdot(lhs, rhs):
    return lax.dot_general(lhs, rhs, (((0,), (0,)), ((), ())), preferred_element_type=F32)


def cells(first, shape):
    v = (first + lax.broadcasted_iota(jnp.int32, shape, 0)).astype(F32)
    q = jnp.floor((v + 0.5) * (1.0 / HALF))
    iz = v - q * HALF
    ix = jnp.floor((q + 0.5) * (1.0 / G))
    iy = q - ix * G
    fx = jnp.where(ix < G // 2, ix, ix - G)
    fy = jnp.where(iy < G // 2, iy, iy - G)
    return fx, fy, iz

N_RECV = 72
N_SEND = 32


def kernel(spec_hbm, tmin_hbm, tmax_hbm, axis_hbm, out_ref, tilt, raw, m, wt, o, ow, ra, rb, rbw, acc, inc, xin0, xin2,
           zl, rz, fin0, fin1, fin2, fin3, pw, cm, tt, tl, tg, tf, cls, hot, own, nsend, oth, cross, load_sem, ssem, rsem, gsend, grecv):
    xl, y, core, z, xh = coords()
    pa = lax.axis_index("pa")
    af = lax.axis_index("af")
    yp, ym = (y + 1) % 4, (y + 3) % 4
    zp, zm = (z + 1) % 8, (z + 7) % 8
    me_x = xh * 2 + xl
    started = []

    def rdma(src, dst, target):
        i = len(started)
        if i >= N_SEND:
            started[i - N_SEND].wait_send()
        c = pltpu.make_async_remote_copy(
            src_ref=src,
            dst_ref=dst,
            send_sem=ssem.at[i % N_SEND],
            recv_sem=rsem.at[i],
            device_id=target,
            device_id_type=MESH,
        )
        c.start()
        started.append(c)
        return c

    def in_group(g, src, dst, target):
        return pltpu.make_async_remote_copy(
            src_ref=src, dst_ref=dst, send_sem=gsend.at[g], recv_sem=grecv.at[g], device_id=target, device_id_type=MESH
        )

    def group_wait(g, size):
        c = in_group(g, size, size, dev(xl, y, 1 - core, z, xh))
        c.wait_recv()
        c.wait_send()

    barrier = pltpu.get_barrier_semaphore()
    peers = [
        dev(xl, y, 1 - core, z, xh),
        dev(1 - xl, y, core, z, xh),
        dev(1 - xl, y, 1 - core, z, xh),
        dev(xl, yp, core, z, xh),
        dev(xl, ym, core, z, xh),
        dev(xl, y, core, z, 1 - xh),
        dev(xl, y, core, zp, xh),
        dev(xl, y, core, zm, xh),
    ]
    for peer in peers:
        pl.semaphore_signal(barrier, inc=1, device_id=peer, device_id_type=MESH)
    loads = []
    for i, ref in enumerate((tmin_hbm, tmax_hbm, axis_hbm)):
        c = pltpu.make_async_copy(ref, tilt.at[i], load_sem.at[i])
        c.start()
        loads.append(c)
    tmin_ref, tmax_ref, axis_ref = tilt.at[0], tilt.at[1], tilt.at[2]
    for first, n in ((core * KC, MID), (MID, KC - MID), ((1 - core) * KC, MID)):
        here = pl.ds(first if isinstance(first, int) else pl.multiple_of(first, 16), n)
        for p in range(2):
            c = pltpu.make_async_copy(spec_hbm.at[p, here], raw.at[p, here], load_sem.at[len(loads)])
            c.start()
            loads.append(c)
    raw[:, VD:, :] = jnp.zeros((2, 2 * KC - VD, 128), BF16)

    for c in loads[:3]:
        c.wait()
    cls[0] = axis_ref[...] * 50 + (-T_LO - tmin_ref[...])
    cls[1] = axis_ref[...] * 50 + (N_T - T_LO + tmax_ref[...])
    lower = slopes(tmin_ref[pl.ds(pa, 1), :])
    upper = slopes(tmax_ref[pl.ds(pa, 1), :])
    axis = axis_ref[pl.ds(pa, 1), :]
    lane = lax.broadcasted_iota(jnp.int32, (1, 128), 1)
    c_axis = (lane >= 50).astype(jnp.int32)
    c_side = ((lane - c_axis * 50) >= 25).astype(jnp.int32)
    c_slope = slopes(lane - c_axis * 50 - c_side * 25 + T_LO)
    c_slope = jnp.where(lane < 100, c_slope, -1.0)

    def own_col(dx, dc):
        return pl.multiple_of(((xl ^ dx) * 2 + (core ^ dc)) * 128, 128)

    def by_chunk(half, body, slots=(0, 4)):
        def slot(s, carry):
            first = half * KC + (y + 3 - s) % 4 * Q
            for r0, n in CHUNKS:
                body(pl.multiple_of(first + r0, 16), pl.ds(pl.multiple_of(s * Q + r0, 16), n), n)
            return carry

        lax.fori_loop(*slots, slot, 0)

    def mask_half(half, slots=(0, 4)):
        def body(r0, to, n):
            fx, fy, iz = cells(af * VD + r0, (n, 128))
            u = jnp.where(axis == 1, fx, fy)
            a = jnp.abs(u)
            b = jnp.where(u >= 0.0, -iz, iz)
            keep = ((a * lower <= b) & (b <= a * upper)).astype(F32)
            for p in range(2):
                m[p, half, to, :] = (raw[p, pl.ds(r0, n), :].astype(F32) * keep).astype(BF16)

        by_chunk(half, body, slots)

    for c in loads[3:7]:
        c.wait()
    mask_half(core, (3, 4))
    pl.semaphore_wait(barrier, len(peers))

    col = own_col(0, 0)

    y1 = [[] for _ in range(4)]

    def to_minus(p, r0, n):
        c = pl.ds(own_col(p // 2, p % 2), 128)
        y1[p].append(rdma(o.at[pl.ds(r0, n), c], ra.at[pl.ds(r0 - Q, n), c], dev(xl, ym, core, z, xh)))

    def to_plus(p, r0, n, to):
        c = pl.ds(own_col(p // 2, p % 2), 128)
        y1[p].append(rdma(o.at[pl.ds(r0, n), c], rb.at[pl.ds(to, n), c], dev(xl, yp, core, z, xh)))

    def y_high(p):
        to_plus(p, 3 * Q, Q, 0)
        to_minus(p, 2 * Q, Q + H1)
        to_plus(p, 2 * Q + H1, H2, 2 * Q)

    def y_low(p):
        to_plus(p, 0, Q, Q)
        to_minus(p, Q, Q)

    def to_x(half, r0, n, target):
        return rdma(m.at[1 - xl, half, pl.ds(r0, n)], o.at[pl.ds(r0, n), pl.ds(col, 128)], target)

    x_same = []

    def first(slots, r0, n):
        if slots:
            mask_half(core, slots)
        here = pl.ds(r0, n)
        x_same.append(to_x(core, r0, n, dev(1 - xl, y, core, z, xh)))
        o[here, pl.ds(col, 128)] = m[xl, core, here]

    first(None, 3 * Q, Q)
    to_plus(0, 3 * Q, Q, 0)
    to_minus(0, 3 * Q, H1)
    first((2, 3), 2 * Q, Q)
    to_minus(0, 2 * Q, Q)
    to_plus(0, 2 * Q + H1, H2, 2 * Q)
    first((0, 2), 0, 2 * Q)
    y_low(0)
    for c in loads[7:]:
        c.wait()
    mask_half(1 - core)
    sib = rdma(m.at[xl, 1 - core], o.at[:, pl.ds(col, 128)], dev(xl, y, 1 - core, z, xh))
    x_other = [to_x(1 - core, q * Q, Q, dev(1 - xl, y, 1 - core, z, xh)) for q in (3, 2, 0, 1)]

    for half in range(2):

        def powers(r0, to, n, half=half):
            fx, fy, iz = cells(af * VD + r0, (n, 128))
            re = m[0, half, to, :].astype(F32)
            im = m[1, half, to, :].astype(F32)
            w = jnp.where((iz < 0.5) | (iz > 23.5), 1.0, 2.0)
            pw[half, to, :] = (w * (re * re + im * im)).astype(BF16)
            u = jnp.where(c_axis == 1, fx, fy)
            side = (u < 0.0).astype(jnp.int32)
            keep = (iz <= jnp.abs(u) * c_slope) & (side == c_side) & (lane < 100)
            cm[half, to, :] = keep.astype(F32).astype(BF16)

        by_chunk(half, powers)
        if half == 0:
            sib.wait_recv()
            y_high(1)
            y_low(1)
    tt[...] = tdot(pw[0], cm[0]) + tdot(pw[1], cm[1])

    def rows16(zz):
        return pl.ds(pl.multiple_of(((zz + 16) % 8) * 16, 16), 16)

    up, down = dev(xl, y, core, zp, xh), dev(xl, y, core, zm, xh)
    t_flows = [dict(way=1, steps=3, target=up), dict(way=-1, steps=4, target=down)]

    def t_step(s):
        for f, flow in enumerate(t_flows):
            if s > flow["steps"]:
                continue
            if s:
                flow["copy"].wait_recv()
            if s == flow["steps"]:
                continue
            here = rows16(z + flow["way"] * (flow["steps"] - s))
            if s == 0:
                src = tt.at[here]
            else:
                src = tl.at[f, s - 1]
                src[...] = src[...] + tt[here, :]
            flow["copy"] = rdma(src, tl.at[f, s], flow["target"])

    t_step(0)

    def weights(r0, to, n):
        iz = cells(af * VD + r0, (n, 128))[2]
        wt[to, :] = jnp.where((iz < 0.5) | (iz > 23.5), 1.0, 2.0).astype(BF16)

    by_chunk(core, weights)

    def weigh(dst, src, x, first, n):
        rows = slice(first, first + n)
        for dc in range(2):
            here = pl.ds(pl.multiple_of(x * 256 + dc * 128, 128), 128)
            dst[rows, here] = src[rows, here] * wt[rows, :]

    x_same[0].wait_recv()
    x_same[1].wait_recv()
    y_high(2)
    t_step(1)
    weigh(ow, o, xl, 0, KC)
    x_same[2].wait_recv()
    y_low(2)
    t_step(2)
    x_other[0].wait_recv()
    to_plus(3, 3 * Q, Q, 0)
    to_minus(3, 3 * Q, H1)
    t_step(3)
    x_other[1].wait_recv()
    to_plus(3, 2 * Q + H1, H2, 2 * Q)
    to_minus(3, 2 * Q, Q)
    t_step(4)
    mine16 = rows16(z)
    mine_g = pl.ds(pl.multiple_of(xh * 128 + z * 16, 16), 16)
    tg[mine_g, :] = tt[mine16, :] + tl[0, 2] + tl[1, 3]
    for dz in range(8):
        for dh in range(2):
            if dz or dh:
                part = tg.at[mine_g]
                in_group(0, part, part, dev(xl, y, core, (z + dz) % 8, xh ^ dh)).start()

    def put(tile, value):
        acc[tile] = value.reshape(2, 8, 2, 8, 256)

    def side(x):
        return pl.multiple_of(x * 256, 256)

    def wrap(x, cond):
        return x ^ cond.astype(jnp.int32)

    def pair_sum(lo, n):
        tiles = pl.ds(lo, n)
        return rdma(acc.at[tiles, 1 - core], inc.at[tiles], dev(xl, y, 1 - core, z, xh))

    def pair_add(copy, lo, n):
        copy.wait_recv()
        for t in range(lo, lo + n):
            inc[t] = inc[t] + acc[t, core]

    def cols(ref, x, first, n):
        return ref[first : first + n, pl.ds(side(x), 256)]

    def add(tile, value):
        acc[tile] = acc[tile] + value.reshape(2, 8, 2, 8, 256)

    def own_tiles(first, n, store):
        for x in range(2):
            for slot, xo in ((0, x), (1, 1 - x)):
                store(x * 2 + slot, tdot(cols(ow, x, first, n), cols(o, xo, first, n)))

    weigh(ow, o, 1 - xl, 2 * Q, 2 * Q)
    own_tiles(2 * Q, 2 * Q, put)
    x_other[2].wait_recv()
    to_plus(3, 0, Q, Q)
    weigh(ow, o, 1 - xl, 0, Q)
    own_tiles(0, Q, add)
    x_other[3].wait_recv()
    to_minus(3, Q, Q)
    weigh(ow, o, 1 - xl, Q, Q)
    own_tiles(Q, Q, add)
    pair0 = pair_sum(0, 4)

    def x_send(lo, n, buf):
        copies = []
        for dx in range(1, 4):
            xo, ho = xl ^ (dx % 2), xh ^ (dx // 2)
            copies.append(
                rdma(inc.at[pl.ds(lo + xo * n, n), :, ho], buf.at[me_x], dev(xo, y, core, z, ho))
            )
        return copies

    def x_sum(lo, n, buf, copies):
        for c in copies:
            c.wait_recv()
        total = inc[pl.ds(lo + xl * n, n), :, xh]
        for dx in range(1, 4):
            total = total + buf[(xh ^ (dx // 2)) * 2 + (xl ^ (dx % 2))]
        buf[me_x] = total

    early = (wrap(xl, y == 3), xl, wrap(1 - xl, y == 0), xl)

    def plus_kinds(lo, late, first, n, store):
        x0, x1 = early[0] ^ late, early[1] ^ late
        store(lo, tdot(cols(ow, x0, first, n), cols(ra, xl ^ late, first, n)))
        store(lo + 1, tdot(cols(ra, x1, first, n), cols(ow, wrap(1 - x1, y == 3), first, n)))

    def minus_kinds(lo, late):
        x2, x3 = early[2] ^ late, early[3] ^ late
        xr = xl ^ late
        put(
            lo + 2,
            tdot(cols(ow, x2, 0, Q), cols(rb, xr, 0, Q))
            + tdot(cols(ow, x2, 3 * Q + H1, H2), cols(rb, xr, 2 * Q, H2)),
        )
        put(
            lo + 3,
            tdot(cols(rb, x3, 0, Q), cols(ow, wrap(x3, y == 0), 0, Q))
            + tdot(cols(rb, x3, 2 * Q, H2), cols(ow, wrap(x3, y == 0), 3 * Q + H1, H2)),
        )

    def second_minus(first, n, store):
        for x in range(2):
            store(12 + x, tdot(cols(rbw, x, first, n), cols(ra, wrap(x, ym >= 2), first, n)))

    def second_plus(first, n, store):
        for x in range(2):
            store(14 + x, tdot(cols(ra, x, first, n), cols(rbw, wrap(x, yp >= 2), first, n)))

    for p in range(2):
        for d in y1[p]:
            d.wait_recv()
    plus_kinds(4, 0, 0, A, put)
    minus_kinds(4, 0)
    pair1 = pair_sum(4, 4)
    weigh(rbw, rb, xl, 0, 2 * Q)
    pair_add(pair0, 0, 4)
    x0 = x_send(0, 2, xin0)

    owners = (y, yp, y, ym)
    flows = []
    for g in range(4):
        for way in (1, -1):
            flows.append(
                dict(
                    lo=4 + g * 2,
                    way=way,
                    far=(g % 2 == 0) == (way == -1),
                    near=up if way > 0 else down,
                    second=dev(xl, y, core, (z + 2 * way + 8) % 8, xh),
                )
            )
    early_flows, late_flows = (0, 4), (4, 8)

    def z_step(s, which):
        for f, flow in list(enumerate(flows))[which[0] : which[1]]:
            tiles, way = pl.ds(flow["lo"], 2), flow["way"]

            def rows_for(d, way=way):
                return (z + way * d + 8) % 8

            if s == 0:
                flow["copy"] = rdma(inc.at[tiles, rows_for(3)], zl.at[f, 0], flow["near"])
                if flow["far"]:
                    flow["copy2"] = rdma(inc.at[tiles, rows_for(4)], zl.at[f, 1], flow["second"])
            elif s == 1:
                flow["copy"].wait_recv()
                value = zl[f, 0] + inc[tiles, rows_for(2)]
                if flow["far"]:
                    flow["copy2"].wait_recv()
                    value = value + zl[f, 1]
                zl[f, 0] = value
                flow["copy"] = rdma(zl.at[f, 0], zl.at[f, 2], flow["near"])
            else:
                flow["copy"].wait_recv()
                zl[f, 2] = zl[f, 2] + inc[tiles, rows_for(1)]
                for i in range(2):
                    kind, late = (flow["lo"] + i) % 4, f // 4
                    for ho in (xh, 1 - xh):
                        in_group(
                            1,
                            zl.at[f, 2, i, ho],
                            fin1.at[(1 - way) // 2, me_x, kind],
                            dev(early[kind] ^ late, owners[kind], core, rows_for(1), ho),
                        ).start()

    def own_rows():
        for kind in range(4):
            rz[kind * 2 + early[kind]] = inc[4 + kind, z]
            rz[kind * 2 + (early[kind] ^ 1)] = inc[8 + kind, z]
        for dx in range(4):
            xo, ho = xl ^ (dx % 2), xh ^ (dx // 2)
            for kind, yo in enumerate(owners):
                if dx or kind % 2:
                    in_group(2, rz.at[2 * kind + xo, ho], fin3.at[me_x * 4 + kind], dev(xo, yo, core, z, ho)).start()
                else:
                    fin3[me_x * 4 + kind] = rz[2 * kind + xo, ho]

    pair_add(pair1, 4, 4)
    z_step(0, early_flows)
    for d in y1[2] + y1[3][:-1]:
        d.wait_recv()
    minus_kinds(8, 1)
    pair_b = pair_sum(10, 2)
    weigh(rbw, rb, 1 - xl, 0, 2 * Q)
    second_minus(Q, Q, put)
    second_plus(Q, Q, put)
    plus_kinds(8, 1, Q, Q + H1, put)
    pair_add(pair_b, 10, 2)
    z_step(0, (6, 8))
    y1[3][-1].wait_recv()
    second_minus(0, Q, add)
    pair_c = pair_sum(12, 2)
    second_plus(0, Q, add)
    pair_d = pair_sum(14, 2)
    plus_kinds(8, 1, 0, Q, add)
    pair_a = pair_sum(8, 2)
    pair_add(pair_c, 12, 2)
    x2 = x_send(12, 1, xin2.at[0])
    pair_add(pair_d, 14, 2)
    x3 = x_send(14, 1, xin2.at[1])
    pair_add(pair_a, 8, 2)
    z_step(0, (4, 6))
    z_step(1, early_flows)
    group_wait(0, tg.at[0:240])
    tf[...] = tg[0:128] + tg[128:256]

    def split(value):
        hi = value.astype(BF16).astype(F32)
        mid = (value - hi).astype(BF16).astype(F32)
        return hi, mid, value - hi - mid

    wide = lax.broadcasted_iota(jnp.int32, (128, 128), 0)
    pick = lax.broadcasted_iota(jnp.int32, (8, 128), 1) == (
        lax.broadcasted_iota(jnp.int32, (8, 128), 0) + af * 8
    )
    lanes = lax.broadcasted_iota(jnp.int32, (8, 128), 1).astype(F32)
    rows8 = []
    for k in range(9):
        j = (pa + k) % 16
        one, two = cls[0, pl.ds(j, 1), :], cls[1, pl.ds(j, 1), :]
        hot[:, k * 128 : (k + 1) * 128] = ((wide == one) | (wide == two)).astype(F32).astype(BF16)
        i = (pa + 16 - k) % 16
        ends = [
            jnp.sum(jnp.where(pick, cls[e, pl.ds(i, 1), :].astype(F32), 0.0), axis=1, keepdims=True) for e in range(2)
        ]
        rows8.append(((lanes == ends[0]) | (lanes == ends[1])).astype(F32))
    rows8.append(jnp.zeros((8, 128), F32))
    rows80 = jnp.concatenate(rows8, axis=0).astype(BF16)
    t8 = jnp.concatenate([*split(tf[pl.ds(pl.multiple_of(af * 8, 8), 8), :]), jnp.zeros((8, 128), F32)], axis=0)
    t8 = jnp.dot(t8.astype(BF16), hot[...], preferred_element_type=F32)
    own[...] = t8[0:8] + t8[8:16] + t8[16:24]
    others = sum(
        lax.dot_general(rows80, part.astype(BF16), (((1,), (1,)), ((), ())), preferred_element_type=F32)
        for part in split(tf[...])
    )
    for k in range(9):
        nsend[k] = others[k * 8 : (k + 1) * 8]
    oth[0] = nsend[0]

    for k in range(1, 9):
        in_group(4, nsend.at[k], oth.at[k], {"pa": (pa + 16 - k) % 16, "af": af}).start()
    z_step(1, (6, 8))
    x_sum(0, 2, xin0, x0)
    for dz in range(1, 8):
        zo = (z + dz) % 8
        in_group(3, xin0.at[me_x, :, zo], fin0.at[z], dev(xl, y, core, zo, xh)).start()
    fin0[z] = xin0[me_x, :, z]
    z_step(1, (4, 6))
    z_step(2, early_flows)
    z_step(2, (6, 8))
    own_rows()

    z_step(2, (4, 6))
    for i, (copies, yo) in enumerate(((x2, ym), (x3, yp))):
        x_sum(12 + 2 * i, 1, xin2.at[i], copies)
        for dz in (4, 3, 5, 2, 6, 1, 7, 0):
            zo = (z + dz) % 8
            in_group(5, xin2.at[i, me_x, 0, zo], fin2.at[z, i], dev(xl, yo, core, zo, xh)).start()
    for c in started[-N_SEND:]:
        c.wait_send()
    group_wait(3, fin0.at[0:7])
    group_wait(4, oth.at[0:8])
    group_wait(2, fin3.at[0:14])

    def total(parts):
        return functools.reduce(lambda p, q: p + q, parts)

    def near(kinds_of):
        return total([fin3[s * 4 + t] for t in kinds_of for s in range(4)])

    def passed_on(kinds_of):
        return total([fin1[w, s, t] for t in kinds_of for w in range(2) for s in range(4)])

    cross[:, 0:256] = total([fin0[s, 0] for s in range(8)])
    cross[:, 1024:1280] = total([fin0[s, 1] for s in range(8)])
    cross[:, 256:512] = near((0, 3))
    cross[:, 768:1024] = near((1, 2))
    for k in range(9):
        here = slice(k * 128, (k + 1) * 128)
        own[:, here] = jnp.sqrt(own[:, here] * oth[k] + eps_norm)
    group_wait(1, fin1)
    cross[:, 256:512] = cross[:, 256:512] + passed_on((0, 3))
    cross[:, 768:1024] = cross[:, 768:1024] + passed_on((1, 2))
    group_wait(5, fin2)
    cross[:, 512:768] = total([fin2[s, t] for t in range(2) for s in range(8)])
    shift = pl.multiple_of(core * 128, 128)
    for k in range(9):
        here = slice(k * 128, (k + 1) * 128)
        out_ref[:, here] = cross[:, pl.ds(pl.multiple_of(shift + k * 128, 128), 128)] / own[:, here]


def slopes(degrees):
    return jnp.tan(degrees.astype(F32) * (math.pi / 180.0))


def shards(spectra, tilt_min, tilt_max, tilt_axis):
    vmem = pl.BlockSpec(memory_space=pltpu.VMEM)
    scratch = [
        pltpu.VMEM((3, 16, 128), jnp.int32),
        pltpu.VMEM((2, 2 * KC, 128), BF16),
        pltpu.VMEM((2, 2, KC, 128), BF16),
        pltpu.VMEM((KC, 128), BF16),
        pltpu.VMEM((KC, 512), BF16),
        pltpu.VMEM((KC, 512), BF16),
        pltpu.VMEM((A, 512), BF16),
        pltpu.VMEM((B, 512), BF16),
        pltpu.VMEM((2 * Q, 512), BF16),
        pltpu.VMEM((16, 2, 8, 2, 8, 256), F32),
        pltpu.VMEM((16, 8, 2, 8, 256), F32),
        pltpu.VMEM((4, 2, 8, 8, 256), F32),
        pltpu.VMEM((2, 4, 1, 8, 8, 256), F32),
        pltpu.VMEM((8, 3, 2, 2, 8, 256), F32),
        pltpu.VMEM((8, 2, 8, 256), F32),
        pltpu.VMEM((8, 2, 8, 256), F32),
        pltpu.VMEM((2, 4, 4, 8, 256), F32),
        pltpu.VMEM((8, 2, 8, 256), F32),
        pltpu.VMEM((16, 8, 256), F32),
        pltpu.VMEM((2, KC, 128), BF16),
        pltpu.VMEM((2, KC, 128), BF16),
        pltpu.VMEM((128, 128), F32),
        pltpu.VMEM((2, 4, 16, 128), F32),
        pltpu.VMEM((256, 128), F32),
        pltpu.VMEM((128, 128), F32),
        pltpu.VMEM((2, 16, 128), jnp.int32),
        pltpu.VMEM((128, 1152), BF16),
        pltpu.VMEM((8, 1152), F32),
        pltpu.VMEM((9, 8, 128), F32),
        pltpu.VMEM((9, 8, 128), F32),
        pltpu.VMEM((8, 1280), F32),
        pltpu.SemaphoreType.DMA((9,)),
        pltpu.SemaphoreType.DMA((N_SEND,)),
        pltpu.SemaphoreType.DMA((N_RECV,)),
        pltpu.SemaphoreType.DMA((6,)),
        pltpu.SemaphoreType.DMA((6,)),
    ]
    tilts = [t.reshape(16, 128) for t in (tilt_min, tilt_max, tilt_axis)]
    return pl.pallas_call(
        kernel,
        out_shape=pltpu.VMEM((8, 1152), F32),
        in_specs=[pl.BlockSpec(memory_space=pl.ANY)] * 4,
        out_specs=vmem,
        scratch_shapes=scratch,
        compiler_params=pltpu.CompilerParams(
            collective_id=0, has_side_effects=True, vmem_limit_bytes=56 * 2**20
        ),
    )(spectra, *tilts)


def solution(mesh):
    in_specs = (P(None, "af", "pa"), P(), P(), P())
    out_specs = P(("pa", "af"), None)
    return jax.shard_map(shards, mesh=mesh, in_specs=in_specs, out_specs=out_specs, check_vma=False)
```
